32 devices in a mesh: clip: 16 (over z, x, core), tm: 2 (over y).
Axes of the slice: x: 2, y: 2, z: 4, core: 2. Of those that a mesh axis runs over, the one named last changes fastest.
Arguments:
- inputs: float32 [32, 2048, 512], P('clip', 'tm'), may hold values from -6 to 6
- band_ids: int32 [32], P('clip'), may hold values from 0 to 3
- offsets: int32 [32], P('clip'), may hold values from 0 to 511
- conv_weight: float32 [7, 512], replicated, may hold values from -2 to 2
- conv_bias: float32 [512], replicated, may hold values from -3 to 3
- scale_table: float32 [4, 512], replicated, may hold values from 0.25 to 1.75
- shift_table: float32 [4, 512], replicated, may hold values from -3 to 3
- up_weight: float32 [512, 1536], replicated, may hold values from -0.25 to 0.25
- up_bias: float32 [1536], replicated, may hold values from -3 to 3
- down_weight: float32 [1536, 512], replicated, may hold values from -0.15625 to 0.15625
- down_bias: float32 [512], replicated, may hold values from -2 to 2
- layer_scale: float32 [512], replicated, may hold values from 0.25 to 1.75
- head_weight: float32 [512, 1282], replicated, may hold values from -0.1875 to 0.1875
- head_bias: float32 [1282], replicated, may hold values from 1.5 to 3.5
- wave_cotangent: float32 [32, 655360], P('clip', 'tm'), may hold values from -6 to 6
Outputs:
- waveform: float32 [32, 655360], P('clip', 'tm')
- grad_inputs: float32 [32, 2048, 512], P('clip', 'tm')
- grad_conv_weight: float32 [7, 512], replicated
- grad_conv_bias: float32 [512], replicated
- grad_scale_table: float32 [4, 512], replicated
- grad_shift_table: float32 [4, 512], replicated
- grad_up_weight: float32 [512, 1536], replicated
- grad_up_bias: float32 [1536], replicated
- grad_down_weight: float32 [1536, 512], replicated
- grad_down_bias: float32 [512], replicated
- grad_layer_scale: float32 [512], replicated
- grad_head_weight: float32 [512, 1282], replicated
- grad_head_bias: float32 [1282], replicated
The draws below stay inside these ranges and needn't reach their ends.
All inputs are finite; a program needn't handle non-finite values.
Results may differ from the reference program's by a relative error of at most 0.0003.
Values sent between devices are 32-bit elements; how exact they have to be, the bound alone decides.
No kernel may reach another device: no remote copies, remote signals or barrier semaphores. Data moves between devices by JAX's collectives and lax.ppermute only.
A program may use at most 192 MiB of HBM per device.

```python
import math
import jax
import jax.numpy as jnp
from jax import lax

D = 512
FF = 1536
NFFT = 1280
HOP = 320
BANDS = 4
KERNEL = 7
FR_DEV = 1024
CLIPS = 32
FRAMES = 2048
NBINS = 641
HEAD = 1282


def with_ends(drawn, key, smallest, largest):
    spot = [jax.random.randint(jax.random.fold_in(key, axis), (), 0, length) for axis, length in enumerate(drawn.shape)]
    widest = drawn.shape.index(max(drawn.shape))
    neighbour = spot[:widest] + [(spot[widest] + 1) % drawn.shape[widest]] + spot[widest + 1:]
    return drawn.at[tuple(spot)].set(smallest).at[tuple(neighbour)].set(largest)


def level_of(stream_key, shape, cuts, smallest, high):
    def one(axis_at, blocks):
        steps = jax.random.uniform(jax.random.fold_in(jax.random.fold_in(stream_key, 6), axis_at), (blocks,), jnp.float32, smallest / len(cuts), high / len(cuts))
        return jnp.repeat(jnp.exp(steps), shape[axis_at] // blocks).reshape((-1,) + (1,) * (len(shape) - axis_at - 1))

    loudness = one(*cuts[0])
    for cut in cuts[1:]:
        loudness = loudness * one(*cut)
    return loudness


def centred(own_key, dims, spread, limit, cuts=(), held_as=jnp.bfloat16):
    gain = level_of(own_key, dims, cuts, -0.22, 0.18) if cuts else 1.0
    drawn = jax.random.normal(own_key, dims, jnp.float32) * spread * gain
    return jnp.minimum(jnp.maximum(drawn, -limit), limit).astype(held_as)


def setup_inputs(seed: int = 0) -> dict:
    key_of = jax.random.split(jax.random.key(seed), 16)
    inputs = centred(key_of[0], (CLIPS, FRAMES, D), 1.0, 6.0, ((0, 16), (1, 2)), jnp.float32)
    band_ids = with_ends(jax.random.randint(key_of[1], (CLIPS,), 0, BANDS), jax.random.fold_in(key_of[1], 1), 0, BANDS - 1).astype(jnp.int32)
    offsets = with_ends(jax.random.randint(key_of[2], (CLIPS,), 0, FR_DEV // 2), jax.random.fold_in(key_of[2], 1), 0, (FR_DEV // 2) - 1).astype(jnp.int32)
    conv_weight = centred(key_of[3], (KERNEL, D), KERNEL ** -0.5, 2.0, (), jnp.float32)
    conv_bias = centred(key_of[4], (D,), 0.5, 3.0, (), jnp.float32)
    scale_table = jnp.clip(1.0 + 0.15 * jax.random.normal(key_of[5], (BANDS, D), jnp.float32), 0.25, 1.75)
    shift_table = centred(key_of[6], (BANDS, D), 0.5, 3.0, (), jnp.float32)
    up_weight = centred(key_of[7], (D, FF), D ** -0.5, 0.25, (), jnp.float32)
    up_bias = centred(key_of[8], (FF,), 0.5, 3.0, (), jnp.float32)
    down_weight = centred(key_of[9], (FF, D), FF ** -0.5, 0.15625, (), jnp.float32)
    down_bias = centred(key_of[10], (D,), 0.3, 2.0, (), jnp.float32)
    layer_scale = jnp.clip(1.0 + 0.15 * jax.random.normal(key_of[11], (D,), jnp.float32), 0.25, 1.75)
    head_weight = centred(key_of[12], (D, HEAD), (2 * D) ** -0.5, 0.1875, (), jnp.float32)
    head_bias = jnp.clip(jax.random.uniform(key_of[13], (HEAD,), jnp.float32, 1.5, 3.5), 1.5, 3.5)
    wave_cotangent = centred(key_of[14], (CLIPS, FRAMES * HOP), 1.0, 6.0, ((0, 16), (1, 2)), jnp.float32)
    return {"inputs": inputs, "band_ids": band_ids, "offsets": offsets, "conv_weight": conv_weight, "conv_bias": conv_bias, "scale_table": scale_table, "shift_table": shift_table, "up_weight": up_weight, "up_bias": up_bias, "down_weight": down_weight, "down_bias": down_bias, "layer_scale": layer_scale, "head_weight": head_weight, "head_bias": head_bias, "wave_cotangent": wave_cotangent}


def hann_window():
    steps = jnp.arange(NFFT).astype(jnp.float32)
    return 0.5 - 0.5 * jnp.cos(2.0 * jnp.pi * steps / NFFT)

def forward(parameters, inputs, band_ids, offsets):
    conv_weight, conv_bias, scale_table, shift_table, up_weight, up_bias, down_weight, down_bias, layer_scale, head_weight, head_bias = parameters
    highest = lax.Precision.HIGHEST
    clip_count = inputs.shape[0]
    positions = jnp.arange(FRAMES).astype(jnp.int32)
    present = (positions[None, :] >= offsets[:, None]).astype(jnp.float32)
    masked = inputs * present[:, :, None]
    padded = jnp.pad(masked, ((0, 0), (3, 3), (0, 0)))
    conved = conv_bias + sum((padded[:, kernel_pos:kernel_pos + FRAMES] * conv_weight[kernel_pos] for kernel_pos in range(KERNEL)))
    center = conved - lax.optimization_barrier(jnp.mean(conved, axis=-1, keepdims=True))
    variance = lax.optimization_barrier(jnp.mean(center * center, axis=-1, keepdims=True))
    normed = center * lax.rsqrt(variance + 1e-06)
    onehot = (band_ids[:, None] == jnp.arange(BANDS).astype(jnp.int32)[None, :]).astype(jnp.float32)
    scales = jnp.dot(onehot, scale_table, precision=highest)
    shifts = jnp.dot(onehot, shift_table, precision=highest)
    adapted = normed * scales[:, None, :] + shifts[:, None, :]
    upward = jnp.einsum('cfd,dh->cfh', adapted, up_weight, precision=highest) + up_bias
    activated = jax.nn.gelu(upward, approximate=False)
    branch = jnp.einsum('cfh,hd->cfd', activated, down_weight, precision=highest) + down_bias
    residual_out = masked + layer_scale * branch
    logits = jnp.einsum('cfd,dk->cfk', residual_out, head_weight, precision=highest) + head_bias
    raw = jnp.exp(logits[..., :NBINS])
    magnitude = 100.0 * jnp.tanh(raw / 100.0) * present[:, :, None]
    angles = logits[..., NBINS:]
    spectrum = magnitude * jnp.cos(angles) + 1j * (magnitude * jnp.sin(angles))
    window = hann_window()
    segments = jnp.fft.irfft(spectrum, n=NFFT, axis=-1) * window
    pieces = segments.reshape(clip_count, FRAMES, 4, HOP)
    summed = sum((jnp.pad(pieces[:, :, quarter], ((0, 0), (quarter, 0), (0, 0)))[:, :FRAMES] for quarter in range(4)))
    squares = (window * window).reshape(4, HOP)
    envelope = sum((jnp.pad(present, ((0, 0), (quarter, 0)))[:, :FRAMES, None] * squares[quarter] for quarter in range(4)))
    envelope = jnp.maximum(envelope, 1.0)
    return (summed / envelope).reshape(clip_count, FRAMES * HOP)

def add_pair(first_term, second_term):
    return first_term + second_term

def reference(inputs, band_ids, offsets, conv_weight, conv_bias, scale_table, shift_table, up_weight, up_bias, down_weight, down_bias, layer_scale, head_weight, head_bias, wave_cotangent):
    parameters = (conv_weight, conv_bias, scale_table, shift_table, up_weight, up_bias, down_weight, down_bias, layer_scale, head_weight, head_bias)
    group = math.gcd(CLIPS, max(1, 4096 // FRAMES))
    blocks = CLIPS // group

    def step(totals, pieces):
        block_inputs, block_ids, block_offsets, block_cotangent = pieces

        def apply(params_in, inputs_in):
            return forward(params_in, inputs_in, block_ids, block_offsets)
        waveform, pullback = jax.vjp(apply, parameters, block_inputs)
        grad_params, grad_block = pullback(block_cotangent)
        totals = jax.tree.map(add_pair, totals, grad_params)
        return (totals, (waveform, grad_block))
    zeros = jax.tree.map(jnp.zeros_like, parameters)
    stacked = (inputs.reshape(blocks, group, FRAMES, D), band_ids.reshape(blocks, group), offsets.reshape(blocks, group), wave_cotangent.reshape(blocks, group, FRAMES * HOP))
    totals, outputs = lax.scan(step, zeros, stacked)
    waveform = outputs[0].reshape(CLIPS, FRAMES * HOP)
    grad_inputs = outputs[1].reshape(CLIPS, FRAMES, D)
    return (waveform, grad_inputs, totals[0], totals[1], totals[2], totals[3], totals[4], totals[5], totals[6], totals[7], totals[8], totals[9], totals[10])
```

```python
import functools

import jax
import jax.numpy as jnp
import ml_dtypes
import numpy as np
from jax import lax
from jax.experimental import pallas as pl
from jax.experimental.pallas import tpu as pltpu
from jax.sharding import PartitionSpec as P

KERNEL = 7
F32 = jnp.float32
BF16 = jnp.bfloat16
LANES = 128
PAIRS = 128
ROWS = 2 * PAIRS
VMEM = 60 * 2**20
SDS = jax.ShapeDtypeStruct

SIN_POLY = (0.999999996, -0.166666580, 8.33305023e-03, -1.98090119e-04, 2.60507821e-06)
COS_POLY = (1.0, -0.499999994, 4.16666361e-02, -1.38883598e-03, 2.47600798e-05, -2.60500270e-07)

NN = (((1,), (0,)), ((), ()))
NT = (((1,), (1,)), ((), ()))


def split(x):
    high = x.astype(BF16)
    return high, (x - high.astype(F32)).astype(BF16)


def dot(a, b, dims=NN):
    return lax.dot_general(a, b, dims, preferred_element_type=F32)


def dot3(a, b, dims=NN):
    return dot(a[0], b[0], dims) + (dot(a[0], b[1], dims) + dot(a[1], b[0], dims))


def fold8(x):
    return jnp.sum(x.reshape(x.shape[0] // 8, 8, x.shape[1]), axis=0)


def np_split(x):
    high = x.astype(np.float32).astype(ml_dtypes.bfloat16)
    return high, (x - high.astype(np.float64)).astype(ml_dtypes.bfloat16)


@functools.lru_cache(None)
def tables(nfft):
    fifth, half, hop = nfft // 5, nfft // 2, nfft // 4
    bins = np.arange(1, half)
    first = bins[np.isin(bins % 5, (1, 4))]
    second = bins[np.isin(bins % 5, (2, 3))]
    zero = np.arange(0, half, 5)
    n0 = np.arange(fifth)

    def paired(ks, residue):
        sign = np.where(ks % 5 == residue, 1.0, -1.0)[:, None]
        turn = 2 * np.pi * ((sign * ks[:, None] * n0[None]) % nfft) / nfft
        weight = 2.0 / nfft
        real = np.concatenate([weight * np.cos(turn), weight * np.sin(turn)], 1)
        imag = np.concatenate([-sign * weight * np.sin(turn), sign * weight * np.cos(turn)], 1)
        return np.concatenate([real, imag], 0)

    turn = 2 * np.pi * ((zero[:, None] * n0[None]) % nfft) / nfft
    weight = np.where(zero == 0, 1.0, 2.0)[:, None] / nfft
    real, imag = weight * np.cos(turn), -weight * np.sin(turn)
    imag[0] = np.cos(np.pi * n0) / nfft
    transforms = [np_split(t) for t in (paired(first, 1), paired(second, 2), np.concatenate([real, imag], 0))]
    n = np.arange(nfft)
    window = 0.5 - 0.5 * np.cos(2 * np.pi * n / nfft)
    windows = np.stack([window, np.roll(window, hop)]).astype(np.float32)
    squares = np.cumsum((window**2).reshape(4, hop), axis=0)
    inverse = np.tile(1.0 / np.maximum(squares, 1.0), (1, 2)).astype(np.float32)
    order = np.concatenate([first, half + 1 + first, second, half + 1 + second, zero, half + 1 + zero])
    turns = np.zeros(nfft)
    place = 0
    for ks in (first, second, zero):
        turns[place + len(ks) : place + 2 * len(ks)] = -(np.pi / 2) * (ks % 4)
        place += 2 * len(ks)
    return transforms, windows, inverse, order, turns.astype(np.float32), (len(first), len(second), len(zero))


def sin_cos(x):
    turns = jnp.round(x * np.float32(0.5 / np.pi))
    h = x * 0.5 - turns * np.float32(3.140625)
    h = h - turns * np.float32(9.67502593994140625e-4)
    h = h - turns * np.float32(1.509957990978376432e-7)
    z = h * h
    s = np.float32(SIN_POLY[-1])
    for c in SIN_POLY[-2::-1]:
        s = s * z + np.float32(c)
    s = s * h
    cosine = np.float32(COS_POLY[-1])
    for c in COS_POLY[-2::-1]:
        cosine = cosine * z + np.float32(c)
    twice = s + s
    return twice * cosine, 1.0 - twice * s


def fifths():
    a = 2 * np.pi / 5
    return [np.float32(v) for v in (np.cos(a), np.cos(2 * a), np.sin(a), np.sin(2 * a))]


def inverse_envelope(first_pair, offset, table_ref, tile, rows):
    lane = tile * LANES + lax.broadcasted_iota(jnp.int32, (rows, LANES), 1)
    row = lax.broadcasted_iota(jnp.int32, (rows, LANES), 0)
    half = table_ref.shape[1] // 2
    since = 2 * (first_pair + row) + (lane >= half).astype(jnp.int32) - offset
    value = jnp.where(since < 0, 1.0, 1.0)
    for i in range(4):
        value = jnp.where(since >= i, table_ref[i : i + 1, tile * LANES : (tile + 1) * LANES], value)
    return value


def head_kernel(
    scalars,
    x_ref,
    before_ref,
    after_ref,
    cot_ref,
    cot_after_ref,
    conv_w,
    conv_b,
    scale_t,
    shift_t,
    up_w,
    up_b,
    down_w,
    down_b,
    layer_scale,
    head_h,
    head_l,
    head_b,
    ext_w,
    ext_b,
    t1h,
    t1l,
    t2h,
    t2l,
    t0h,
    t0l,
    windows,
    inverse,
    o_norm,
    o_istd,
    o_adt_h,
    o_adt_l,
    o_act_h,
    o_act_l,
    o_slope,
    o_spec,
    o_gm,
    o_gb_h,
    o_gb_l,
    o_gbt_h,
    o_gbt_l,
    o_ghw,
    o_ghb,
    o_ghwe,
    o_ghbe,
    o_gls,
    o_gmb,
    up_h,
    up_l,
    down_h,
    down_l,
    pad4,
    nrm4,
    istd1,
    gs5,
    gm4,
    gl_h,
    gl_l,
    acc_ghb,
    acc_ghwe,
    acc_ghbe,
    acc_gls,
    acc_gmb,
):
    clip, blk = pl.program_id(0), pl.program_id(1)
    clips, blks = pl.num_programs(0), pl.num_programs(1)
    frames, width = x_ref.shape[1], x_ref.shape[2]
    tiles = width // LANES
    start = scalars[0]
    band = scalars[1 + clip]
    local = scalars[1 + clips + clip] - start
    rows8 = before_ref.shape[1]

    @pl.when((clip == 0) & (blk == 0))
    def _():
        up_h[...], up_l[...] = split(up_w[...])
        down_h[...], down_l[...] = split(down_w[...])
        for ref in (o_ghw, acc_ghb, acc_ghwe, acc_ghbe, acc_gls, acc_gmb):
            ref[...] = jnp.zeros_like(ref)

    @pl.when(blk == 0)
    def _():
        def masked(value, first):
            row = first + lax.broadcasted_iota(jnp.int32, value.shape, 0)
            return jnp.where(row >= local, value, 0.0)

        before = masked(before_ref[0], -rows8)
        after = masked(after_ref[0], frames)
        for t in range(tiles):
            lanes = slice(t * LANES, (t + 1) * LANES)
            pad4[t, 0:rows8, :] = before[:, lanes]
            pad4[t, rows8 + frames : 2 * rows8 + frames, :] = after[:, lanes]

        chunk = 64

        def fill(i, carry):
            r = pl.multiple_of(i * chunk, chunk)
            value = masked(x_ref[0, pl.ds(r, chunk), :], r)
            for t in range(tiles):
                pad4[t, pl.ds(r + rows8, chunk), :] = value[:, t * LANES : (t + 1) * LANES]
            return carry

        lax.fori_loop(0, frames // chunk, fill, 0)

        def conv(i, carry):
            r = pl.multiple_of(i * chunk, chunk)
            parts = []
            for t in range(tiles):
                lanes = slice(t * LANES, (t + 1) * LANES)
                total = conv_b[0:1, lanes]
                for k in range(KERNEL):
                    total = total + pad4[t, pl.ds(r + rows8 - 3 + k, chunk), :] * conv_w[k : k + 1, lanes]
                parts.append(total)
            mean = jnp.sum(sum(parts[1:], parts[0]), axis=1, keepdims=True) * (1.0 / width)
            parts = [p - mean for p in parts]
            squares = [p * p for p in parts]
            variance = jnp.sum(sum(squares[1:], squares[0]), axis=1, keepdims=True) * (1.0 / width)
            istd = lax.rsqrt(variance + 1e-6)
            for t in range(tiles):
                nrm4[t, pl.ds(r, chunk), :] = parts[t] * istd
            istd1[pl.ds(r, chunk), :] = jnp.broadcast_to(istd, (chunk, LANES))
            return carry

        lax.fori_loop(0, frames // chunk, conv, 0)

        pairs = frames // 2
        wave_tiles = gs5.shape[0]

        def cotangent(i, carry):
            r = pl.multiple_of(i * chunk, chunk)
            for t in range(wave_tiles):
                first = clips * (wave_tiles * r + t) + clip
                value = cot_ref[pl.ds(first, chunk, stride=clips * wave_tiles), :]
                gs5[t, pl.ds(r, chunk), :] = value * inverse_envelope(r, local, inverse, t, chunk)
            return carry

        lax.fori_loop(0, pairs // chunk, cotangent, 0)
        for t in range(wave_tiles):
            value = cot_after_ref[0, :, t * LANES : (t + 1) * LANES]
            gs5[t, pairs : pairs + 8, :] = value * inverse_envelope(pairs, local, inverse, t, 8)

    base = pl.multiple_of(blk * ROWS, ROWS)
    normed = jnp.concatenate(
        [
            jnp.concatenate([nrm4[t, pl.ds(base + par, PAIRS, stride=2), :] for t in range(tiles)], 1)
            for par in range(2)
        ],
        0,
    )
    o_norm[...] = normed
    for par in range(2):
        o_istd[par * PAIRS : (par + 1) * PAIRS, :] = istd1[pl.ds(base + par, PAIRS, stride=2), :]
    adapted = normed * scale_t[pl.ds(band, 1), :] + shift_t[pl.ds(band, 1), :]
    ad = split(adapted)
    o_adt_h[...], o_adt_l[...] = split(adapted.T)

    hidden = up_h.shape[1]
    step = 256
    for j in range(hidden // step):
        cols = slice(j * step, (j + 1) * step)
        upward = dot3(ad, (up_h[:, cols], up_l[:, cols])) + up_b[0:1, cols]
        cdf = 0.5 + 0.5 * lax.erf(upward * np.float32(0.7071067811865476))
        density = jnp.exp(upward * upward * -0.5) * np.float32(0.3989422804014327)
        o_slope[:, cols] = cdf + upward * density
        o_act_h[:, cols], o_act_l[:, cols] = split(upward * cdf)
    branch = dot3((o_act_h[...], o_act_l[...]), (down_h[...], down_l[...])) + down_b[0:1, :]
    masked_rows = jnp.concatenate(
        [
            jnp.concatenate([pad4[t, pl.ds(base + rows8 + par, PAIRS, stride=2), :] for t in range(tiles)], 1)
            for par in range(2)
        ],
        0,
    )
    residual = masked_rows + layer_scale[0:1, :] * branch
    res = split(residual)
    res_t = split(residual.T)

    first_pair = pl.multiple_of(blk * PAIRS, PAIRS)
    wave_tiles = gs5.shape[0]
    now, one, two = (
        [gs5[t, pl.ds(first_pair + d, PAIRS), :] for t in range(wave_tiles)] for d in range(3)
    )
    mid = wave_tiles // 2
    right = lax.broadcasted_iota(jnp.int32, (PAIRS, LANES), 1) >= LANES // 2
    odd = two[:mid] + [jnp.where(right, now[mid], two[mid])] + now[mid + 1 :] + one
    c1, c2, s1, s2 = fifths()
    folded = []
    for par, segment in enumerate((now + one, odd)):
        seg = [v * windows[par : par + 1, t * LANES : (t + 1) * LANES] for t, v in enumerate(segment)]
        v = [jnp.concatenate(seg[2 * j : 2 * j + 2], 1) for j in range(5)]
        p14, m41, p23, m32 = v[1] + v[4], v[4] - v[1], v[2] + v[3], v[3] - v[2]
        folded.append(
            (
                v[0] + p14 + p23,
                v[0] + c1 * p14 + c2 * p23,
                s1 * m41 + s2 * m32,
                v[0] + c2 * p14 + c1 * p23,
                s2 * m41 - s1 * m32,
            )
        )
    f0, fa, fb, fc, fd = (jnp.concatenate([e, o], 0) for e, o in zip(*folded))
    spectrum_grads = (
        dot3(split(jnp.concatenate([fa, fb], 1)), (t1h[...], t1l[...]), NT),
        dot3(split(jnp.concatenate([fc, fd], 1)), (t2h[...], t2l[...]), NT),
        dot3(split(f0), (t0h[...], t0l[...]), NT),
    )

    ext = split(ext_w[...])
    ext_logits = dot3(ext, res, NT) + ext_b[:, 0:1]
    lane = lax.broadcasted_iota(jnp.int32, (1, ROWS), 1)
    ext_frame = base + jnp.where(lane < PAIRS, 2 * lane, 2 * (lane - PAIRS) + 1)
    ext_present = ext_frame >= local

    def magnitudes(logits, present):
        raw = jnp.where(present, jnp.exp(logits), 0.0)
        squashed = jnp.tanh(raw * np.float32(0.01))
        return 100.0 * squashed, raw * (1.0 - squashed * squashed)

    ext_mag, ext_slope = magnitudes(ext_logits[0:1], ext_present)
    ext_sin, ext_cos = sin_cos(ext_logits[1:2])
    ext_real = ext_mag * ext_cos
    ext_imag = ext_mag * ext_sin
    ext_real_col = jnp.concatenate([ext_real, jnp.zeros((7, ROWS), F32)], 0).T[:, 0:1]

    row = lax.broadcasted_iota(jnp.int32, (PAIRS, 1), 0)
    place = 0
    for index, grads in enumerate(spectrum_grads):
        n = grads.shape[1] // 2
        cols = slice(place, place + 2 * n)
        logits = dot3(res, (head_h[:, cols], head_l[:, cols]))
        for par in range(2):
            rows = slice(par * PAIRS, (par + 1) * PAIRS)
            present = base + 2 * row + par >= local
            value = logits[rows] + head_b[par : par + 1, cols]
            magnitude, slope = magnitudes(value[:, :n], present)
            sine, cosine = sin_cos(value[:, n:])
            real, imag = magnitude * cosine, magnitude * sine
            g_real, g_imag = grads[rows, :n], grads[rows, n:]
            if index == 2:
                corner = lax.broadcasted_iota(jnp.int32, (PAIRS, n), 1) == 0
                shown = jnp.where(corner, ext_real_col[rows], imag)
                g_imag = jnp.where(corner, 0.0, g_imag)
            else:
                shown = imag
            o_spec[rows, place : place + n] = real
            o_spec[rows, place + n : place + 2 * n] = shown
            g_mag = slope * (g_real * cosine + g_imag * sine)
            g_ang = g_imag * real - g_real * imag
            gl = jnp.concatenate([g_mag, g_ang], 1)
            acc_ghb[:, cols] += fold8(gl)
            gl_h[rows, cols], gl_l[rows, cols] = split(gl)
        place += 2 * n

    corner_t = spectrum_grads[2][:, spectrum_grads[2].shape[1] // 2 :].T
    ext_g = corner_t[0:1, :]
    ext_grads = jnp.concatenate(
        [ext_slope * ext_g * ext_cos, -ext_g * ext_imag, jnp.zeros((6, ROWS), F32)], 0
    )
    acc_ghbe[...] += ext_grads
    acc_ghwe[...] += dot3(split(ext_grads), res)
    gl = (gl_h[...], gl_l[...])
    o_ghw[...] += dot3(res_t, gl)
    ext_cols = ext_grads.T
    grad_mixed = (
        dot3(gl, (head_h[...], head_l[...]), NT)
        + ext_cols[:, 0:1] * ext_w[0:1, :]
        + ext_cols[:, 1:2] * ext_w[1:2, :]
    )
    acc_gls[...] += fold8(grad_mixed * branch)
    acc_gmb[...] += fold8(grad_mixed)
    for par in range(2):
        rows = slice(par * PAIRS, (par + 1) * PAIRS)
        for t in range(tiles):
            gm4[t, pl.ds(par, PAIRS, stride=2), :] = grad_mixed[rows, t * LANES : (t + 1) * LANES]
    for t in range(tiles):
        o_gm[:, t * LANES : (t + 1) * LANES] = gm4[t]
    grad_branch = grad_mixed * layer_scale[0:1, :]
    o_gb_h[...], o_gb_l[...] = split(grad_branch)
    o_gbt_h[...], o_gbt_l[...] = split(grad_branch.T)

    @pl.when((clip == clips - 1) & (blk == blks - 1))
    def _():
        o_ghb[...] = jnp.sum(acc_ghb[...], axis=0, keepdims=True)
        o_ghwe[...] = acc_ghwe[...]
        o_ghbe[...] = jnp.sum(acc_ghbe[...], axis=1, keepdims=True)
        o_gls[...] = jnp.sum(acc_gls[...], axis=0, keepdims=True)
        o_gmb[...] = jnp.sum(acc_gmb[...], axis=0, keepdims=True)


def whole(shape):
    return pl.BlockSpec(shape, lambda *_: (0,) * len(shape))


def run_head(scalars, x, before, after, cot, cot_after, weights, head, consts):
    clips, frames, width = x.shape
    blks = frames // ROWS
    count = clips * frames
    hidden = weights[4].shape[1]
    nfft = head[0].shape[1]
    block = lambda i, j, *_: (i * blks + j, 0)
    column = lambda i, j, *_: (0, i * blks + j)
    per_clip = lambda shape: pl.BlockSpec((1,) + shape, lambda i, j, *_: (i, 0, 0))
    in_specs = [per_clip((frames, width)), per_clip(before.shape[1:]), per_clip(after.shape[1:])]
    in_specs += [whole(cot.shape), per_clip(cot_after.shape[1:])]
    operands = list(weights) + list(head) + list(consts)
    in_specs += [whole(v.shape) for v in operands]
    outs = [
        (SDS((count, width), F32), pl.BlockSpec((ROWS, width), block)),
        (SDS((count, LANES), F32), pl.BlockSpec((ROWS, LANES), block)),
        (SDS((width, count), BF16), pl.BlockSpec((width, ROWS), column)),
        (SDS((width, count), BF16), pl.BlockSpec((width, ROWS), column)),
        (SDS((count, hidden), BF16), pl.BlockSpec((ROWS, hidden), block)),
        (SDS((count, hidden), BF16), pl.BlockSpec((ROWS, hidden), block)),
        (SDS((count, hidden), F32), pl.BlockSpec((ROWS, hidden), block)),
        (SDS((count, nfft), F32), pl.BlockSpec((ROWS, nfft), block)),
        (SDS((count, width), F32), pl.BlockSpec((ROWS, width), block)),
        (SDS((count, width), BF16), pl.BlockSpec((ROWS, width), block)),
        (SDS((count, width), BF16), pl.BlockSpec((ROWS, width), block)),
        (SDS((width, count), BF16), pl.BlockSpec((width, ROWS), column)),
        (SDS((width, count), BF16), pl.BlockSpec((width, ROWS), column)),
    ]
    for shape in ((width, nfft), (1, nfft), (8, width), (8, 1), (1, width), (1, width)):
        outs.append((SDS(shape, F32), whole(shape)))
    wave_tiles = nfft // 2 // LANES
    tiles = width // LANES
    scratch = [pltpu.VMEM((width, hidden), BF16)] * 2 + [pltpu.VMEM((hidden, width), BF16)] * 2
    scratch += [
        pltpu.VMEM((tiles, frames + 2 * before.shape[1], LANES), F32),
        pltpu.VMEM((tiles, frames, LANES), F32),
        pltpu.VMEM((frames, LANES), F32),
        pltpu.VMEM((wave_tiles, frames // 2 + 8, LANES), F32),
        pltpu.VMEM((tiles, ROWS, LANES), F32),
        pltpu.VMEM((ROWS, nfft), BF16),
        pltpu.VMEM((ROWS, nfft), BF16),
        pltpu.VMEM((8, nfft), F32),
        pltpu.VMEM((8, width), F32),
        pltpu.VMEM((8, ROWS), F32),
        pltpu.VMEM((8, width), F32),
        pltpu.VMEM((8, width), F32),
    ]
    return pl.pallas_call(
        head_kernel,
        grid_spec=pltpu.PrefetchScalarGridSpec(
            num_scalar_prefetch=1,
            grid=(clips, blks),
            in_specs=in_specs,
            out_specs=[s for _, s in outs],
            scratch_shapes=scratch,
        ),
        out_shape=[s for s, _ in outs],
        compiler_params=pltpu.CompilerParams(vmem_limit_bytes=VMEM),
        name="head",
    )(scalars, x, before, after, cot, cot_after, *operands)


def ffn_kernel(
    gb_h, gb_l, gbt_h, gbt_l, act_h, act_l, slope, adt_h, adt_l, down_w,
    o_gdn, o_gup, o_gub, o_gu_h, o_gu_l, dw_h, dw_l, acc_gub,
):
    step = pl.program_id(0)

    @pl.when(step == 0)
    def _():
        dw_h[...], dw_l[...] = split(down_w[...])
        for ref in (o_gdn, o_gup, acc_gub):
            ref[...] = jnp.zeros_like(ref)

    o_gdn[...] += dot3((gbt_h[...], gbt_l[...]), (act_h[...], act_l[...]))
    cols = 256
    for j in range(slope.shape[1] // cols):
        part = slice(j * cols, (j + 1) * cols)
        gu = dot3((gb_h[...], gb_l[...]), (dw_h[part, :], dw_l[part, :]), NT) * slope[:, part]
        acc_gub[:, part] += fold8(gu)
        gs = split(gu)
        o_gu_h[:, part], o_gu_l[:, part] = gs
        o_gup[:, part] += dot3((adt_h[...], adt_l[...]), gs)

    @pl.when(step == pl.num_programs(0) - 1)
    def _():
        o_gub[...] = jnp.sum(acc_gub[...], axis=0, keepdims=True)


def run_ffn(gb, gbt, act, slope, adt, down_w, part, parts):
    count, width = gb[0].shape
    hidden = slope.shape[1] // parts
    rows = 512
    row = lambda i: (i, 0)
    mine = lambda i: (i, part)
    col = lambda i: (0, i)
    in_specs = [pl.BlockSpec((rows, width), row)] * 2 + [pl.BlockSpec((width, rows), col)] * 2
    in_specs += [pl.BlockSpec((rows, hidden), mine)] * 3 + [pl.BlockSpec((width, rows), col)] * 2
    in_specs += [pl.BlockSpec((hidden, width), lambda i: (part, 0))]
    return pl.pallas_call(
        ffn_kernel,
        grid=(count // rows,),
        in_specs=in_specs,
        out_specs=[
            whole((width, hidden)),
            whole((width, hidden)),
            whole((1, hidden)),
            pl.BlockSpec((rows, hidden), row),
            pl.BlockSpec((rows, hidden), row),
        ],
        out_shape=[
            SDS((width, hidden), F32),
            SDS((width, hidden), F32),
            SDS((1, hidden), F32),
            SDS((count, hidden), BF16),
            SDS((count, hidden), BF16),
        ],
        scratch_shapes=[pltpu.VMEM((hidden, width), BF16)] * 2 + [pltpu.VMEM((8, hidden), F32)],
        compiler_params=pltpu.CompilerParams(vmem_limit_bytes=VMEM),
        name="ffn_grads",
    )(*gb, *gbt, *act, slope, *adt, down_w)


def norm_kernel(parts, scalars, *refs):
    gu = refs[: 2 * parts]
    up_w, norm, istd, scale_t, o_gh, o_scale, o_shift, up_h, up_l, nat4, acc_scale, acc_shift = refs[2 * parts :]
    clip, blk = pl.program_id(0), pl.program_id(1)
    clips, blks = pl.num_programs(0), pl.num_programs(1)
    band = scalars[1 + clip]
    width = norm.shape[1]
    tiles = width // LANES

    @pl.when((clip == 0) & (blk == 0))
    def _():
        up_h[...], up_l[...] = split(up_w[...])
        o_scale[...] = jnp.zeros_like(o_scale)
        o_shift[...] = jnp.zeros_like(o_shift)

    @pl.when(blk == 0)
    def _():
        acc_scale[...] = jnp.zeros_like(acc_scale)
        acc_shift[...] = jnp.zeros_like(acc_shift)

    hidden = up_w.shape[1] // parts
    ga = None
    for j in range(parts):
        cols = slice(j * hidden, (j + 1) * hidden)
        term = dot3((gu[2 * j][...], gu[2 * j + 1][...]), (up_h[:, cols], up_l[:, cols]), NT)
        ga = term if ga is None else ga + term
    normed = norm[...]
    acc_scale[...] += fold8(ga * normed)
    acc_shift[...] += fold8(ga)
    gn = ga * scale_t[pl.ds(band, 1), :]
    mean = jnp.sum(gn, axis=1, keepdims=True) * (1.0 / width)
    along = jnp.sum(gn * normed, axis=1, keepdims=True) * (1.0 / width)
    gh = istd[:, 0:1] * (gn - mean - normed * along)
    half = norm.shape[0] // 2
    for par in range(2):
        for t in range(tiles):
            nat4[t, pl.ds(par, half, stride=2), :] = gh[par * half : (par + 1) * half, t * LANES : (t + 1) * LANES]
    for t in range(tiles):
        o_gh[:, t * LANES : (t + 1) * LANES] = nat4[t]

    @pl.when(blk == blks - 1)
    def _():
        o_scale[pl.ds(band, 1), :] += jnp.sum(acc_scale[...], axis=0, keepdims=True)
        o_shift[pl.ds(band, 1), :] += jnp.sum(acc_shift[...], axis=0, keepdims=True)


def run_norm(scalars, gus, up_w, norm, istd, scale_t, clips):
    count, width = norm.shape
    blks = count // clips // ROWS
    parts = len(gus)
    block = lambda i, j, *_: (i * blks + j, 0)
    flat = [v for pair in gus for v in pair]
    in_specs = [pl.BlockSpec((ROWS, v.shape[1]), block) for v in flat]
    in_specs += [whole(up_w.shape), pl.BlockSpec((ROWS, width), block)]
    in_specs += [pl.BlockSpec((ROWS, LANES), block), whole(scale_t.shape)]
    return pl.pallas_call(
        functools.partial(norm_kernel, parts),
        grid_spec=pltpu.PrefetchScalarGridSpec(
            num_scalar_prefetch=1,
            grid=(clips, blks),
            in_specs=in_specs,
            out_specs=[pl.BlockSpec((ROWS, width), block), whole(scale_t.shape), whole(scale_t.shape)],
            scratch_shapes=[pltpu.VMEM(up_w.shape, BF16)] * 2
            + [pltpu.VMEM((width // LANES, ROWS, LANES), F32)]
            + [pltpu.VMEM((8, width), F32)] * 2,
        ),
        out_shape=[SDS((count, width), F32), SDS(scale_t.shape, F32), SDS(scale_t.shape, F32)],
        compiler_params=pltpu.CompilerParams(vmem_limit_bytes=VMEM),
        name="norm_grads",
    )(scalars, *flat, up_w, norm, istd, scale_t)


def conv_kernel(
    scalars, x_ref, before_ref, after_ref, gh_ref, gh_before, gh_after, gm_ref, conv_w,
    o_gi, o_gcw, o_gcb, pad4, gh4, acc_w, acc_b,
):
    clip = pl.program_id(0)
    clips = pl.num_programs(0)
    frames, width = x_ref.shape[1], x_ref.shape[2]
    tiles = width // LANES
    local = scalars[1 + clips + clip] - scalars[0]
    rows8 = before_ref.shape[1]
    chunk = 64

    @pl.when(clip == 0)
    def _():
        acc_w[...] = jnp.zeros_like(acc_w)
        acc_b[...] = jnp.zeros_like(acc_b)

    def masked(value, first):
        row = first + lax.broadcasted_iota(jnp.int32, value.shape, 0)
        return jnp.where(row >= local, value, 0.0)

    before, after = masked(before_ref[0], -rows8), masked(after_ref[0], frames)
    for t in range(tiles):
        lanes = slice(t * LANES, (t + 1) * LANES)
        pad4[t, 0:rows8, :] = before[:, lanes]
        pad4[t, rows8 + frames : 2 * rows8 + frames, :] = after[:, lanes]
        gh4[t, 0:rows8, :] = gh_before[0, :, lanes]
        gh4[t, rows8 + frames : 2 * rows8 + frames, :] = gh_after[0, :, lanes]

    def fill(i, carry):
        r = pl.multiple_of(i * chunk, chunk)
        value = masked(x_ref[0, pl.ds(r, chunk), :], r)
        for t in range(tiles):
            lanes = slice(t * LANES, (t + 1) * LANES)
            pad4[t, pl.ds(r + rows8, chunk), :] = value[:, lanes]
            gh4[t, pl.ds(r + rows8, chunk), :] = gh_ref[0, pl.ds(r, chunk), lanes]
        return carry

    lax.fori_loop(0, frames // chunk, fill, 0)

    def conv(i, carry):
        r = pl.multiple_of(i * chunk, chunk)
        shown = r + lax.broadcasted_iota(jnp.int32, (chunk, LANES), 0) >= local
        for t in range(tiles):
            lanes = slice(t * LANES, (t + 1) * LANES)
            gh = gh4[t, pl.ds(r + rows8, chunk), :]
            acc_b[:, lanes] += fold8(gh)
            total = gm_ref[0, pl.ds(r, chunk), lanes]
            for k in range(KERNEL):
                total = total + conv_w[k : k + 1, lanes] * gh4[t, pl.ds(r + rows8 + 3 - k, chunk), :]
                acc_w[8 * k : 8 * k + 8, lanes] += fold8(gh * pad4[t, pl.ds(r + rows8 - 3 + k, chunk), :])
            o_gi[0, pl.ds(r, chunk), lanes] = jnp.where(shown, total, 0.0)
        return carry

    lax.fori_loop(0, frames // chunk, conv, 0)

    @pl.when(clip == clips - 1)
    def _():
        for k in range(KERNEL):
            o_gcw[k : k + 1, :] = jnp.sum(acc_w[8 * k : 8 * k + 8, :], axis=0, keepdims=True)
        o_gcb[...] = jnp.sum(acc_b[...], axis=0, keepdims=True)


def run_conv(scalars, x, before, after, gh, gh_before, gh_after, gm, conv_w):
    clips, frames, width = x.shape
    rows8 = before.shape[1]
    per_clip = lambda n: pl.BlockSpec((1, n, width), lambda i, *_: (i, 0, 0))
    padded = pltpu.VMEM((width // LANES, frames + 2 * rows8, LANES), F32)
    return pl.pallas_call(
        conv_kernel,
        grid_spec=pltpu.PrefetchScalarGridSpec(
            num_scalar_prefetch=1,
            grid=(clips,),
            in_specs=[per_clip(n) for n in (frames, rows8, rows8, frames, rows8, rows8, frames)]
            + [whole(conv_w.shape)],
            out_specs=[per_clip(frames), whole(conv_w.shape), whole((1, width))],
            scratch_shapes=[padded, padded, pltpu.VMEM((8 * KERNEL, width), F32), pltpu.VMEM((8, width), F32)],
        ),
        out_shape=[SDS(x.shape, F32), SDS(conv_w.shape, F32), SDS((1, width), F32)],
        compiler_params=pltpu.CompilerParams(vmem_limit_bytes=VMEM),
        name="conv_grads",
    )(scalars, x, before, after, gh, gh_before, gh_after, gm, conv_w)


def wave_kernel(
    scalars, spec, t1h, t1l, t2h, t2l, t0h, t0l, windows, inverse, o_wave, o_tail, acc5
):
    clip, blk = pl.program_id(0), pl.program_id(1)
    clips, blks = pl.num_programs(0), pl.num_programs(1)
    local = scalars[1 + clips + clip] - scalars[0]
    tiles = acc5.shape[0]

    @pl.when(blk == 0)
    def _():
        acc5[...] = jnp.zeros_like(acc5)

    @pl.when(blk > 0)
    def _():
        for t in range(tiles):
            acc5[t, 0:8, :] = acc5[t, PAIRS : PAIRS + 8, :]
            acc5[t, 8:, :] = jnp.zeros((PAIRS, LANES), F32)

    n1, n2 = t1h.shape[0], t2h.shape[0]
    ab = dot3(split(spec[:, :n1]), (t1h[...], t1l[...]))
    cd = dot3(split(spec[:, n1 : n1 + n2]), (t2h[...], t2l[...]))
    p0 = dot3(split(spec[:, n1 + n2 :]), (t0h[...], t0l[...]))
    c1, c2, s1, s2 = fifths()
    sides = []
    for par in range(2):
        rows = slice(par * PAIRS, (par + 1) * PAIRS)
        w = p0.shape[1]
        a, b, c, d, p = ab[rows, :w], ab[rows, w:], cd[rows, :w], cd[rows, w:], p0[rows]
        e1, o1 = p + c1 * a + c2 * c, s1 * b + s2 * d
        e2, o2 = p + c2 * a + c1 * c, s2 * b - s1 * d
        v = [p + a + c, e1 - o1, e2 - o2, e2 + o2, e1 + o1]
        seg = []
        for t in range(2 * tiles):
            part = v[t // 2][:, (t % 2) * LANES : (t % 2 + 1) * LANES]
            seg.append(part * windows[par : par + 1, t * LANES : (t + 1) * LANES])
        sides.append(seg)
    even, odd = sides
    mid = tiles // 2
    right = lax.broadcasted_iota(jnp.int32, (PAIRS, LANES), 1) >= LANES // 2
    for t in range(tiles):
        here = even[t]
        if t > mid:
            here = here + odd[t]
        if t == mid:
            here = here + jnp.where(right, odd[t], 0.0)
        acc5[t, 0:PAIRS, :] += here
        acc5[t, 1 : PAIRS + 1, :] += even[tiles + t] + odd[tiles + t]
        if t < mid:
            acc5[t, 2 : PAIRS + 2, :] += odd[t]
        if t == mid:
            acc5[t, 2 : PAIRS + 2, :] += jnp.where(right, 0.0, odd[t])
        first = pl.multiple_of(blk * PAIRS, PAIRS)
        value = acc5[t, 0:PAIRS, :] * inverse_envelope(first, local, inverse, t, PAIRS)
        o_wave[pl.ds(clips * (tiles * first + t) + clip, PAIRS, stride=clips * tiles), :] = value

    @pl.when(blk == blks - 1)
    def _():
        for t in range(tiles):
            o_tail[0, :, t * LANES : (t + 1) * LANES] = acc5[t, PAIRS : PAIRS + 8, :]


def run_wave(scalars, spec, consts, clips):
    count, nfft = spec.shape
    blks = count // clips // ROWS
    tiles = nfft // 2 // LANES
    chunks = count * nfft // 4 // LANES
    return pl.pallas_call(
        wave_kernel,
        grid_spec=pltpu.PrefetchScalarGridSpec(
            num_scalar_prefetch=1,
            grid=(clips, blks),
            in_specs=[pl.BlockSpec((ROWS, nfft), lambda i, j, *_: (i * blks + j, 0))]
            + [whole(v.shape) for v in consts],
            out_specs=[
                whole((chunks, LANES)),
                pl.BlockSpec((1, 8, nfft // 2), lambda i, j, *_: (i, 0, 0)),
            ],
            scratch_shapes=[pltpu.VMEM((tiles, PAIRS + 8, LANES), F32)],
        ),
        out_shape=[SDS((chunks, LANES), F32), SDS((clips, 8, nfft // 2), F32)],
        compiler_params=pltpu.CompilerParams(vmem_limit_bytes=VMEM),
        name="wave",
    )(scalars, spec, *consts)


def neighbours(last, first, axis):
    devices = lax.axis_size(axis)
    up = [(i, i + 1) for i in range(devices - 1)]
    down = [(j, i) for i, j in up]
    return lax.ppermute(last, axis, up), lax.ppermute(first, axis, down)


def to_chunks(wave):
    clips, samples = wave.shape
    return wave.reshape(clips, samples // LANES, LANES).transpose(1, 0, 2).reshape(-1, LANES)


def from_chunks(chunks, clips):
    rows = chunks.shape[0] // clips
    return chunks.reshape(rows, clips, LANES).transpose(1, 0, 2).reshape(clips, rows * LANES)


def body(
    inputs,
    band_ids,
    offsets,
    conv_weight,
    conv_bias,
    scale_table,
    shift_table,
    up_weight,
    up_bias,
    down_weight,
    down_bias,
    layer_scale,
    head_weight,
    head_bias,
    wave_cotangent,
):
    clips, frames, width = inputs.shape
    nfft = head_weight.shape[1] - 2
    half = nfft // 2
    start = lax.axis_index("tm") * frames
    scalars = jnp.concatenate([start[None].astype(jnp.int32), band_ids, offsets])
    transforms, windows, inverse, order, turns, _ = tables(nfft)
    dft = [jnp.asarray(v) for pair in transforms for v in pair]
    consts = dft + [jnp.asarray(windows), jnp.asarray(inverse)]

    before, after = neighbours(inputs[:, -8:], inputs[:, :8], "tm")
    _, cot_after = neighbours(wave_cotangent[:, : 2 * half], wave_cotangent[:, : 2 * half], "tm")
    cot_after = jnp.pad(cot_after.reshape(clips, 2, half), ((0, 0), (0, 6), (0, 0)))

    place = np.zeros((nfft + 2, nfft), np.float32)
    place[order, np.arange(nfft)] = 1.0
    place = jnp.asarray(place.astype(ml_dtypes.bfloat16))
    head_high = lax.reduce_precision(head_weight, 8, 7)
    head_h = dot(head_high.astype(BF16), place).astype(BF16)
    head_l = dot((head_weight - head_high).astype(BF16), place).astype(BF16)
    bias = jnp.dot(head_bias[None], place.astype(F32), precision=lax.Precision.HIGHEST)
    bias = jnp.concatenate([bias, bias + turns[None]], 0)
    ends = jnp.asarray([half, nfft + 1])
    ext_w = jnp.concatenate([head_weight[:, half : half + 1], head_weight[:, nfft + 1 :]], 1).T
    ext_w = jnp.pad(ext_w, ((0, 6), (0, 0)))
    ext_b = jnp.pad(jnp.stack([head_bias[half], head_bias[nfft + 1]])[:, None], ((0, 6), (0, 0)))

    weights = (
        conv_weight,
        conv_bias[None],
        scale_table,
        shift_table,
        up_weight,
        up_bias[None],
        down_weight,
        down_bias[None],
        layer_scale[None],
    )
    (
        norm, istd, adt_h, adt_l, act_h, act_l, slope, spec, gm, gb_h, gb_l, gbt_h, gbt_l,
        ghw, ghb, ghwe, ghbe, gls, gmb,
    ) = run_head(
        scalars, inputs, before, after, to_chunks(wave_cotangent), cot_after, weights,
        (head_h, head_l, bias, ext_w, ext_b), consts,
    )

    parts = 3
    gdn, gup, gub, gus = [], [], [], []
    for part in range(parts):
        down, up, up_b, gu_h, gu_l = run_ffn(
            (gb_h, gb_l), (gbt_h, gbt_l), (act_h, act_l), slope, (adt_h, adt_l), down_weight, part, parts
        )
        gdn.append(down)
        gup.append(up)
        gub.append(up_b)
        gus.append((gu_h, gu_l))
    gh, gscale, gshift = run_norm(scalars, gus, up_weight, norm, istd, scale_table, clips)
    gh = gh.reshape(clips, frames, width)
    gh_before, gh_after = neighbours(gh[:, -8:], gh[:, :8], "tm")
    gm = gm.reshape(clips, frames, width)
    grad_inputs, gcw, gcb = run_conv(scalars, inputs, before, after, gh, gh_before, gh_after, gm, conv_weight)

    wave, tail = run_wave(scalars, spec, consts, clips)
    arrived, _ = neighbours(tail[:, :2].reshape(clips, nfft), tail[:, :2].reshape(clips, nfft), "tm")
    arrived = arrived * jnp.tile(jnp.asarray(inverse[3:4]), (1, 2))
    head_rows = clips * nfft // LANES
    wave = wave.at[:head_rows].add(to_chunks(arrived))
    waveform = from_chunks(wave, clips)

    sums = lax.psum(
        (gcw, gcb, gscale, gshift, *gup, *gub, *gdn, gmb, gls, ghw, ghwe, ghb, ghbe), ("clip", "tm")
    )
    gcw, gcb, gscale, gshift = sums[:4]
    gup, gub, gdn = sums[4 : 4 + parts], sums[4 + parts : 4 + 2 * parts], sums[4 + 2 * parts : 4 + 3 * parts]
    gmb, gls, ghw, ghwe, ghb, ghbe = sums[4 + 3 * parts :]
    ghw_high = lax.reduce_precision(ghw, 8, 7)
    ghw = dot(ghw_high.astype(BF16), place, NT) + dot((ghw - ghw_high).astype(BF16), place, NT)
    ghw = ghw.at[:, half].set(ghwe[0]).at[:, nfft + 1].set(ghwe[1])
    ghb = jnp.dot(ghb, place.astype(F32).T, precision=lax.Precision.HIGHEST)[0]
    ghb = ghb.at[half].set(ghbe[0, 0]).at[nfft + 1].set(ghbe[1, 0])
    return (
        waveform,
        grad_inputs,
        gcw,
        gcb[0],
        gscale,
        gshift,
        jnp.concatenate(gup, 1),
        jnp.concatenate(gub, 1)[0],
        jnp.concatenate([g.T for g in gdn], 0),
        gmb[0] * layer_scale,
        gls[0],
        ghw,
        ghb,
    )


def solution(mesh):
    in_specs = (P("clip", "tm", None), P("clip"), P("clip")) + (P(),) * 11 + (P("clip", "tm"),)
    out_specs = (P("clip", "tm"), P("clip", "tm", None)) + (P(),) * 11
    return jax.shard_map(body, mesh=mesh, in_specs=in_specs, out_specs=out_specs, check_vma=False)
```

```python
import functools

import jax
import jax.numpy as jnp
import ml_dtypes
import numpy as np
from jax import lax
from jax.experimental import pallas as pl
from jax.experimental.pallas import tpu as pltpu
from jax.sharding import PartitionSpec as P

KERNEL = 7
CLASSES = ((1, 4), (2, 3), (0,))
F32 = jnp.float32
BF16 = jnp.bfloat16
LANES = 128
PAIRS = 128
ROWS = 2 * PAIRS
VMEM = 60 * 2**20
FFN_PARTS = ((1024, 0), (512, 2))
SDS = jax.ShapeDtypeStruct

SIN_POLY = (0.999999996, -0.166666580, 8.33305023e-03, -1.98090119e-04, 2.60507821e-06)
COS_POLY = (1.0, -0.499999994, 4.16666361e-02, -1.38883598e-03, 2.47600798e-05, -2.60500270e-07)

NN = (((1,), (0,)), ((), ()))
NT = (((1,), (1,)), ((), ()))


def split(x):
    high = x.astype(BF16)
    return high, (x - high.astype(F32)).astype(BF16)


def dot(a, b, dims=NN):
    return lax.dot_general(a, b, dims, preferred_element_type=F32)


def dot3(a, b, dims=NN):
    return dot(a[0], b[0], dims) + (dot(a[0], b[1], dims) + dot(a[1], b[0], dims))


def fold8(x):
    return jnp.sum(x.reshape(x.shape[0] // 8, 8, x.shape[1]), axis=0)


def np_split(x):
    high = x.astype(np.float32).astype(ml_dtypes.bfloat16)
    return high, (x - high.astype(np.float64)).astype(ml_dtypes.bfloat16)


@functools.lru_cache(None)
def tables(nfft):
    fifth, half, hop = nfft // 5, nfft // 2, nfft // 4
    bins = np.arange(1, half)
    first, second = (np.concatenate([bins[bins % 5 == r] for r in rs]) for rs in CLASSES[:2])
    zero = np.arange(0, half, 5)
    n0 = np.arange(fifth)

    def paired(ks, residue):
        sign = np.where(ks % 5 == residue, 1.0, -1.0)[:, None]
        turn = 2 * np.pi * ((sign * ks[:, None] * n0[None]) % nfft) / nfft
        weight = 2.0 / nfft
        real = np.concatenate([weight * np.cos(turn), weight * np.sin(turn)], 1)
        imag = np.concatenate([-sign * weight * np.sin(turn), sign * weight * np.cos(turn)], 1)
        return np.concatenate([real, imag], 0)

    turn = 2 * np.pi * ((zero[:, None] * n0[None]) % nfft) / nfft
    weight = np.where(zero == 0, 1.0, 2.0)[:, None] / nfft
    real, imag = weight * np.cos(turn), -weight * np.sin(turn)
    imag[0] = np.cos(np.pi * n0) / nfft
    transforms = [np_split(t) for t in (paired(first, 1), paired(second, 2), np.concatenate([real, imag], 0))]
    n = np.arange(nfft)
    window = 0.5 - 0.5 * np.cos(2 * np.pi * n / nfft)
    windows = np.stack([window, np.roll(window, hop)]).astype(np.float32)
    squares = np.cumsum((window**2).reshape(4, hop), axis=0)
    inverse = np.tile(1.0 / np.maximum(squares, 1.0), (1, 2)).astype(np.float32)
    turns = np.zeros(nfft)
    place = 0
    for ks in (first, second, zero):
        turns[place + len(ks) : place + 2 * len(ks)] = -(np.pi / 2) * (ks % 4)
        place += 2 * len(ks)
    return transforms, windows, inverse, turns.astype(np.float32)[None]


def class_places(nfft):
    length, places, at = nfft // 10, [], 0
    for residues in CLASSES:
        for offset in (0, nfft // 2 + 1):
            for r in residues:
                places.append((at, offset + r))
                at += length
    return places


def sin_cos(x):
    turns = jnp.round(x * np.float32(0.5 / np.pi))
    h = x * 0.5 - turns * np.float32(3.140625)
    h = h - turns * np.float32(9.67502593994140625e-4)
    h = h - turns * np.float32(1.509957990978376432e-7)
    z = h * h
    s = np.float32(SIN_POLY[-1])
    for c in SIN_POLY[-2::-1]:
        s = s * z + np.float32(c)
    s = s * h
    cosine = np.float32(COS_POLY[-1])
    for c in COS_POLY[-2::-1]:
        cosine = cosine * z + np.float32(c)
    twice = s + s
    return twice * cosine, 1.0 - twice * s


def fifths():
    a = 2 * np.pi / 5
    return [np.float32(v) for v in (np.cos(a), np.cos(2 * a), np.sin(a), np.sin(2 * a))]


def inverse_envelope(first_pair, offset, table_ref, tile, rows):
    lane = tile * LANES + lax.broadcasted_iota(jnp.int32, (rows, LANES), 1)
    row = lax.broadcasted_iota(jnp.int32, (rows, LANES), 0)
    half = table_ref.shape[1] // 2
    since = 2 * (first_pair + row) + (lane >= half).astype(jnp.int32) - offset
    value = jnp.where(since < 0, 1.0, 1.0)
    for i in range(4):
        value = jnp.where(since >= i, table_ref[i : i + 1, tile * LANES : (tile + 1) * LANES], value)
    return value


def head_kernel(
    bands,
    offsets,
    x_ref,
    x_up,
    x_down,
    edge_ref,
    cot_ref,
    cot_edge,
    conv_w,
    conv_b,
    scale_t,
    shift_t,
    up_w,
    up_b,
    down_w,
    down_b,
    layer_scale,
    head_wt,
    head_b,
    turns,
    t1h,
    t1l,
    t2h,
    t2l,
    t0h,
    t0l,
    windows,
    inverse,
    o_norm,
    o_istd,
    o_adt_h,
    o_adt_l,
    o_act_h,
    o_act_l,
    o_slope,
    o_spec,
    o_gm,
    o_gb_h,
    o_gb_l,
    o_gbt_h,
    o_gbt_l,
    o_keep,
    o_send,
    o_small,
    up_h,
    up_l,
    down_h,
    down_l,
    head_h,
    head_l,
    head_bias,
    ext_w,
    head4,
    bias4,
    pad4,
    nrm4,
    istd1,
    gs5,
    gm4,
    gl_h,
    gl_l,
    acc_ghw,
    acc_ghb,
    acc_ghwe,
    acc_ghbe,
    acc_gls,
    acc_gmb,
):
    clip, blk = pl.program_id(0), pl.program_id(1)
    clips, blks = pl.num_programs(0), pl.num_programs(1)
    width = x_ref.shape[2]
    frames = blks * ROWS
    tiles = width // LANES
    nfft = turns.shape[1]
    half = nfft // 2
    tm = lax.axis_index("tm")
    band = bands[clip]
    local = offsets[clip] - tm * frames
    rows8 = edge_ref.shape[1]
    places = class_places(nfft)

    @pl.when((clip == 0) & (blk == 0))
    def _():
        up_h[...], up_l[...] = split(up_w[...])
        down_h[...], down_l[...] = split(down_w[...])
        for t in range(tiles):
            head4[t, 0 : nfft + 2, :] = head_wt[:, t * LANES : (t + 1) * LANES]
        bias = head_b[...].reshape(1, nfft + 2)
        for c in range(0, nfft, LANES):
            bias4[c : c + LANES, :] = jnp.broadcast_to(bias[:, c : c + LANES], (LANES, LANES)).T
        for c in (nfft, nfft + 1):
            bias4[c : c + 1, :] = jnp.broadcast_to(bias[:, c : c + 1], (1, LANES))
        for at, first in places:
            rows = jnp.concatenate([head4[t, pl.ds(first, LANES, stride=5), :] for t in range(tiles)], 1)
            head_h[at : at + LANES, :], head_l[at : at + LANES, :] = split(rows)
            moved = bias4[pl.ds(first, LANES, stride=5), :].T[0:1, :]
            head_bias[0:1, at : at + LANES] = moved
            head_bias[1:2, at : at + LANES] = moved + turns[:, at : at + LANES]
        ext_w[0:1, :] = head_wt[half : half + 1, :]
        ext_w[1:2, :] = head_wt[nfft + 1 : nfft + 2, :]
        ext_w[2:8, :] = jnp.zeros((6, width), F32)
        for ref in (acc_ghw, acc_ghb, acc_ghwe, acc_ghbe, acc_gls, acc_gmb):
            ref[...] = jnp.zeros_like(ref)

    base = pl.multiple_of(blk * ROWS, ROWS)

    def masked(value, first):
        row = first + lax.broadcasted_iota(jnp.int32, value.shape, 0)
        return jnp.where(row >= local, value, 0.0)

    before = masked(jnp.where(blk == 0, jnp.where(tm > 0, edge_ref[0], 0.0), x_up[0]), base - rows8)
    after = masked(jnp.where(blk == blks - 1, jnp.where(tm > 0, 0.0, edge_ref[0]), x_down[0]), base + ROWS)
    middle = masked(x_ref[0], base)
    for t in range(tiles):
        lanes = slice(t * LANES, (t + 1) * LANES)
        pad4[t, 0:rows8, :] = before[:, lanes]
        pad4[t, rows8 : rows8 + ROWS, :] = middle[:, lanes]
        pad4[t, rows8 + ROWS :, :] = after[:, lanes]
    bias = conv_b[...].reshape(1, width)
    chunk = 64
    for r in range(0, ROWS, chunk):
        parts = []
        for t in range(tiles):
            lanes = slice(t * LANES, (t + 1) * LANES)
            total = bias[:, lanes]
            for k in range(KERNEL):
                first = r + rows8 - KERNEL // 2 + k
                total = total + pad4[t, first : first + chunk, :] * conv_w[k : k + 1, lanes]
            parts.append(total)
        mean = jnp.sum(sum(parts[1:], parts[0]), axis=1, keepdims=True) * (1.0 / width)
        parts = [p - mean for p in parts]
        squares = [p * p for p in parts]
        variance = jnp.sum(sum(squares[1:], squares[0]), axis=1, keepdims=True) * (1.0 / width)
        istd = lax.rsqrt(variance + 1e-6)
        for t in range(tiles):
            nrm4[t, r : r + chunk, :] = parts[t] * istd
        istd1[r : r + chunk, :] = jnp.broadcast_to(istd, (chunk, LANES))

    def by_parity(ref, first):
        return jnp.concatenate(
            [
                jnp.concatenate([ref[t, pl.ds(first + par, PAIRS, stride=2), :] for t in range(tiles)], 1)
                for par in range(2)
            ],
            0,
        )

    normed = by_parity(nrm4, 0)
    o_norm[...] = normed
    for par in range(2):
        o_istd[par * PAIRS : (par + 1) * PAIRS, :] = istd1[pl.ds(par, PAIRS, stride=2), :]
    adapted = normed * scale_t[pl.ds(band, 1), :] + shift_t[pl.ds(band, 1), :]
    ad = split(adapted)
    o_adt_h[...], o_adt_l[...] = split(adapted.T)

    first_pair = pl.multiple_of(blk * PAIRS, PAIRS)
    wave_tiles = gs5.shape[0]
    pairs = frames // 2
    next_pair = jnp.minimum(first_pair + PAIRS, pairs - 8)
    for t in range(wave_tiles):
        lanes = slice(t * LANES, (t + 1) * LANES)
        stride = clips * wave_tiles
        value = cot_ref[pl.ds(stride * first_pair + clips * t + clip, PAIRS, stride=stride), :]
        gs5[t, 0:PAIRS, :] = value * inverse_envelope(first_pair, local, inverse, t, PAIRS)
        value = cot_ref[pl.ds(stride * next_pair + clips * t + clip, 8, stride=stride), :]
        value = jnp.where(blk == blks - 1, jnp.where(tm > 0, 0.0, cot_edge[0, :, lanes]), value)
        gs5[t, PAIRS : PAIRS + 8, :] = value * inverse_envelope(first_pair + PAIRS, local, inverse, t, 8)
    now, one, two = ([gs5[t, d : d + PAIRS, :] for t in range(wave_tiles)] for d in range(3))
    mid = wave_tiles // 2
    right = lax.broadcasted_iota(jnp.int32, (PAIRS, LANES), 1) >= LANES // 2
    odd = two[:mid] + [jnp.where(right, now[mid], two[mid])] + now[mid + 1 :] + one
    c1, c2, s1, s2 = fifths()
    folded = []
    for par, segment in enumerate((now + one, odd)):
        seg = [v * windows[par : par + 1, t * LANES : (t + 1) * LANES] for t, v in enumerate(segment)]
        v = [jnp.concatenate(seg[2 * j : 2 * j + 2], 1) for j in range(5)]
        p14, m41, p23, m32 = v[1] + v[4], v[4] - v[1], v[2] + v[3], v[3] - v[2]
        folded.append(
            (
                v[0] + p14 + p23,
                v[0] + c1 * p14 + c2 * p23,
                s1 * m41 + s2 * m32,
                v[0] + c2 * p14 + c1 * p23,
                s2 * m41 - s1 * m32,
            )
        )
    f0, fa, fb, fc, fd = (jnp.concatenate([e, o], 0) for e, o in zip(*folded))
    spectrum_grads = (
        dot3(split(jnp.concatenate([fa, fb], 1)), (t1h[...], t1l[...]), NT),
        dot3(split(jnp.concatenate([fc, fd], 1)), (t2h[...], t2l[...]), NT),
        dot3(split(f0), (t0h[...], t0l[...]), NT),
    )

    hidden = up_h.shape[1]
    step = 256
    up_bias = up_b[...].reshape(1, hidden)
    for j in range(hidden // step):
        cols = slice(j * step, (j + 1) * step)
        upward = dot3(ad, (up_h[:, cols], up_l[:, cols])) + up_bias[:, cols]
        cdf = 0.5 + 0.5 * lax.erf(upward * np.float32(0.7071067811865476))
        density = jnp.exp(upward * upward * -0.5) * np.float32(0.3989422804014327)
        o_slope[:, cols] = cdf + upward * density
        o_act_h[:, cols], o_act_l[:, cols] = split(upward * cdf)
    branch = dot3((o_act_h[...], o_act_l[...]), (down_h[...], down_l[...])) + down_b[...].reshape(1, width)
    scale = layer_scale[...].reshape(1, width)
    residual = by_parity(pad4, rows8) + scale * branch
    res = split(residual)
    res_t = split(residual.T)

    bias = head_b[...].reshape(1, nfft + 2)
    ext = split(ext_w[...])
    ext_logits = dot3(ext, res, NT)
    lane = lax.broadcasted_iota(jnp.int32, (1, ROWS), 1)
    ext_frame = base + jnp.where(lane < PAIRS, 2 * lane, 2 * (lane - PAIRS) + 1)
    ext_present = ext_frame >= local

    def magnitudes(logits, present):
        raw = jnp.where(present, jnp.exp(logits), 0.0)
        squashed = jnp.tanh(raw * np.float32(0.01))
        return 100.0 * squashed, raw * (1.0 - squashed * squashed)

    ext_mag, ext_slope = magnitudes(ext_logits[0:1] + bias[:, half : half + 1], ext_present)
    ext_sin, ext_cos = sin_cos(ext_logits[1:2] + bias[:, nfft + 1 : nfft + 2])
    ext_real = ext_mag * ext_cos
    ext_imag = ext_mag * ext_sin
    ext_real_col = jnp.concatenate([ext_real, jnp.zeros((7, ROWS), F32)], 0).T[:, 0:1]

    row = lax.broadcasted_iota(jnp.int32, (PAIRS, 1), 0)
    at = 0
    for index, grads in enumerate(spectrum_grads):
        n = grads.shape[1] // 2
        cols = slice(at, at + 2 * n)
        logits = dot3(res, (head_h[cols, :], head_l[cols, :]), NT)
        for par in range(2):
            rows = slice(par * PAIRS, (par + 1) * PAIRS)
            present = base + 2 * row + par >= local
            value = logits[rows] + head_bias[par : par + 1, cols]
            magnitude, slope = magnitudes(value[:, :n], present)
            sine, cosine = sin_cos(value[:, n:])
            real, imag = magnitude * cosine, magnitude * sine
            g_real, g_imag = grads[rows, :n], grads[rows, n:]
            if index == 2:
                corner = lax.broadcasted_iota(jnp.int32, (PAIRS, n), 1) == 0
                shown = jnp.where(corner, ext_real_col[rows], imag)
                g_imag = jnp.where(corner, 0.0, g_imag)
            else:
                shown = imag
            o_spec[rows, at : at + n] = real
            o_spec[rows, at + n : at + 2 * n] = shown
            g_mag = slope * (g_real * cosine + g_imag * sine)
            g_ang = g_imag * real - g_real * imag
            gl = jnp.concatenate([g_mag, g_ang], 1)
            acc_ghb[:, cols] += fold8(gl)
            gl_h[rows, cols], gl_l[rows, cols] = split(gl)
        at += 2 * n

    corner_t = spectrum_grads[2][:, spectrum_grads[2].shape[1] // 2 :].T
    ext_g = corner_t[0:1, :]
    ext_grads = jnp.concatenate(
        [ext_slope * ext_g * ext_cos, -ext_g * ext_imag, jnp.zeros((6, ROWS), F32)], 0
    )
    acc_ghbe[...] += ext_grads
    acc_ghwe[...] += dot3(split(ext_grads), res)
    gl = (gl_h[...], gl_l[...])
    ext_cols = ext_grads.T
    grad_mixed = (
        dot3(gl, (head_h[...], head_l[...]))
        + ext_cols[:, 0:1] * ext_w[0:1, :]
        + ext_cols[:, 1:2] * ext_w[1:2, :]
    )
    acc_ghw[...] += dot3(res_t, gl)
    acc_gls[...] += fold8(grad_mixed * branch)
    acc_gmb[...] += fold8(grad_mixed)
    for par in range(2):
        rows = slice(par * PAIRS, (par + 1) * PAIRS)
        for t in range(tiles):
            gm4[t, pl.ds(par, PAIRS, stride=2), :] = grad_mixed[rows, t * LANES : (t + 1) * LANES]
    for t in range(tiles):
        o_gm[:, t * LANES : (t + 1) * LANES] = gm4[t]
    grad_branch = grad_mixed * scale
    o_gb_h[...], o_gb_l[...] = split(grad_branch)
    o_gbt_h[...], o_gbt_l[...] = split(grad_branch.T)

    @pl.when((clip == clips - 1) & (blk == blks - 1))
    def _():
        total = jnp.sum(acc_ghb[...], axis=0, keepdims=True)
        for at, first in places:
            for t in range(tiles):
                block = acc_ghw[t * LANES : (t + 1) * LANES, at : at + LANES]
                head4[t, pl.ds(first, LANES, stride=5), :] = block.T
            block = jnp.broadcast_to(total[:, at : at + LANES], (LANES, LANES))
            bias4[pl.ds(first, LANES, stride=5), :] = block.T
        ext_sums = jnp.sum(acc_ghbe[...], axis=1, keepdims=True)
        for i, c in enumerate((half, nfft + 1)):
            for t in range(tiles):
                head4[t, c : c + 1, :] = acc_ghwe[i : i + 1, t * LANES : (t + 1) * LANES]
            bias4[c : c + 1, :] = jnp.broadcast_to(ext_sums[i : i + 1], (1, LANES))
        core = lax.axis_index("clip") % 2
        rows = o_keep.shape[0]
        for t in range(tiles):
            head4[t, nfft + 2 :, :] = jnp.zeros((2 * rows - nfft - 2, LANES), F32)
            for ref, part in ((o_keep, core), (o_send, 1 - core)):
                mine = pl.ds(pl.multiple_of(part * rows, rows), rows)
                ref[:, t * LANES : (t + 1) * LANES] = head4[t, mine, :]
        o_small[...] = jnp.zeros_like(o_small)
        for c in range(0, nfft, LANES):
            o_small[0:1, c : c + LANES] = bias4[c : c + LANES, :].T[0:1, :]
        o_small[0:1, nfft : nfft + 2] = jnp.concatenate(
            [bias4[nfft : nfft + 1, 0:1], bias4[nfft + 1 : nfft + 2, 0:1]], 1
        )
        o_small[1:2, :width] = jnp.sum(acc_gls[...], axis=0, keepdims=True)
        o_small[2:3, :width] = jnp.sum(acc_gmb[...], axis=0, keepdims=True) * scale


def whole(shape):
    return pl.BlockSpec(shape, lambda *_: (0,) * len(shape))


def fixed(shape):
    return pl.BlockSpec(shape, lambda *_: (0,) * len(shape), pipeline_mode=pl.Buffered(1))


def row_halves(blks, rows, rows8, width, clip=None):
    per, last = rows // rows8, blks * rows // rows8 - 1
    places = [
        (rows, lambda j: j),
        (rows8, lambda j: jnp.maximum(j * per - 1, 0)),
        (rows8, lambda j: jnp.minimum(j * per + per, last)),
    ]
    if clip is None:
        return [pl.BlockSpec((1, n, width), lambda i, j, *_, f=f: (i, f(j), 0)) for n, f in places]
    return [pl.BlockSpec((1, n, width), lambda j, *_, f=f: (clip, f(j), 0)) for n, f in places]


def run_head(bands, offsets, x, edge, cot, cot_edge, weights, turns, consts):
    clips, frames, width = x.shape
    blks = frames // ROWS
    count = clips * frames
    hidden = weights[4].shape[1]
    nfft = turns.shape[1]
    block = lambda i, j, *_: (i * blks + j, 0)
    column = lambda i, j, *_: (0, i * blks + j)
    per_clip = lambda shape: pl.BlockSpec((1,) + shape, lambda i, j, *_: (i, 0, 0))
    in_specs = row_halves(blks, ROWS, edge.shape[1], width)
    in_specs += [per_clip(edge.shape[1:])]
    operands = list(weights) + [turns] + list(consts)
    in_specs += [fixed(cot.shape), per_clip(cot_edge.shape[1:])] + [fixed(v.shape) for v in operands]
    padded = -(-(nfft + 2) // 64) * 64
    row_out = lambda n, dtype: (SDS((count, n), dtype), pl.BlockSpec((ROWS, n), block))
    col_out = (SDS((width, count), BF16), pl.BlockSpec((width, ROWS), column))
    outs = [
        row_out(width, F32),
        row_out(LANES, F32),
        col_out,
        col_out,
        row_out(hidden, BF16),
        row_out(hidden, BF16),
        row_out(hidden, F32),
        row_out(nfft, F32),
        row_out(width, F32),
        row_out(width, BF16),
        row_out(width, BF16),
        col_out,
        col_out,
        (SDS((padded // 2, width), F32), whole((padded // 2, width))),
        (SDS((padded // 2, width), F32), whole((padded // 2, width))),
        (SDS((8, hidden), F32), whole((8, hidden))),
    ]
    wave_tiles = nfft // 2 // LANES
    tiles = width // LANES
    scratch = [pltpu.VMEM((width, hidden), BF16)] * 2 + [pltpu.VMEM((hidden, width), BF16)] * 2
    scratch += [
        pltpu.VMEM((nfft, width), BF16),
        pltpu.VMEM((nfft, width), BF16),
        pltpu.VMEM((2, nfft), F32),
        pltpu.VMEM((8, width), F32),
        pltpu.VMEM((tiles, padded, LANES), F32),
        pltpu.VMEM((nfft + 8, LANES), F32),
        pltpu.VMEM((tiles, ROWS + 2 * edge.shape[1], LANES), F32),
        pltpu.VMEM((tiles, ROWS, LANES), F32),
        pltpu.VMEM((ROWS, LANES), F32),
        pltpu.VMEM((wave_tiles, PAIRS + 8, LANES), F32),
        pltpu.VMEM((tiles, ROWS, LANES), F32),
        pltpu.VMEM((ROWS, nfft), BF16),
        pltpu.VMEM((ROWS, nfft), BF16),
        pltpu.VMEM((width, nfft), F32),
        pltpu.VMEM((8, nfft), F32),
        pltpu.VMEM((8, width), F32),
        pltpu.VMEM((8, ROWS), F32),
        pltpu.VMEM((8, width), F32),
        pltpu.VMEM((8, width), F32),
    ]
    return pl.pallas_call(
        head_kernel,
        grid_spec=pltpu.PrefetchScalarGridSpec(
            num_scalar_prefetch=2,
            grid=(clips, blks),
            in_specs=in_specs,
            out_specs=[s for _, s in outs],
            scratch_shapes=scratch,
        ),
        out_shape=[s for s, _ in outs],
        compiler_params=pltpu.CompilerParams(vmem_limit_bytes=VMEM),
        cost_estimate=pl.CostEstimate(flops=80_000_000_000, bytes_accessed=90_000_000, transcendentals=0),
        name="head",
    )(bands, offsets, x, x, x, edge, cot, cot_edge, *operands)


def ffn_kernel(
    gb_h, gb_l, gbt_h, gbt_l, act_h, act_l, slope, adt_h, adt_l, down_w, *refs
):
    o_keep, o_send, o_gub, o_gu_h, o_gu_l, dw_h, dw_l, acc_gdn, acc_gup, acc_gub = refs[-10:]
    step = pl.program_id(0)
    hidden, width = down_w.shape

    @pl.when(step == 0)
    def _():
        dw_h[...], dw_l[...] = split(down_w[...])
        for ref in (acc_gdn, acc_gup, acc_gub):
            ref[...] = jnp.zeros_like(ref)

    acc_gdn[...] += dot3((gbt_h[...], gbt_l[...]), (act_h[...], act_l[...]))
    cols = 256
    for j in range(hidden // cols):
        part = slice(j * cols, (j + 1) * cols)
        gu = dot3((gb_h[...], gb_l[...]), (dw_h[part, :], dw_l[part, :]), NT) * slope[:, part]
        acc_gub[:, part] += fold8(gu)
        gs = split(gu)
        o_gu_h[:, part], o_gu_l[:, part] = gs
        acc_gup[:, part] += dot3((adt_h[...], adt_l[...]), gs)

    @pl.when(step == pl.num_programs(0) - 1)
    def _():
        o_gub[...] = jnp.sum(acc_gub[...], axis=0, keepdims=True)
        core = lax.axis_index("clip") % 2
        rows = hidden // 2
        for ref, half in ((o_keep, core), (o_send, 1 - core)):
            mine = pl.ds(pl.multiple_of(half * rows, rows), rows)
            ref[0:rows, :] = acc_gdn[:, mine].T
            ref[rows:, :] = acc_gup[:, mine].T


def after(values):
    return [pl.BlockSpec(memory_space=pl.ANY)] * len(values), list(values)


def run_ffn(gb, gbt, act, slope, adt, down_w, hidden, part, waits=()):
    count, width = gb[0].shape
    rows = 512
    row = lambda i, *_: (i, 0)
    mine = lambda i, *_: (i, part)
    col = lambda i, *_: (0, i)
    in_specs = [pl.BlockSpec((rows, width), row)] * 2 + [pl.BlockSpec((width, rows), col)] * 2
    in_specs += [pl.BlockSpec((rows, hidden), mine)] * 3 + [pl.BlockSpec((width, rows), col)] * 2
    in_specs += [pl.BlockSpec((hidden, width), lambda i, *_: (part, 0), pipeline_mode=pl.Buffered(1))]
    wait_specs, waits = after(waits)
    return pl.pallas_call(
        ffn_kernel,
        grid=(count // rows,),
        in_specs=in_specs + wait_specs,
        out_specs=[
            whole((hidden, width)),
            whole((hidden, width)),
            whole((1, hidden)),
            pl.BlockSpec((rows, hidden), row),
            pl.BlockSpec((rows, hidden), row),
        ],
        out_shape=[
            SDS((hidden, width), F32),
            SDS((hidden, width), F32),
            SDS((1, hidden), F32),
            SDS((count, hidden), BF16),
            SDS((count, hidden), BF16),
        ],
        scratch_shapes=[pltpu.VMEM((hidden, width), BF16)] * 2
        + [pltpu.VMEM((width, hidden), F32)] * 2
        + [pltpu.VMEM((8, hidden), F32)],
        compiler_params=pltpu.CompilerParams(vmem_limit_bytes=VMEM),
        cost_estimate=pl.CostEstimate(
            flops=18 * count * width * hidden, bytes_accessed=12 * count * hidden, transcendentals=0
        ),
        name="ffn_grads",
    )(*gb, *gbt, *act, slope, *adt, down_w, *waits)


def norm_kernel(sizes, clip, bands, *refs):
    gu = refs[: 2 * len(sizes)]
    up_w, norm, istd, scale_t = refs[2 * len(sizes) : 2 * len(sizes) + 4]
    o_gh, o_scale, o_shift, up_h, up_l, nat4, acc_scale, acc_shift = refs[-8:]
    blk, blks = pl.program_id(0), pl.num_programs(0)
    band = bands[clip]
    width = norm.shape[1]
    tiles = width // LANES

    @pl.when(blk == 0)
    def _():
        up_h[...], up_l[...] = split(up_w[...])
        for ref in (o_scale, o_shift, acc_scale, acc_shift):
            ref[...] = jnp.zeros_like(ref)

    ga, at = None, 0
    for j, hidden in enumerate(sizes):
        cols = slice(at, at + hidden)
        term = dot3((gu[2 * j][...], gu[2 * j + 1][...]), (up_h[:, cols], up_l[:, cols]), NT)
        ga = term if ga is None else ga + term
        at += hidden
    normed = norm[...]
    acc_scale[...] += fold8(ga * normed)
    acc_shift[...] += fold8(ga)
    gn = ga * scale_t[pl.ds(band, 1), :]
    mean = jnp.sum(gn, axis=1, keepdims=True) * (1.0 / width)
    along = jnp.sum(gn * normed, axis=1, keepdims=True) * (1.0 / width)
    gh = istd[:, 0:1] * (gn - mean - normed * along)
    for par in range(2):
        for t in range(tiles):
            nat4[t, pl.ds(par, PAIRS, stride=2), :] = gh[par * PAIRS : (par + 1) * PAIRS, t * LANES : (t + 1) * LANES]
    for t in range(tiles):
        o_gh[:, t * LANES : (t + 1) * LANES] = nat4[t]

    @pl.when(blk == blks - 1)
    def _():
        o_scale[pl.ds(band, 1), :] = jnp.sum(acc_scale[...], axis=0, keepdims=True)
        o_shift[pl.ds(band, 1), :] = jnp.sum(acc_shift[...], axis=0, keepdims=True)


def run_norm(bands, gus, up_w, norm, istd, scale_t, clips, clip, waits=()):
    count, width = norm.shape
    blks = count // clips // ROWS
    block = lambda j, *_: (clip * blks + j, 0)
    flat = [v for pair in gus for v in pair]
    in_specs = [pl.BlockSpec((ROWS, v.shape[1]), block) for v in flat]
    in_specs += [fixed(up_w.shape), pl.BlockSpec((ROWS, width), block)]
    in_specs += [pl.BlockSpec((ROWS, LANES), block), fixed(scale_t.shape)]
    wait_specs, waits = after(waits)
    return pl.pallas_call(
        functools.partial(norm_kernel, [pair[0].shape[1] for pair in gus], clip),
        grid_spec=pltpu.PrefetchScalarGridSpec(
            num_scalar_prefetch=1,
            grid=(blks,),
            in_specs=in_specs + wait_specs,
            out_specs=[pl.BlockSpec((ROWS, width), lambda j, *_: (j, 0)), whole(scale_t.shape), whole(scale_t.shape)],
            scratch_shapes=[pltpu.VMEM(up_w.shape, BF16)] * 2
            + [pltpu.VMEM((width // LANES, ROWS, LANES), F32)]
            + [pltpu.VMEM((8, width), F32)] * 2,
        ),
        out_shape=[SDS((count // clips, width), F32), SDS(scale_t.shape, F32), SDS(scale_t.shape, F32)],
        compiler_params=pltpu.CompilerParams(vmem_limit_bytes=VMEM),
        cost_estimate=pl.CostEstimate(flops=5_000_000_000, bytes_accessed=12_000_000, transcendentals=0),
        name="norm_grads",
    )(bands, *flat, up_w, norm, istd, scale_t, *waits)


def conv_kernel(
    clip, offsets, x_ref, x_up, x_down, edge_ref, gh_ref, gh_up, gh_down, gh_edge, gm_ref, conv_w, acc_in, *refs
):
    o_gi, o_acc, pad4, gh4 = refs[-4:]
    blk, blks = pl.program_id(0), pl.num_programs(0)
    rows, width = x_ref.shape[1], x_ref.shape[2]
    tiles = width // LANES
    tm = lax.axis_index("tm")
    local = offsets[clip] - tm * blks * rows
    rows8 = edge_ref.shape[1]
    base = blk * rows

    @pl.when(blk == 0)
    def _():
        o_acc[...] = acc_in[...]

    def masked(value, first):
        row = first + lax.broadcasted_iota(jnp.int32, value.shape, 0)
        return jnp.where(row >= local, value, 0.0)

    def above(edge, up):
        return jnp.where(blk == 0, jnp.where(tm > 0, edge[0], 0.0), up[0])

    def below(edge, down):
        return jnp.where(blk == blks - 1, jnp.where(tm > 0, 0.0, edge[0]), down[0])

    before, after = masked(above(edge_ref, x_up), base - rows8), masked(below(edge_ref, x_down), base + rows)
    g_before, g_after = above(gh_edge, gh_up), below(gh_edge, gh_down)
    middle = masked(x_ref[0], base)
    for t in range(tiles):
        lanes = slice(t * LANES, (t + 1) * LANES)
        pad4[t, 0:rows8, :] = before[:, lanes]
        pad4[t, rows8 : rows8 + rows, :] = middle[:, lanes]
        pad4[t, rows8 + rows :, :] = after[:, lanes]
        gh4[t, 0:rows8, :] = g_before[:, lanes]
        gh4[t, rows8 : rows8 + rows, :] = gh_ref[0, :, lanes]
        gh4[t, rows8 + rows :, :] = g_after[:, lanes]
    chunk = 64
    for r in range(0, rows, chunk):
        shown = base + r + lax.broadcasted_iota(jnp.int32, (chunk, LANES), 0) >= local
        for t in range(tiles):
            lanes = slice(t * LANES, (t + 1) * LANES)
            gh = gh4[t, rows8 + r : rows8 + r + chunk, :]
            o_acc[8 * KERNEL :, lanes] += fold8(gh)
            total = gm_ref[0, r : r + chunk, lanes]
            for k in range(KERNEL):
                first = r + rows8 + KERNEL // 2 - k
                total = total + conv_w[k : k + 1, lanes] * gh4[t, first : first + chunk, :]
                first = r + rows8 - KERNEL // 2 + k
                o_acc[8 * k : 8 * k + 8, lanes] += fold8(gh * pad4[t, first : first + chunk, :])
            o_gi[0, r : r + chunk, lanes] = jnp.where(shown, total, 0.0)


def run_conv(offsets, x, edge, gh, gh_edge, gm, conv_w, clip, so_far, waits=()):
    clips, frames, width = x.shape
    blks = frames // ROWS
    rows8 = edge.shape[1]
    mine = pl.BlockSpec((1, rows8, width), lambda j, *_: (clip, 0, 0))
    padded = pltpu.VMEM((width // LANES, ROWS + 2 * rows8, LANES), F32)
    blocks = row_halves(blks, ROWS, rows8, width, clip)
    in_specs = blocks + [mine] + row_halves(blks, ROWS, rows8, width, 0) + [mine] + blocks[:1]
    grads, acc = so_far
    in_specs += [fixed(conv_w.shape), fixed(acc.shape)]
    operands = [x, x, x, edge, gh, gh, gh, gh_edge, gm, conv_w, acc]
    aliases = {}
    wait_specs, waits = after(waits)
    if grads is not None:
        aliases = {1 + len(operands): 0}
        operands.append(grads)
        in_specs.append(pl.BlockSpec(memory_space=pl.ANY))
    return pl.pallas_call(
        functools.partial(conv_kernel, clip),
        grid_spec=pltpu.PrefetchScalarGridSpec(
            num_scalar_prefetch=1,
            grid=(blks,),
            in_specs=in_specs + wait_specs,
            out_specs=[blocks[0], whole(acc.shape)],
            scratch_shapes=[padded, padded],
        ),
        out_shape=[SDS(x.shape, F32), SDS(acc.shape, F32)],
        input_output_aliases=aliases,
        compiler_params=pltpu.CompilerParams(vmem_limit_bytes=VMEM),
        cost_estimate=pl.CostEstimate(flops=5_000_000_000, bytes_accessed=17_000_000, transcendentals=0),
        name="conv_grads",
    )(offsets, *operands, *waits)


def pack_kernel(acc, small, scales0, scales1, shifts0, shifts1, *refs):
    gubs, o_pack = refs[:-1], refs[-1]
    width = acc.shape[1]
    for k in range(KERNEL + 1):
        o_pack[k : k + 1, :] = jnp.sum(acc[8 * k : 8 * k + 8, :], axis=0, keepdims=True)
    o_pack[8:12, :] = scales0[...] + scales1[...]
    o_pack[12:16, :] = shifts0[...] + shifts1[...]
    o_pack[16:18, :] = small[1:3, :width]
    for i in range(3):
        o_pack[18 + i : 19 + i, :] = small[0:1, i * width : (i + 1) * width]
        gub = jnp.concatenate([v[...] for v in gubs], 1)
        o_pack[21 + i : 22 + i, :] = gub[:, i * width : (i + 1) * width]
    o_pack[24:, :] = jnp.zeros((o_pack.shape[0] - 24, width), F32)


def wave_kernel(
    first_blk, frames, offsets, spec, carry, t1h, t1l, t2h, t2l, t0h, t0l, windows, inverse, *refs
):
    o_wave, o_tail, accs = refs[-3:]
    blk, clip = pl.program_id(0), pl.program_id(1)
    blks, clips = pl.num_programs(0), pl.num_programs(1)
    tiles = accs.shape[1]
    first = (first_blk + blk) * PAIRS
    local = offsets[clip] - lax.axis_index("tm") * frames
    acc5 = accs.at[clip]

    @pl.when(blk == 0)
    def _():
        for t in range(tiles):
            acc5[t, 0:8, :] = carry[0, :, t * LANES : (t + 1) * LANES]

    @pl.when(blk > 0)
    def _():
        for t in range(tiles):
            acc5[t, 0:8, :] = acc5[t, PAIRS : PAIRS + 8, :]

    for t in range(tiles):
        acc5[t, 8:, :] = jnp.zeros((PAIRS, LANES), F32)

    n1, n2 = t1h.shape[0], t2h.shape[0]
    ab = dot3(split(spec[:, :n1]), (t1h[...], t1l[...]))
    cd = dot3(split(spec[:, n1 : n1 + n2]), (t2h[...], t2l[...]))
    p0 = dot3(split(spec[:, n1 + n2 :]), (t0h[...], t0l[...]))
    c1, c2, s1, s2 = fifths()
    sides = []
    for par in range(2):
        rows = slice(par * PAIRS, (par + 1) * PAIRS)
        w = p0.shape[1]
        a, b, c, d, p = ab[rows, :w], ab[rows, w:], cd[rows, :w], cd[rows, w:], p0[rows]
        e1, o1 = p + c1 * a + c2 * c, s1 * b + s2 * d
        e2, o2 = p + c2 * a + c1 * c, s2 * b - s1 * d
        v = [p + a + c, e1 - o1, e2 - o2, e2 + o2, e1 + o1]
        seg = []
        for t in range(2 * tiles):
            part = v[t // 2][:, (t % 2) * LANES : (t % 2 + 1) * LANES]
            seg.append(part * windows[par : par + 1, t * LANES : (t + 1) * LANES])
        sides.append(seg)
    even, odd = sides
    mid = tiles // 2
    right = lax.broadcasted_iota(jnp.int32, (PAIRS, LANES), 1) >= LANES // 2
    for t in range(tiles):
        here = even[t]
        if t > mid:
            here = here + odd[t]
        if t == mid:
            here = here + jnp.where(right, odd[t], 0.0)
        acc5[t, 0:PAIRS, :] += here
        acc5[t, 1 : PAIRS + 1, :] += even[tiles + t] + odd[tiles + t]
        if t < mid:
            acc5[t, 2 : PAIRS + 2, :] += odd[t]
        if t == mid:
            acc5[t, 2 : PAIRS + 2, :] += jnp.where(right, 0.0, odd[t])
        value = acc5[t, 0:PAIRS, :] * inverse_envelope(first, local, inverse, t, PAIRS)
        o_wave[pl.ds(clips * t + clip, PAIRS, stride=clips * tiles), :] = value

    @pl.when(blk == blks - 1)
    def _():
        for t in range(tiles):
            o_tail[0, :, t * LANES : (t + 1) * LANES] = acc5[t, PAIRS : PAIRS + 8, :]


def run_wave(offsets, spec, consts, clips, first_blk, blks, carry, wave=None, waits=()):
    count, nfft = spec.shape
    all_blks = count // clips // ROWS
    tiles = nfft // 2 // LANES
    rows = clips * PAIRS * tiles
    in_specs = [pl.BlockSpec((ROWS, nfft), lambda j, i, *_: (i * all_blks + first_blk + j, 0))]
    in_specs += [pl.BlockSpec((1, 8, nfft // 2), lambda j, i, *_: (i, 0, 0))]
    in_specs += [fixed(v.shape) for v in consts]
    operands = [spec, carry, *consts]
    aliases = {}
    wait_specs, waits = after(waits)
    if wave is not None:
        aliases = {1 + len(operands): 0}
        operands.append(wave)
        in_specs.append(pl.BlockSpec(memory_space=pl.ANY))
    return pl.pallas_call(
        functools.partial(wave_kernel, first_blk, count // clips),
        grid_spec=pltpu.PrefetchScalarGridSpec(
            num_scalar_prefetch=1,
            grid=(blks, clips),
            in_specs=in_specs + wait_specs,
            out_specs=[
                pl.BlockSpec((rows, LANES), lambda j, i, *_: (first_blk + j, 0)),
                pl.BlockSpec((1, 8, nfft // 2), lambda j, i, *_: (i, 0, 0)),
            ],
            scratch_shapes=[pltpu.VMEM((clips, tiles, PAIRS + 8, LANES), F32)],
        ),
        out_shape=[SDS((rows * all_blks, LANES), F32), SDS((clips, 8, nfft // 2), F32)],
        input_output_aliases=aliases,
        compiler_params=pltpu.CompilerParams(vmem_limit_bytes=VMEM),
        cost_estimate=pl.CostEstimate(flops=5_000_000_000, bytes_accessed=8_000_000, transcendentals=0),
        name="wave",
    )(offsets, *operands, *waits)


def levels():
    clip = [("clip", 1 << i) for i in range((lax.axis_size("clip") - 1).bit_length())]
    tm = [("tm", 1 << i) for i in range((lax.axis_size("tm") - 1).bit_length())]
    return clip[:1] + clip[1:2] + tm + clip[2:]


def exchange(value, level):
    axis, distance = level
    return lax.ppermute(value, axis, [(i, i ^ distance) for i in range(lax.axis_size(axis))])


def side(level):
    axis, distance = level
    return lax.axis_index(axis) // distance % 2


class Sums:
    def __init__(self):
        self.running = []

    def add(self, steps, holds=()):
        entry = {"steps": steps, "holds": holds, "count": 0, "sent": None, "came": None, "left": 0, "sum": None}
        self.step(entry, None)
        self.running.append(entry)
        return entry

    def step(self, entry, value):
        try:
            entry["sent"] = entry["steps"].send(value)
            while entry["sent"][1] == levels()[0]:
                entry["sent"] = entry["steps"].send(exchange(*entry["sent"]))
        except StopIteration as stop:
            entry["sent"], entry["sum"] = None, stop.value

    def waits(self):
        sent = []
        for entry in self.running:
            if entry["came"] is None and entry["sent"] is not None:
                entry["came"] = exchange(*entry["sent"])
                entry["left"] = dict(entry["holds"]).get(entry["count"], 1)
                entry["count"] += 1
                sent.append(entry["sent"][0])
        return sent

    def advance(self, results):
        done = []
        for entry in self.running:
            if entry["came"] is not None:
                entry["left"] -= 1
                if entry["left"] <= 0:
                    done.append(entry)
        if done:
            came, results = lax.optimization_barrier(([entry["came"] for entry in done], results))
            for entry, value in zip(done, came):
                entry["came"] = None
                self.step(entry, value)
        return results

    def finish(self, entry):
        while entry["sum"] is None:
            self.waits()
            self.advance(())
        return entry["sum"]


def halves_steps(keep, send, turn):
    core, *rest = levels()
    first, last = rest[:2], rest[2:]
    if turn % 2:
        first = first[::-1]
    value = keep + (yield send, core)
    for level in first:
        rows, s = value.shape[0] // 2, side(level)
        away = lax.dynamic_slice_in_dim(value, (1 - s) * rows, rows)
        value = lax.dynamic_slice_in_dim(value, s * rows, rows) + (yield away, level)
    for level in last:
        value = value + (yield value, level)
    for level in first[::-1]:
        value = jnp.concatenate([value, (yield value, level)])
    other = yield value, core
    return value, other, [core, *first]


def whole_steps(value):
    for level in levels():
        value = value + (yield value, level)
    return value


def natural_blocks(order, mine, other, copy):
    s = [side(level) for level in order]
    rows = mine.shape[0] // 4
    for half in range(2):
        for ref, here in ((mine, s[0] == half), (other, s[0] != half)):

            @pl.when(here)
            def _(ref=ref, half=half):
                for a in range(2):
                    for b in range(2):
                        first = (2 * jnp.bitwise_xor(a, s[1]) + jnp.bitwise_xor(b, s[2])) * rows
                        copy(half, a, b, ref[pl.ds(pl.multiple_of(first, 8), rows), :])


def head_order_kernel(order, mine, other, *refs):
    out = refs[-1]

    def copy(half, a, b, block):
        rows = block.shape[0]
        first = ((2 * half + a) * 2 + b) * rows
        end = min(first + rows, out.shape[0])
        out[first:end, :] = block[: end - first]

    natural_blocks(order, mine, other, copy)


def ffn_order_kernel(order, mine, other, *refs):
    o_down, o_up, up_t = refs[-3:]

    def copy(half, a, b, block):
        rows = block.shape[0]
        first = (2 * half + b) * rows
        (up_t if a else o_down)[first : first + rows, :] = block

    natural_blocks(order, mine, other, copy)
    for c in range(0, up_t.shape[0], LANES):
        o_up[:, c : c + LANES] = up_t[c : c + LANES, :].T


def order_head(total, rows, waits=()):
    mine, other, order = total
    wait_specs, waits = after(waits)
    return pl.pallas_call(
        functools.partial(head_order_kernel, order),
        in_specs=[pl.BlockSpec(memory_space=pltpu.VMEM)] * 2 + wait_specs,
        out_shape=SDS((rows, mine.shape[1]), F32),
        compiler_params=pltpu.CompilerParams(vmem_limit_bytes=VMEM),
        name="head_order",
    )(mine, other, *waits)


def order_ffn(total, hidden, part, so_far, waits=()):
    mine, other, order = total
    size, width = mine.shape[0], mine.shape[1]
    so_far = list(so_far)
    wait_specs, waits = after(waits)
    return pl.pallas_call(
        functools.partial(ffn_order_kernel, order),
        grid=(1,),
        in_specs=[whole(mine.shape)] * 2 + [pl.BlockSpec(memory_space=pl.ANY)] * len(so_far) + wait_specs,
        out_specs=[
            pl.BlockSpec((size, width), lambda i: (part, 0)),
            pl.BlockSpec((width, size), lambda i: (0, part)),
        ],
        out_shape=[SDS((hidden, width), F32), SDS((width, hidden), F32)],
        scratch_shapes=[pltpu.VMEM((size, width), F32)],
        input_output_aliases={2 + i: i for i in range(len(so_far))},
        compiler_params=pltpu.CompilerParams(vmem_limit_bytes=VMEM),
        name="ffn_order",
    )(mine, other, *so_far, *waits)


def unpack_kernel(pack, gcw, gcb, gscale, gshift, gls, gdb, ghb, gub):
    width = pack.shape[1]
    gcw[...] = pack[0:KERNEL, :]
    gcb[...] = pack[KERNEL : KERNEL + 1, :].reshape(width)
    gscale[...] = pack[8:12, :]
    gshift[...] = pack[12:16, :]
    gls[...] = pack[16:17, :].reshape(width)
    gdb[...] = pack[17:18, :].reshape(width)
    rows = [pack[18 + i : 19 + i, :] for i in range(6)]
    ghb[...] = jnp.concatenate(rows[:3], 1)[:, : ghb.shape[0]].reshape(ghb.shape[0])
    gub[...] = jnp.concatenate(rows[3:], 1).reshape(gub.shape[0])


def edges(value, index):
    n = value.shape[1]
    return jnp.where(index == 0, value[:, n - 8 :], value[:, :8])


def to_chunks(wave):
    clips, samples = wave.shape
    return wave.reshape(clips, samples // LANES, LANES).transpose(1, 0, 2).reshape(-1, LANES)


def from_chunks(chunks, clips):
    rows = chunks.shape[0] // clips
    return chunks.reshape(rows, clips, LANES).transpose(1, 0, 2).reshape(clips, rows * LANES)


def body(
    inputs,
    band_ids,
    offsets,
    conv_weight,
    conv_bias,
    scale_table,
    shift_table,
    up_weight,
    up_bias,
    down_weight,
    down_bias,
    layer_scale,
    head_weight,
    head_bias,
    wave_cotangent,
):
    clips, frames, width = inputs.shape
    assert lax.axis_size("tm") == 2
    nfft = head_weight.shape[1] - 2
    half = nfft // 2
    hidden = up_weight.shape[1]
    tm = lax.axis_index("tm")
    core = lax.axis_index("clip") % 2
    swap = lambda v: lax.ppermute(v, "tm", [(0, 1), (1, 0)])
    transforms, windows, inverse, turns = tables(nfft)
    dft = [jnp.asarray(v) for pair in transforms for v in pair]
    consts = dft + [jnp.asarray(windows), jnp.asarray(inverse)]

    edge = swap(edges(inputs, tm))
    cot_edge = swap(jnp.pad(wave_cotangent[:, :nfft].reshape(clips, 2, half), ((0, 0), (0, 6), (0, 0))))
    weights = (
        conv_weight,
        conv_bias,
        scale_table,
        shift_table,
        up_weight,
        up_bias,
        down_weight,
        down_bias,
        layer_scale,
        head_weight.T,
        head_bias,
    )
    (
        norm, istd, adt_h, adt_l, act_h, act_l, slope, spec, gm, gb_h, gb_l, gbt_h, gbt_l, hg_keep, hg_send, small,
    ) = run_head(
        band_ids, offsets, inputs, edge, to_chunks(wave_cotangent), cot_edge, weights, jnp.asarray(turns), consts
    )

    sums = Sums()
    turn = 0
    totals = [sums.add(halves_steps(hg_keep, hg_send, turn), {5: 2})]
    blks = frames // ROWS
    carry = jnp.zeros((clips, 8, half), F32)
    gubs, gus = [], []
    for size, part in FFN_PARTS:
        results = run_ffn(
            (gb_h, gb_l), (gbt_h, gbt_l), (act_h, act_l), slope, (adt_h, adt_l), down_weight, size, part,
            waits=sums.waits(),
        )
        keep, send, gub, gu_h, gu_l = sums.advance(results)
        turn += 1
        totals.append(sums.add(halves_steps(keep, send, turn), {3: 2} if turn == 1 else {}))
        gubs.append(gub)
        gus.append((gu_h, gu_l))
    normed = []
    for clip in range(clips):
        results = run_norm(band_ids, gus, up_weight, norm, istd, scale_table, clips, clip, waits=sums.waits())
        normed.append(sums.advance(results))
    gh = [v[0][None] for v in normed]
    gh_edge = swap(jnp.concatenate([edges(v, tm) for v in gh]))
    wave, carry = run_wave(offsets, spec, consts, clips, 0, blks // 2, carry, waits=sums.waits())
    wave, carry = sums.advance((wave, carry))
    so_far = (None, jnp.zeros((8 * (KERNEL + 1), width), F32))
    gm = gm.reshape(clips, frames, width)
    for clip in range(clips):
        so_far = run_conv(
            offsets, inputs, edge, gh[clip], gh_edge, gm, conv_weight, clip, so_far, waits=sums.waits()
        )
        so_far = sums.advance(so_far)
    grad_inputs, acc = so_far
    pack = pl.pallas_call(pack_kernel, out_shape=SDS((32, width), F32), name="pack")(
        acc, small, *[v[1] for v in normed], *[v[2] for v in normed], *gubs
    )
    totals.append(sums.add(whole_steps(pack)))

    wave, tail = run_wave(
        offsets, spec, consts, clips, blks // 2, blks - blks // 2, carry, wave, waits=sums.waits()
    )
    wave, tail = sums.advance((wave, tail))
    arrived = lax.ppermute(tail[:, :2].reshape(clips, nfft), "tm", [(0, 1)])
    arrived = arrived * jnp.tile(jnp.asarray(inverse[3:4]), (1, 2))
    wave = wave.at[: clips * nfft // LANES].add(to_chunks(arrived))
    waveform = from_chunks(wave, clips)

    head_total, *ffn_totals, small_total = totals
    head_grad = order_head(sums.finish(head_total), nfft + 2, sums.waits())
    head_grad = sums.advance(head_grad)
    ffn_grads = ()
    for (_, part), total in zip(FFN_PARTS, ffn_totals):
        total = sums.finish(total)
        ffn_grads = order_ffn(total, hidden, part, ffn_grads, sums.waits())
        ffn_grads = sums.advance(ffn_grads)
    down_grad, up_grad = ffn_grads
    pack = sums.finish(small_total)
    small_shapes = [(KERNEL, width), (width,), scale_table.shape, scale_table.shape]
    small_shapes += [(width,), (width,), (nfft + 2,), (hidden,)]
    gcw, gcb, gscale, gshift, gls, gdb, ghb, gub = pl.pallas_call(
        unpack_kernel, out_shape=[SDS(shape, F32) for shape in small_shapes], name="unpack"
    )(pack)
    return (
        waveform,
        grad_inputs,
        gcw,
        gcb,
        gscale,
        gshift,
        up_grad,
        gub,
        down_grad,
        gdb,
        gls,
        head_grad.T,
        ghb,
    )


def solution(mesh):
    in_specs = (P("clip", "tm", None), P("clip"), P("clip")) + (P(),) * 11 + (P("clip", "tm"),)
    out_specs = (P("clip", "tm"), P("clip", "tm", None)) + (P(),) * 11
    return jax.shard_map(body, mesh=mesh, in_specs=in_specs, out_specs=out_specs, check_vma=False)
```

```python
import functools

import jax
import jax.numpy as jnp
import ml_dtypes
import numpy as np
from jax import lax
from jax.experimental import pallas as pl
from jax.experimental.pallas import tpu as pltpu
from jax.sharding import PartitionSpec as P

KERNEL = 7
CLASSES = ((1, 4), (2, 3), (0,))
F32 = jnp.float32
BF16 = jnp.bfloat16
LANES = 128
PAIRS = 128
ROWS = 2 * PAIRS
VMEM = 60 * 2**20
UP_PARTS = ((1024, 0), (512, 2))
HEAD_ROWS = 704
SDS = jax.ShapeDtypeStruct

SIN_POLY = (0.999999996, -0.166666580, 8.33305023e-03, -1.98090119e-04, 2.60507821e-06)
COS_POLY = (1.0, -0.499999994, 4.16666361e-02, -1.38883598e-03, 2.47600798e-05, -2.60500270e-07)

NN = (((1,), (0,)), ((), ()))
NT = (((1,), (1,)), ((), ()))


def split(x):
    high = x.astype(BF16)
    return high, (x - high.astype(F32)).astype(BF16)


def dot(a, b, dims=NN):
    return lax.dot_general(a, b, dims, preferred_element_type=F32)


def dot3(a, b, dims=NN):
    return dot(a[0], b[0], dims) + (dot(a[0], b[1], dims) + dot(a[1], b[0], dims))


def fold8(x):
    return jnp.sum(x.reshape(x.shape[0] // 8, 8, x.shape[1]), axis=0)


def np_split(x):
    high = x.astype(np.float32).astype(ml_dtypes.bfloat16)
    return high, (x - high.astype(np.float64)).astype(ml_dtypes.bfloat16)


@functools.lru_cache(None)
def tables(nfft):
    fifth, half, hop = nfft // 5, nfft // 2, nfft // 4
    bins = np.arange(1, half)
    first, second = (np.concatenate([bins[bins % 5 == r] for r in rs]) for rs in CLASSES[:2])
    zero = np.arange(0, half, 5)
    n0 = np.arange(fifth)

    def paired(ks, residue):
        sign = np.where(ks % 5 == residue, 1.0, -1.0)[:, None]
        turn = 2 * np.pi * ((sign * ks[:, None] * n0[None]) % nfft) / nfft
        weight = 2.0 / nfft
        real = np.concatenate([weight * np.cos(turn), weight * np.sin(turn)], 1)
        imag = np.concatenate([-sign * weight * np.sin(turn), sign * weight * np.cos(turn)], 1)
        return np.concatenate([real, imag], 0)

    turn = 2 * np.pi * ((zero[:, None] * n0[None]) % nfft) / nfft
    weight = np.where(zero == 0, 1.0, 2.0)[:, None] / nfft
    real, imag = weight * np.cos(turn), -weight * np.sin(turn)
    imag[0] = np.cos(np.pi * n0) / nfft
    transforms = [np_split(t) for t in (paired(first, 1), paired(second, 2), np.concatenate([real, imag], 0))]
    n = np.arange(nfft)
    window = 0.5 - 0.5 * np.cos(2 * np.pi * n / nfft)
    windows = np.stack([window, np.roll(window, hop)]).astype(np.float32)
    squares = np.cumsum((window**2).reshape(4, hop), axis=0)
    inverse = np.tile(1.0 / np.maximum(squares, 1.0), (1, 2)).astype(np.float32)
    turns = np.zeros(nfft)
    place = 0
    for ks in (first, second, zero):
        turns[place + len(ks) : place + 2 * len(ks)] = -(np.pi / 2) * (ks % 4)
        place += 2 * len(ks)
    return transforms, windows, inverse, turns.astype(np.float32)[None]


def class_places(nfft):
    length, places, at = nfft // 10, [], 0
    for residues in CLASSES:
        for offset in (0, nfft // 2 + 1):
            for r in residues:
                places.append((at, offset + r))
                at += length
    return places


def sin_cos(x):
    turns = jnp.round(x * np.float32(0.5 / np.pi))
    h = x * 0.5 - turns * np.float32(3.140625)
    h = h - turns * np.float32(9.67502593994140625e-4)
    h = h - turns * np.float32(1.509957990978376432e-7)
    z = h * h
    s = np.float32(SIN_POLY[-1])
    for c in SIN_POLY[-2::-1]:
        s = s * z + np.float32(c)
    s = s * h
    cosine = np.float32(COS_POLY[-1])
    for c in COS_POLY[-2::-1]:
        cosine = cosine * z + np.float32(c)
    twice = s + s
    return twice * cosine, 1.0 - twice * s


def fifths():
    a = 2 * np.pi / 5
    return [np.float32(v) for v in (np.cos(a), np.cos(2 * a), np.sin(a), np.sin(2 * a))]


def inverse_envelope(first_pair, offset, table_ref, tile, rows):
    lane = tile * LANES + lax.broadcasted_iota(jnp.int32, (rows, LANES), 1)
    row = lax.broadcasted_iota(jnp.int32, (rows, LANES), 0)
    half = table_ref.shape[1] // 2
    since = 2 * (first_pair + row) + (lane >= half).astype(jnp.int32) - offset
    value = jnp.where(since < 0, 1.0, 1.0)
    for i in range(4):
        value = jnp.where(since >= i, table_ref[i : i + 1, tile * LANES : (tile + 1) * LANES], value)
    return value


def head_kernel(
    bands,
    offsets,
    x_ref,
    x_up,
    x_down,
    edge_ref,
    cot_ref,
    cot_edge,
    conv_w,
    conv_b,
    scale_t,
    shift_t,
    up_w,
    up_b,
    down_w,
    down_b,
    layer_scale,
    head_wt,
    head_b,
    turns,
    t1h,
    t1l,
    t2h,
    t2l,
    t0h,
    t0l,
    windows,
    inverse,
    o_norm,
    o_istd,
    o_adt_h,
    o_adt_l,
    o_act_h,
    o_act_l,
    o_slope,
    o_spec,
    o_gm,
    o_gb_h,
    o_gb_l,
    o_gbt_h,
    o_gbt_l,
    o_keep,
    o_send,
    o_small,
    up_h,
    up_l,
    down_h,
    down_l,
    head_h,
    head_l,
    head_bias,
    ext_w,
    head4,
    bias4,
    pad4,
    nrm4,
    istd1,
    gs5,
    gm4,
    gl_h,
    gl_l,
    acc_ghw,
    acc_ghb,
    acc_ghwe,
    acc_ghbe,
    acc_gls,
    acc_gmb,
):
    clip, blk = pl.program_id(0), pl.program_id(1)
    clips, blks = pl.num_programs(0), pl.num_programs(1)
    width = x_ref.shape[2]
    frames = blks * ROWS
    tiles = width // LANES
    nfft = turns.shape[1]
    half = nfft // 2
    tm = lax.axis_index("tm")
    band = bands[clip]
    local = offsets[clip] - tm * frames
    rows8 = edge_ref.shape[1]
    places = class_places(nfft)

    @pl.when((clip == 0) & (blk == 0))
    def _():
        up_h[...], up_l[...] = split(up_w[...])
        down_h[...], down_l[...] = split(down_w[...])
        for t in range(tiles):
            head4[t, 0 : nfft + 2, :] = head_wt[:, t * LANES : (t + 1) * LANES]
        bias = head_b[...].reshape(1, nfft + 2)
        for c in range(0, nfft, LANES):
            bias4[c : c + LANES, :] = jnp.broadcast_to(bias[:, c : c + LANES], (LANES, LANES)).T
        for c in (nfft, nfft + 1):
            bias4[c : c + 1, :] = jnp.broadcast_to(bias[:, c : c + 1], (1, LANES))
        for at, first in places:
            rows = jnp.concatenate([head4[t, pl.ds(first, LANES, stride=5), :] for t in range(tiles)], 1)
            head_h[at : at + LANES, :], head_l[at : at + LANES, :] = split(rows)
            moved = bias4[pl.ds(first, LANES, stride=5), :].T[0:1, :]
            head_bias[0:1, at : at + LANES] = moved
            head_bias[1:2, at : at + LANES] = moved + turns[:, at : at + LANES]
        ext_w[0:1, :] = head_wt[half : half + 1, :]
        ext_w[1:2, :] = head_wt[nfft + 1 : nfft + 2, :]
        ext_w[2:8, :] = jnp.zeros((6, width), F32)
        for ref in (acc_ghw, acc_ghb, acc_ghwe, acc_ghbe, acc_gls, acc_gmb):
            ref[...] = jnp.zeros_like(ref)

    base = pl.multiple_of(blk * ROWS, ROWS)

    def masked(value, first):
        row = first + lax.broadcasted_iota(jnp.int32, value.shape, 0)
        return jnp.where(row >= local, value, 0.0)

    before = masked(jnp.where(blk == 0, jnp.where(tm > 0, edge_ref[0], 0.0), x_up[0]), base - rows8)
    after = masked(jnp.where(blk == blks - 1, jnp.where(tm > 0, 0.0, edge_ref[0]), x_down[0]), base + ROWS)
    middle = masked(x_ref[0], base)
    for t in range(tiles):
        lanes = slice(t * LANES, (t + 1) * LANES)
        pad4[t, 0:rows8, :] = before[:, lanes]
        pad4[t, rows8 : rows8 + ROWS, :] = middle[:, lanes]
        pad4[t, rows8 + ROWS :, :] = after[:, lanes]
    bias = conv_b[...].reshape(1, width)
    chunk = 64
    for r in range(0, ROWS, chunk):
        parts = []
        for t in range(tiles):
            lanes = slice(t * LANES, (t + 1) * LANES)
            total = bias[:, lanes]
            for k in range(KERNEL):
                first = r + rows8 - KERNEL // 2 + k
                total = total + pad4[t, first : first + chunk, :] * conv_w[k : k + 1, lanes]
            parts.append(total)
        mean = jnp.sum(sum(parts[1:], parts[0]), axis=1, keepdims=True) * (1.0 / width)
        parts = [p - mean for p in parts]
        squares = [p * p for p in parts]
        variance = jnp.sum(sum(squares[1:], squares[0]), axis=1, keepdims=True) * (1.0 / width)
        istd = lax.rsqrt(variance + 1e-6)
        for t in range(tiles):
            nrm4[t, r : r + chunk, :] = parts[t] * istd
        istd1[r : r + chunk, :] = jnp.broadcast_to(istd, (chunk, LANES))

    def by_parity(ref, first):
        return jnp.concatenate(
            [
                jnp.concatenate([ref[t, pl.ds(first + par, PAIRS, stride=2), :] for t in range(tiles)], 1)
                for par in range(2)
            ],
            0,
        )

    normed = by_parity(nrm4, 0)
    o_norm[...] = normed
    for par in range(2):
        o_istd[par * PAIRS : (par + 1) * PAIRS, :] = istd1[pl.ds(par, PAIRS, stride=2), :]
    adapted = normed * scale_t[pl.ds(band, 1), :] + shift_t[pl.ds(band, 1), :]
    ad = split(adapted)
    o_adt_h[...], o_adt_l[...] = ad[0].T, ad[1].T

    first_pair = pl.multiple_of(blk * PAIRS, PAIRS)
    wave_tiles = gs5.shape[0]
    pairs = frames // 2
    next_pair = jnp.minimum(first_pair + PAIRS, pairs - 8)
    for t in range(wave_tiles):
        lanes = slice(t * LANES, (t + 1) * LANES)
        stride = clips * wave_tiles
        value = cot_ref[pl.ds(stride * first_pair + clips * t + clip, PAIRS, stride=stride), :]
        gs5[t, 0:PAIRS, :] = value * inverse_envelope(first_pair, local, inverse, t, PAIRS)
        value = cot_ref[pl.ds(stride * next_pair + clips * t + clip, 8, stride=stride), :]
        value = jnp.where(blk == blks - 1, jnp.where(tm > 0, 0.0, cot_edge[0, :, lanes]), value)
        gs5[t, PAIRS : PAIRS + 8, :] = value * inverse_envelope(first_pair + PAIRS, local, inverse, t, 8)
    now, one, two = ([gs5[t, d : d + PAIRS, :] for t in range(wave_tiles)] for d in range(3))
    mid = wave_tiles // 2
    right = lax.broadcasted_iota(jnp.int32, (PAIRS, LANES), 1) >= LANES // 2
    odd = two[:mid] + [jnp.where(right, now[mid], two[mid])] + now[mid + 1 :] + one
    c1, c2, s1, s2 = fifths()
    folded = []
    for par, segment in enumerate((now + one, odd)):
        seg = [v * windows[par : par + 1, t * LANES : (t + 1) * LANES] for t, v in enumerate(segment)]
        v = [jnp.concatenate(seg[2 * j : 2 * j + 2], 1) for j in range(5)]
        p14, m41, p23, m32 = v[1] + v[4], v[4] - v[1], v[2] + v[3], v[3] - v[2]
        folded.append(
            (
                v[0] + p14 + p23,
                v[0] + c1 * p14 + c2 * p23,
                s1 * m41 + s2 * m32,
                v[0] + c2 * p14 + c1 * p23,
                s2 * m41 - s1 * m32,
            )
        )
    f0, fa, fb, fc, fd = (jnp.concatenate([e, o], 0) for e, o in zip(*folded))
    spectrum_grads = (
        dot3(split(jnp.concatenate([fa, fb], 1)), (t1h[...], t1l[...]), NT),
        dot3(split(jnp.concatenate([fc, fd], 1)), (t2h[...], t2l[...]), NT),
        dot3(split(f0), (t0h[...], t0l[...]), NT),
    )

    hidden = up_h.shape[1]
    step = 256
    up_bias = up_b[...].reshape(1, hidden)
    for j in range(hidden // step):
        cols = slice(j * step, (j + 1) * step)
        upward = dot3(ad, (up_h[:, cols], up_l[:, cols])) + up_bias[:, cols]
        cdf = 0.5 + 0.5 * lax.erf(upward * np.float32(0.7071067811865476))
        density = jnp.exp(upward * upward * -0.5) * np.float32(0.3989422804014327)
        o_slope[:, cols] = cdf + upward * density
        o_act_h[:, cols], o_act_l[:, cols] = split(upward * cdf)
    branch = dot3((o_act_h[...], o_act_l[...]), (down_h[...], down_l[...])) + down_b[...].reshape(1, width)
    scale = layer_scale[...].reshape(1, width)
    residual = by_parity(pad4, rows8) + scale * branch
    res = split(residual)
    res_t = res[0].T, res[1].T

    bias = head_b[...].reshape(1, nfft + 2)
    ext = split(ext_w[...])
    ext_logits = dot3(ext, res, NT)
    lane = lax.broadcasted_iota(jnp.int32, (1, ROWS), 1)
    ext_frame = base + jnp.where(lane < PAIRS, 2 * lane, 2 * (lane - PAIRS) + 1)
    ext_present = ext_frame >= local

    def magnitudes(logits, present):
        raw = jnp.where(present, jnp.exp(logits), 0.0)
        squashed = jnp.tanh(raw * np.float32(0.01))
        return 100.0 * squashed, raw * (1.0 - squashed * squashed)

    ext_mag, ext_slope = magnitudes(ext_logits[0:1] + bias[:, half : half + 1], ext_present)
    ext_sin, ext_cos = sin_cos(ext_logits[1:2] + bias[:, nfft + 1 : nfft + 2])
    ext_real = ext_mag * ext_cos
    ext_imag = ext_mag * ext_sin
    ext_real_col = jnp.concatenate([ext_real, jnp.zeros((7, ROWS), F32)], 0).T[:, 0:1]

    row = lax.broadcasted_iota(jnp.int32, (PAIRS, 1), 0)
    at = 0
    for index, grads in enumerate(spectrum_grads):
        n = grads.shape[1] // 2
        cols = slice(at, at + 2 * n)
        logits = dot3(res, (head_h[cols, :], head_l[cols, :]), NT)
        for par in range(2):
            rows = slice(par * PAIRS, (par + 1) * PAIRS)
            present = base + 2 * row + par >= local
            value = logits[rows] + head_bias[par : par + 1, cols]
            magnitude, slope = magnitudes(value[:, :n], present)
            sine, cosine = sin_cos(value[:, n:])
            real, imag = magnitude * cosine, magnitude * sine
            g_real, g_imag = grads[rows, :n], grads[rows, n:]
            if index == 2:
                corner = lax.broadcasted_iota(jnp.int32, (PAIRS, n), 1) == 0
                shown = jnp.where(corner, ext_real_col[rows], imag)
                g_imag = jnp.where(corner, 0.0, g_imag)
            else:
                shown = imag
            o_spec[rows, at : at + n] = real
            o_spec[rows, at + n : at + 2 * n] = shown
            g_mag = slope * (g_real * cosine + g_imag * sine)
            g_ang = g_imag * real - g_real * imag
            gl = jnp.concatenate([g_mag, g_ang], 1)
            acc_ghb[:, cols] += fold8(gl)
            gl_h[rows, cols], gl_l[rows, cols] = split(gl)
        at += 2 * n

    corner_t = spectrum_grads[2][:, spectrum_grads[2].shape[1] // 2 :].T
    ext_g = corner_t[0:1, :]
    ext_grads = jnp.concatenate(
        [ext_slope * ext_g * ext_cos, -ext_g * ext_imag, jnp.zeros((6, ROWS), F32)], 0
    )
    acc_ghbe[...] += ext_grads
    acc_ghwe[...] += dot3(split(ext_grads), res)
    gl = (gl_h[...], gl_l[...])
    ext_cols = ext_grads.T
    grad_mixed = (
        dot3(gl, (head_h[...], head_l[...]))
        + ext_cols[:, 0:1] * ext_w[0:1, :]
        + ext_cols[:, 1:2] * ext_w[1:2, :]
    )
    acc_ghw[...] += dot3(res_t, gl)
    acc_gls[...] += fold8(grad_mixed * branch)
    acc_gmb[...] += fold8(grad_mixed)
    for par in range(2):
        rows = slice(par * PAIRS, (par + 1) * PAIRS)
        for t in range(tiles):
            gm4[t, pl.ds(par, PAIRS, stride=2), :] = grad_mixed[rows, t * LANES : (t + 1) * LANES]
    for t in range(tiles):
        o_gm[:, t * LANES : (t + 1) * LANES] = gm4[t]
    grad_branch = grad_mixed * scale
    gb = split(grad_branch)
    o_gb_h[...], o_gb_l[...] = gb
    o_gbt_h[...], o_gbt_l[...] = gb[0].T, gb[1].T

    @pl.when((clip == clips - 1) & (blk == blks - 1))
    def _():
        total = jnp.sum(acc_ghb[...], axis=0, keepdims=True)
        for at, first in places:
            for t in range(tiles):
                block = acc_ghw[t * LANES : (t + 1) * LANES, at : at + LANES]
                head4[t, pl.ds(first, LANES, stride=5), :] = block.T
            block = jnp.broadcast_to(total[:, at : at + LANES], (LANES, LANES))
            bias4[pl.ds(first, LANES, stride=5), :] = block.T
        ext_sums = jnp.sum(acc_ghbe[...], axis=1, keepdims=True)
        for i, c in enumerate((half, nfft + 1)):
            for t in range(tiles):
                head4[t, c : c + 1, :] = acc_ghwe[i : i + 1, t * LANES : (t + 1) * LANES]
            bias4[c : c + 1, :] = jnp.broadcast_to(ext_sums[i : i + 1], (1, LANES))
        core = lax.axis_index("clip") % 2
        for here, first in ((core == 0, 0), (core == 1, half + 1)):

            @pl.when(here)
            def _(first=first):
                for t in range(tiles):
                    lanes = slice(t * LANES, (t + 1) * LANES)
                    for ref, at in ((o_keep, first), (o_send, half + 1 - first)):
                        ref[0 : half + 1, lanes] = head4[t, at : at + half + 1, :]
                        ref[half + 1 :, lanes] = jnp.zeros((ref.shape[0] - half - 1, LANES), F32)

        o_small[...] = jnp.zeros_like(o_small)
        for c in range(0, nfft, LANES):
            o_small[0:1, c : c + LANES] = bias4[c : c + LANES, :].T[0:1, :]
        o_small[0:1, nfft : nfft + 2] = jnp.concatenate(
            [bias4[nfft : nfft + 1, 0:1], bias4[nfft + 1 : nfft + 2, 0:1]], 1
        )
        o_small[1:2, :width] = jnp.sum(acc_gls[...], axis=0, keepdims=True)
        o_small[2:3, :width] = jnp.sum(acc_gmb[...], axis=0, keepdims=True) * scale


def whole(shape):
    return pl.BlockSpec(shape, lambda *_: (0,) * len(shape))


def fixed(shape):
    return pl.BlockSpec(shape, lambda *_: (0,) * len(shape), pipeline_mode=pl.Buffered(1))


def row_halves(blks, rows, rows8, width, clip=None):
    per, last = rows // rows8, blks * rows // rows8 - 1
    places = [
        (rows, lambda j: j),
        (rows8, lambda j: jnp.maximum(j * per - 1, 0)),
        (rows8, lambda j: jnp.minimum(j * per + per, last)),
    ]
    if clip is None:
        return [pl.BlockSpec((1, n, width), lambda i, j, *_, f=f: (i, f(j), 0)) for n, f in places]
    return [pl.BlockSpec((1, n, width), lambda j, *_, f=f: (clip, f(j), 0)) for n, f in places]


def run_head(bands, offsets, x, edge, cot, cot_edge, weights, turns, consts):
    clips, frames, width = x.shape
    blks = frames // ROWS
    count = clips * frames
    hidden = weights[4].shape[1]
    nfft = turns.shape[1]
    block = lambda i, j, *_: (i * blks + j, 0)
    column = lambda i, j, *_: (0, i * blks + j)
    per_clip = lambda shape: pl.BlockSpec((1,) + shape, lambda i, j, *_: (i, 0, 0))
    in_specs = row_halves(blks, ROWS, edge.shape[1], width)
    in_specs += [per_clip(edge.shape[1:])]
    operands = list(weights) + [turns] + list(consts)
    in_specs += [fixed(cot.shape), per_clip(cot_edge.shape[1:])] + [fixed(v.shape) for v in operands]
    row_out = lambda n, dtype: (SDS((count, n), dtype), pl.BlockSpec((ROWS, n), block))
    col_out = (SDS((width, count), BF16), pl.BlockSpec((width, ROWS), column))
    outs = [
        row_out(width, F32),
        row_out(LANES, F32),
        col_out,
        col_out,
        row_out(hidden, BF16),
        row_out(hidden, BF16),
        row_out(hidden, F32),
        row_out(nfft, F32),
        row_out(width, F32),
        row_out(width, BF16),
        row_out(width, BF16),
        col_out,
        col_out,
        (SDS((HEAD_ROWS + hidden // 2, width), F32), whole((HEAD_ROWS, width))),
        (SDS((HEAD_ROWS + hidden // 2, width), F32), whole((HEAD_ROWS, width))),
        (SDS((8, hidden), F32), whole((8, hidden))),
    ]
    wave_tiles = nfft // 2 // LANES
    tiles = width // LANES
    scratch = [pltpu.VMEM((width, hidden), BF16)] * 2 + [pltpu.VMEM((hidden, width), BF16)] * 2
    scratch += [
        pltpu.VMEM((nfft, width), BF16),
        pltpu.VMEM((nfft, width), BF16),
        pltpu.VMEM((2, nfft), F32),
        pltpu.VMEM((8, width), F32),
        pltpu.VMEM((tiles, nfft + 8, LANES), F32),
        pltpu.VMEM((nfft + 8, LANES), F32),
        pltpu.VMEM((tiles, ROWS + 2 * edge.shape[1], LANES), F32),
        pltpu.VMEM((tiles, ROWS, LANES), F32),
        pltpu.VMEM((ROWS, LANES), F32),
        pltpu.VMEM((wave_tiles, PAIRS + 8, LANES), F32),
        pltpu.VMEM((tiles, ROWS, LANES), F32),
        pltpu.VMEM((ROWS, nfft), BF16),
        pltpu.VMEM((ROWS, nfft), BF16),
        pltpu.VMEM((width, nfft), F32),
        pltpu.VMEM((8, nfft), F32),
        pltpu.VMEM((8, width), F32),
        pltpu.VMEM((8, ROWS), F32),
        pltpu.VMEM((8, width), F32),
        pltpu.VMEM((8, width), F32),
    ]
    return pl.pallas_call(
        head_kernel,
        grid_spec=pltpu.PrefetchScalarGridSpec(
            num_scalar_prefetch=2,
            grid=(clips, blks),
            in_specs=in_specs,
            out_specs=[s for _, s in outs],
            scratch_shapes=scratch,
        ),
        out_shape=[s for s, _ in outs],
        compiler_params=pltpu.CompilerParams(vmem_limit_bytes=VMEM),
        cost_estimate=pl.CostEstimate(flops=80_000_000_000, bytes_accessed=90_000_000, transcendentals=0),
        name="head",
    )(bands, offsets, x, x, x, edge, cot, cot_edge, *operands)


def down_kernel(gbt_h, gbt_l, act_h, act_l, *refs):
    o_keep, o_send, acc, keep, send, sems = refs[-6:]
    step = pl.program_id(0)

    @pl.when(step == 0)
    def _():
        acc[...] = jnp.zeros_like(acc)

    acc[...] += dot3((gbt_h[...], gbt_l[...]), (act_h[...], act_l[...]))

    @pl.when(step == pl.num_programs(0) - 1)
    def _():
        core = lax.axis_index("clip") % 2
        rows = keep.shape[0]
        copies = []
        for i, (ref, out, half) in enumerate(((keep, o_keep, core), (send, o_send, 1 - core))):
            mine = pl.ds(pl.multiple_of(half * rows, rows), rows)
            ref[...] = acc[:, mine].T
            above = out.shape[0] - rows
            copies.append(pltpu.make_async_copy(ref, out.at[pl.ds(above, rows), :], sems.at[i]))
            copies[-1].start()
        for copy in copies:
            copy.wait()


def run_down(gbt, act, keep, send):
    width, count = gbt[0].shape
    hidden = act[0].shape[1]
    rows = 512
    any_spec = pl.BlockSpec(memory_space=pl.ANY)
    half = pltpu.VMEM((hidden // 2, width), F32)
    return pl.pallas_call(
        down_kernel,
        grid=(count // rows,),
        in_specs=[pl.BlockSpec((width, rows), lambda i: (0, i))] * 2
        + [pl.BlockSpec((rows, hidden), lambda i: (i, 0))] * 2
        + [any_spec] * 2,
        out_specs=[any_spec] * 2,
        out_shape=[SDS(keep.shape, F32), SDS(send.shape, F32)],
        input_output_aliases={4: 0, 5: 1},
        scratch_shapes=[pltpu.VMEM((width, hidden), F32), half, half, pltpu.SemaphoreType.DMA((2,))],
        compiler_params=pltpu.CompilerParams(vmem_limit_bytes=VMEM),
        cost_estimate=pl.CostEstimate(flops=10_000_000_000, bytes_accessed=20_000_000, transcendentals=0),
        name="down_grads",
    )(*gbt, *act, keep, send)


def up_kernel(gb_h, gb_l, slope, adt_h, adt_l, down_w, *refs):
    o_keep, o_send, o_gub, o_gu_h, o_gu_l, dw_h, dw_l, acc, acc_gub = refs[-9:]
    step = pl.program_id(0)
    hidden = slope.shape[1]

    @pl.when(step == 0)
    def _():
        dw_h[...], dw_l[...] = split(down_w[...])
        acc[...] = jnp.zeros_like(acc)
        acc_gub[...] = jnp.zeros_like(acc_gub)

    cols = 512
    for j in range(hidden // cols):
        part = slice(j * cols, (j + 1) * cols)
        gu = dot3((gb_h[...], gb_l[...]), (dw_h[part, :], dw_l[part, :]), NT) * slope[:, part]
        acc_gub[:, part] += fold8(gu)
        gs = split(gu)
        o_gu_h[:, part], o_gu_l[:, part] = gs
        acc[:, part] += dot3((adt_h[...], adt_l[...]), gs)

    @pl.when(step == pl.num_programs(0) - 1)
    def _():
        o_gub[...] = jnp.sum(acc_gub[...], axis=0, keepdims=True)
        core = lax.axis_index("clip") % 2
        rows = o_keep.shape[0]
        for ref, half in ((o_keep, core), (o_send, 1 - core)):
            ref[...] = acc[:, pl.ds(pl.multiple_of(half * rows, rows), rows)].T


def after(values):
    return [pl.BlockSpec(memory_space=pl.ANY)] * len(values), list(values)


def run_up(gb, slope, adt, down_w, size, part, so_far, waits=()):
    count, width = gb[0].shape
    hidden = slope.shape[1]
    rows = 512
    row = lambda i: (i, 0)
    in_specs = [pl.BlockSpec((rows, width), row)] * 2 + [pl.BlockSpec((rows, size), lambda i: (i, part))]
    in_specs += [pl.BlockSpec((width, rows), lambda i: (0, i))] * 2
    in_specs += [pl.BlockSpec((size, width), lambda i: (part, 0), pipeline_mode=pl.Buffered(1))]
    so_far = list(so_far)
    wait_specs, waits = after(waits)
    return pl.pallas_call(
        up_kernel,
        grid=(count // rows,),
        in_specs=in_specs + [pl.BlockSpec(memory_space=pl.ANY)] * len(so_far) + wait_specs,
        out_specs=[pl.BlockSpec((size // 2, width), lambda i: (part, 0))] * 2
        + [whole((1, size)), pl.BlockSpec((rows, size), row), pl.BlockSpec((rows, size), row)],
        out_shape=[
            SDS((hidden // 2, width), F32),
            SDS((hidden // 2, width), F32),
            SDS((1, size), F32),
            SDS((count, size), BF16),
            SDS((count, size), BF16),
        ],
        input_output_aliases={6 + i: i for i in range(len(so_far))},
        scratch_shapes=[pltpu.VMEM((size, width), BF16)] * 2
        + [pltpu.VMEM((width, size), F32), pltpu.VMEM((8, size), F32)],
        compiler_params=pltpu.CompilerParams(vmem_limit_bytes=VMEM),
        cost_estimate=pl.CostEstimate(flops=10_000_000_000, bytes_accessed=20_000_000, transcendentals=0),
        name="up_grads",
    )(*gb, slope, *adt, down_w, *so_far, *waits)


def norm_kernel(sizes, clip, bands, *refs):
    gu = refs[: 2 * len(sizes)]
    up_w, norm, istd, scale_t, edge_in = refs[2 * len(sizes) : 2 * len(sizes) + 5]
    o_gh, o_edge, o_scale, o_shift, up_h, up_l, nat4, acc_scale, acc_shift = refs[-9:]
    blk, blks = pl.program_id(0), pl.num_programs(0)
    band = bands[clip]
    width = norm.shape[1]
    tiles = width // LANES

    @pl.when(blk == 0)
    def _():
        up_h[...], up_l[...] = split(up_w[...])
        for ref in (o_scale, o_shift, acc_scale, acc_shift):
            ref[...] = jnp.zeros_like(ref)
        o_edge[...] = edge_in[...]

    ga, at = None, 0
    for j, hidden in enumerate(sizes):
        cols = slice(at, at + hidden)
        term = dot3((gu[2 * j][...], gu[2 * j + 1][...]), (up_h[:, cols], up_l[:, cols]), NT)
        ga = term if ga is None else ga + term
        at += hidden
    normed = norm[...]
    acc_scale[...] += fold8(ga * normed)
    acc_shift[...] += fold8(ga)
    gn = ga * scale_t[pl.ds(band, 1), :]
    mean = jnp.sum(gn, axis=1, keepdims=True) * (1.0 / width)
    along = jnp.sum(gn * normed, axis=1, keepdims=True) * (1.0 / width)
    gh = istd[:, 0:1] * (gn - mean - normed * along)
    for par in range(2):
        for t in range(tiles):
            nat4[t, pl.ds(par, PAIRS, stride=2), :] = gh[par * PAIRS : (par + 1) * PAIRS, t * LANES : (t + 1) * LANES]
    for t in range(tiles):
        o_gh[:, t * LANES : (t + 1) * LANES] = nat4[t]
    tm = lax.axis_index("tm")
    for here, first in (((tm == 0) & (blk == blks - 1), ROWS - 8), ((tm == 1) & (blk == 0), 0)):

        @pl.when(here)
        def _(first=first):
            for t in range(tiles):
                o_edge[clip, :, t * LANES : (t + 1) * LANES] = nat4[t, first : first + 8, :]

    @pl.when(blk == blks - 1)
    def _():
        o_scale[pl.ds(band, 1), :] = jnp.sum(acc_scale[...], axis=0, keepdims=True)
        o_shift[pl.ds(band, 1), :] = jnp.sum(acc_shift[...], axis=0, keepdims=True)


def run_norm(bands, gus, up_w, norm, istd, scale_t, edge, clip, waits=()):
    clips = edge.shape[0]
    count, width = norm.shape
    blks = count // clips // ROWS
    block = lambda j, *_: (clip * blks + j, 0)
    flat = [v for pair in gus for v in pair]
    in_specs = [pl.BlockSpec((ROWS, v.shape[1]), block) for v in flat]
    in_specs += [fixed(up_w.shape), pl.BlockSpec((ROWS, width), block)]
    in_specs += [pl.BlockSpec((ROWS, LANES), block), fixed(scale_t.shape), fixed(edge.shape)]
    wait_specs, waits = after(waits)
    return pl.pallas_call(
        functools.partial(norm_kernel, [pair[0].shape[1] for pair in gus], clip),
        grid_spec=pltpu.PrefetchScalarGridSpec(
            num_scalar_prefetch=1,
            grid=(blks,),
            in_specs=in_specs + wait_specs,
            out_specs=[pl.BlockSpec((ROWS, width), lambda j, *_: (j, 0)), whole(edge.shape)] + [whole(scale_t.shape)] * 2,
            scratch_shapes=[pltpu.VMEM(up_w.shape, BF16)] * 2
            + [pltpu.VMEM((width // LANES, ROWS, LANES), F32)]
            + [pltpu.VMEM((8, width), F32)] * 2,
        ),
        out_shape=[SDS((count // clips, width), F32), SDS(edge.shape, F32)] + [SDS(scale_t.shape, F32)] * 2,
        compiler_params=pltpu.CompilerParams(vmem_limit_bytes=VMEM),
        cost_estimate=pl.CostEstimate(flops=5_000_000_000, bytes_accessed=12_000_000, transcendentals=0),
        name="norm_grads",
    )(bands, *flat, up_w, norm, istd, scale_t, edge, *waits)


def conv_kernel(
    clip, offsets, x_ref, x_up, x_down, edge_ref, gh_ref, gh_up, gh_down, gh_edge, gm_ref, conv_w, acc_in, *refs
):
    o_gi, o_acc, pad4, gh4 = refs[-4:]
    blk, blks = pl.program_id(0), pl.num_programs(0)
    rows, width = x_ref.shape[1], x_ref.shape[2]
    tiles = width // LANES
    tm = lax.axis_index("tm")
    local = offsets[clip] - tm * blks * rows
    rows8 = edge_ref.shape[1]
    base = blk * rows

    @pl.when(blk == 0)
    def _():
        o_acc[...] = acc_in[...]

    def masked(value, first):
        row = first + lax.broadcasted_iota(jnp.int32, value.shape, 0)
        return jnp.where(row >= local, value, 0.0)

    def above(edge, up):
        return jnp.where(blk == 0, jnp.where(tm > 0, edge[0], 0.0), up[0])

    def below(edge, down):
        return jnp.where(blk == blks - 1, jnp.where(tm > 0, 0.0, edge[0]), down[0])

    before, after = masked(above(edge_ref, x_up), base - rows8), masked(below(edge_ref, x_down), base + rows)
    g_before, g_after = above(gh_edge, gh_up), below(gh_edge, gh_down)
    middle = masked(x_ref[0], base)
    for t in range(tiles):
        lanes = slice(t * LANES, (t + 1) * LANES)
        pad4[t, 0:rows8, :] = before[:, lanes]
        pad4[t, rows8 : rows8 + rows, :] = middle[:, lanes]
        pad4[t, rows8 + rows :, :] = after[:, lanes]
        gh4[t, 0:rows8, :] = g_before[:, lanes]
        gh4[t, rows8 : rows8 + rows, :] = gh_ref[0, :, lanes]
        gh4[t, rows8 + rows :, :] = g_after[:, lanes]
    chunk = 64
    for r in range(0, rows, chunk):
        shown = base + r + lax.broadcasted_iota(jnp.int32, (chunk, LANES), 0) >= local
        for t in range(tiles):
            lanes = slice(t * LANES, (t + 1) * LANES)
            gh = gh4[t, rows8 + r : rows8 + r + chunk, :]
            o_acc[8 * KERNEL :, lanes] += fold8(gh)
            total = gm_ref[0, r : r + chunk, lanes]
            for k in range(KERNEL):
                first = r + rows8 + KERNEL // 2 - k
                total = total + conv_w[k : k + 1, lanes] * gh4[t, first : first + chunk, :]
                first = r + rows8 - KERNEL // 2 + k
                o_acc[8 * k : 8 * k + 8, lanes] += fold8(gh * pad4[t, first : first + chunk, :])
            o_gi[0, r : r + chunk, lanes] = jnp.where(shown, total, 0.0)


def run_conv(offsets, x, edge, gh, gh_edge, gm, conv_w, clip, so_far, waits=()):
    clips, frames, width = x.shape
    blks = frames // ROWS
    rows8 = edge.shape[1]
    mine = pl.BlockSpec((1, rows8, width), lambda j, *_: (clip, 0, 0))
    padded = pltpu.VMEM((width // LANES, ROWS + 2 * rows8, LANES), F32)
    blocks = row_halves(blks, ROWS, rows8, width, clip)
    in_specs = blocks + [mine] + row_halves(blks, ROWS, rows8, width, 0) + [mine] + blocks[:1]
    grads, acc = so_far
    in_specs += [fixed(conv_w.shape), fixed(acc.shape)]
    operands = [x, x, x, edge, gh, gh, gh, gh_edge, gm, conv_w, acc]
    aliases = {}
    wait_specs, waits = after(waits)
    if grads is not None:
        aliases = {1 + len(operands): 0}
        operands.append(grads)
        in_specs.append(pl.BlockSpec(memory_space=pl.ANY))
    return pl.pallas_call(
        functools.partial(conv_kernel, clip),
        grid_spec=pltpu.PrefetchScalarGridSpec(
            num_scalar_prefetch=1,
            grid=(blks,),
            in_specs=in_specs + wait_specs,
            out_specs=[blocks[0], whole(acc.shape)],
            scratch_shapes=[padded, padded],
        ),
        out_shape=[SDS(x.shape, F32), SDS(acc.shape, F32)],
        input_output_aliases=aliases,
        compiler_params=pltpu.CompilerParams(vmem_limit_bytes=VMEM),
        cost_estimate=pl.CostEstimate(flops=5_000_000_000, bytes_accessed=17_000_000, transcendentals=0),
        name="conv_grads",
    )(offsets, *operands, *waits)


def pack_kernel(acc, small, scales0, scales1, shifts0, shifts1, *refs):
    gubs, o_pack = refs[:-1], refs[-1]
    width = acc.shape[1]
    for k in range(KERNEL + 1):
        o_pack[k : k + 1, :] = jnp.sum(acc[8 * k : 8 * k + 8, :], axis=0, keepdims=True)
    o_pack[8:12, :] = scales0[...] + scales1[...]
    o_pack[12:16, :] = shifts0[...] + shifts1[...]
    o_pack[16:18, :] = small[1:3, :width]
    for i in range(3):
        o_pack[18 + i : 19 + i, :] = small[0:1, i * width : (i + 1) * width]
        gub = jnp.concatenate([v[...] for v in gubs], 1)
        o_pack[21 + i : 22 + i, :] = gub[:, i * width : (i + 1) * width]
    o_pack[24:, :] = jnp.zeros((o_pack.shape[0] - 24, width), F32)


def wave_kernel(
    first_blk, frames, scaled, offsets, spec, carry, t1h, t1l, t2h, t2l, t0h, t0l, windows, inverse, *refs
):
    o_wave, o_tail, accs = refs[-3:]
    blk, clip = pl.program_id(0), pl.program_id(1)
    blks, clips = pl.num_programs(0), pl.num_programs(1)
    tiles = accs.shape[1]
    first = (first_blk + blk) * PAIRS
    local = offsets[clip] - lax.axis_index("tm") * frames
    acc5 = accs.at[clip]

    @pl.when(blk == 0)
    def _():
        for t in range(tiles):
            acc5[t, 0:8, :] = carry[0, :, t * LANES : (t + 1) * LANES]

    @pl.when(blk > 0)
    def _():
        for t in range(tiles):
            acc5[t, 0:8, :] = acc5[t, PAIRS : PAIRS + 8, :]

    for t in range(tiles):
        acc5[t, 8:, :] = jnp.zeros((PAIRS, LANES), F32)

    n1, n2 = t1h.shape[0], t2h.shape[0]
    ab = dot3(split(spec[:, :n1]), (t1h[...], t1l[...]))
    cd = dot3(split(spec[:, n1 : n1 + n2]), (t2h[...], t2l[...]))
    p0 = dot3(split(spec[:, n1 + n2 :]), (t0h[...], t0l[...]))
    c1, c2, s1, s2 = fifths()
    sides = []
    for par in range(2):
        rows = slice(par * PAIRS, (par + 1) * PAIRS)
        w = p0.shape[1]
        a, b, c, d, p = ab[rows, :w], ab[rows, w:], cd[rows, :w], cd[rows, w:], p0[rows]
        e1, o1 = p + c1 * a + c2 * c, s1 * b + s2 * d
        e2, o2 = p + c2 * a + c1 * c, s2 * b - s1 * d
        v = [p + a + c, e1 - o1, e2 - o2, e2 + o2, e1 + o1]
        seg = []
        for t in range(2 * tiles):
            part = v[t // 2][:, (t % 2) * LANES : (t % 2 + 1) * LANES]
            seg.append(part * windows[par : par + 1, t * LANES : (t + 1) * LANES])
        sides.append(seg)
    even, odd = sides
    mid = tiles // 2
    right = lax.broadcasted_iota(jnp.int32, (PAIRS, LANES), 1) >= LANES // 2
    for t in range(tiles):
        here = even[t]
        if t > mid:
            here = here + odd[t]
        if t == mid:
            here = here + jnp.where(right, odd[t], 0.0)
        acc5[t, 0:PAIRS, :] += here
        acc5[t, 1 : PAIRS + 1, :] += even[tiles + t] + odd[tiles + t]
        if t < mid:
            acc5[t, 2 : PAIRS + 2, :] += odd[t]
        if t == mid:
            acc5[t, 2 : PAIRS + 2, :] += jnp.where(right, 0.0, odd[t])
        value = acc5[t, 0:PAIRS, :] * inverse_envelope(first, local, inverse, t, PAIRS)
        o_wave[pl.ds(clips * t + clip, PAIRS, stride=clips * tiles), :] = value

    @pl.when(blk == blks - 1)
    def _():
        for t in range(tiles):
            value = acc5[t, PAIRS : PAIRS + 8, :]
            if scaled:
                value = value * inverse_envelope(first + PAIRS, local, inverse, t, 8)
            o_tail[0, :, t * LANES : (t + 1) * LANES] = value


def run_wave(offsets, spec, consts, clips, first_blk, blks, carry, wave=None, waits=()):
    count, nfft = spec.shape
    all_blks = count // clips // ROWS
    tiles = nfft // 2 // LANES
    rows = clips * PAIRS * tiles
    in_specs = [pl.BlockSpec((ROWS, nfft), lambda j, i, *_: (i * all_blks + first_blk + j, 0))]
    in_specs += [pl.BlockSpec((1, 8, nfft // 2), lambda j, i, *_: (i, 0, 0))]
    in_specs += [fixed(v.shape) for v in consts]
    operands = [spec, carry, *consts]
    aliases = {}
    wait_specs, waits = after(waits)
    if wave is not None:
        aliases = {1 + len(operands): 0}
        operands.append(wave)
        in_specs.append(pl.BlockSpec(memory_space=pl.ANY))
    return pl.pallas_call(
        functools.partial(wave_kernel, first_blk, count // clips, first_blk == 0),
        grid_spec=pltpu.PrefetchScalarGridSpec(
            num_scalar_prefetch=1,
            grid=(blks, clips),
            in_specs=in_specs + wait_specs,
            out_specs=[
                pl.BlockSpec((rows, LANES), lambda j, i, *_: (first_blk + j, 0)),
                pl.BlockSpec((1, 8, nfft // 2), lambda j, i, *_: (i, 0, 0)),
            ],
            scratch_shapes=[pltpu.VMEM((clips, tiles, PAIRS + 8, LANES), F32)],
        ),
        out_shape=[SDS((rows * all_blks, LANES), F32), SDS((clips, 8, nfft // 2), F32)],
        input_output_aliases=aliases,
        compiler_params=pltpu.CompilerParams(vmem_limit_bytes=VMEM),
        cost_estimate=pl.CostEstimate(flops=5_000_000_000, bytes_accessed=8_000_000, transcendentals=0),
        name="wave",
    )(offsets, *operands, *waits)


def levels():
    clip = [("clip", 1 << i) for i in range((lax.axis_size("clip") - 1).bit_length())]
    tm = [("tm", 1 << i) for i in range((lax.axis_size("tm") - 1).bit_length())]
    return clip[:1] + clip[1:2] + tm + clip[2:]


def exchange(value, level):
    if level == "next":
        return lax.ppermute(value, "tm", [(i, i + 1) for i in range(lax.axis_size("tm") - 1)])
    across = {"clip": 0, "tm": 0}
    for axis, distance in level if isinstance(level, list) else [level]:
        across[axis] += distance
    if not across["tm"]:
        return lax.ppermute(value, "clip", [(i, i ^ across["clip"]) for i in range(lax.axis_size("clip"))])
    if not across["clip"]:
        return lax.ppermute(value, "tm", [(i, i ^ across["tm"]) for i in range(lax.axis_size("tm"))])
    n, m = lax.axis_size("clip"), lax.axis_size("tm")
    pairs = [(i * m + j, (i ^ across["clip"]) * m + (j ^ across["tm"])) for i in range(n) for j in range(m)]
    return lax.ppermute(value, ("clip", "tm"), pairs)


def side(level):
    axis, distance = level
    return lax.axis_index(axis) // distance % 2


class Sums:
    def __init__(self):
        self.running = []

    def add(self, steps, holds=()):
        entry = {"steps": steps, "holds": holds, "count": 0, "sent": None, "came": None, "left": 0, "sum": None}
        self.step(entry, None)
        self.running.append(entry)
        return entry

    def step(self, entry, values):
        try:
            entry["sent"] = entry["steps"].send(values)
            while entry["sent"][0][1] == levels()[0]:
                entry["sent"] = entry["steps"].send([exchange(*pair) for pair in entry["sent"]])
        except StopIteration as stop:
            entry["sent"], entry["sum"] = None, stop.value

    def waits(self):
        sent = []
        for entry in self.running:
            if entry["came"] is None and entry["sent"] is not None:
                entry["came"] = [exchange(*pair) for pair in entry["sent"]]
                entry["left"] = dict(entry["holds"]).get(entry["count"], 1)
                entry["count"] += 1
                sent += [pair[0] for pair in entry["sent"]]
        return sent

    def advance(self, results):
        done = []
        for entry in self.running:
            if entry["came"] is not None:
                entry["left"] -= 1
                if entry["left"] <= 0:
                    done.append(entry)
        if done:
            came, results = lax.optimization_barrier(([entry["came"] for entry in done], results))
            for entry, values in zip(done, came):
                entry["came"] = None
                self.step(entry, values)
        return results

    def finish(self, entry):
        while entry["sum"] is None:
            self.waits()
            self.advance(())
        return entry["sum"]


def halves_steps(keep, send, narrow):
    core, one, two, *last = levels()
    orders = ((one, two), (two, one))
    (came,) = yield [(send, core)]
    total = keep + came
    cols = total.shape[1] // 2
    parts = [total[:, :cols], total[:, cols:]]
    for i in range(2):
        sent, kept = [], []
        for part, order in zip(parts, orders):
            rows, s = part.shape[0] // 2, side(order[i])
            sent.append((lax.dynamic_slice_in_dim(part, (1 - s) * rows, rows), order[i]))
            kept.append(lax.dynamic_slice_in_dim(part, s * rows, rows))
        came = yield sent
        parts = [a + b for a, b in zip(kept, came)]
    rows = parts[0].shape[0]
    value = jnp.concatenate(parts)
    halved = last if narrow and rows % (4 << len(last)) == 0 else []
    for level in halved:
        n, s = value.shape[0] // 2, side(level)
        (came,) = yield [(lax.dynamic_slice_in_dim(value, (1 - s) * n, n), level)]
        value = lax.dynamic_slice_in_dim(value, s * n, n) + came
    for level in last[len(halved) :]:
        (came,) = yield [(value, level)]
        value = value + came
    for level in halved[::-1]:
        s = side(level)
        (came,) = yield [(value, level)]
        value = jnp.concatenate([jnp.where(s == 0, value, came), jnp.where(s == 0, came, value)])
    parts = [value[:rows], value[rows:]]
    for i in (1, 0):
        came = yield [(part, order[i]) for part, order in zip(parts, orders)]
        parts = [jnp.concatenate(pair) for pair in zip(parts, came)]
    others = yield [(part, core) for part in parts]
    return parts, others, orders


def whole_steps(value):
    core, *rest = levels()
    (came,) = yield [(value, core)]
    value = value + came
    for pair in [rest[:1]] + [rest[i : i + 2] for i in range(1, len(rest), 2)]:
        came = yield [(value, [level]) for level in pair] + ([(value, pair)] if len(pair) == 2 else [])
        for other in came:
            value = value + other
    return value


def one_step(value, level):
    (came,) = yield [(value, level)]
    return came


def natural_blocks(orders, refs, copy):
    core = side(levels()[0])
    cols = refs[0].shape[1]
    rows = refs[0].shape[0] // 4
    for half in range(2):
        for here, pair in ((core == half, refs[:2]), (core != half, refs[2:])):

            @pl.when(here)
            def _(pair=pair, half=half):
                for i, (ref, order) in enumerate(zip(pair, orders)):
                    a, b = (side(level) for level in order)
                    for block in range(4):
                        first = (2 * jnp.bitwise_xor(block // 2, a) + jnp.bitwise_xor(block % 2, b)) * rows
                        value = ref[pl.ds(pl.multiple_of(first, 8), rows), :]
                        copy(half, slice(i * cols, (i + 1) * cols), block * rows, value)


def to_runs(runs):
    def copy(half, cols, first, value):
        for start, out, place, rows in runs:
            low, high = max(first, start), min(first + value.shape[0], start + rows)
            if low < high:
                at = place(half) + low - start
                out[at : at + high - low, cols] = value[low - first : high - first]

    return copy


def first_order_kernel(orders, *refs):
    o_head, o_down = refs[-2:]
    copy = to_runs(
        (
            (0, o_head, lambda half: half * (o_head.shape[0] // 2), o_head.shape[0] // 2),
            (HEAD_ROWS, o_down, lambda half: half * (o_down.shape[0] // 2), o_down.shape[0] // 2),
        )
    )
    natural_blocks(orders, refs[:4], copy)


def up_order_kernel(orders, *refs):
    o_up, up_t = refs[-2:]

    runs, at = [], 0
    for size, part in UP_PARTS:
        runs.append((at, up_t, lambda half, size=size, part=part: size * part + half * (size // 2), size // 2))
        at += size // 2
    copy = to_runs(runs)
    natural_blocks(orders, refs[:4], copy)
    for c in range(0, up_t.shape[0], LANES):
        o_up[:, c : c + LANES] = up_t[c : c + LANES, :].T


def run_order(kernel, total, out_shape, scratch=(), waits=()):
    parts, others, orders = total
    wait_specs, waits = after(waits)
    return pl.pallas_call(
        functools.partial(kernel, orders),
        in_specs=[pl.BlockSpec(memory_space=pltpu.VMEM)] * 4 + wait_specs,
        out_shape=out_shape,
        scratch_shapes=list(scratch),
        compiler_params=pltpu.CompilerParams(vmem_limit_bytes=VMEM),
        name="in_order",
    )(*parts, *others, *waits)


def unpack_kernel(pack, gcw, gcb, gscale, gshift, gls, gdb, ghb, gub):
    width = pack.shape[1]
    gcw[...] = pack[0:KERNEL, :]
    gcb[...] = pack[KERNEL : KERNEL + 1, :].reshape(width)
    gscale[...] = pack[8:12, :]
    gshift[...] = pack[12:16, :]
    gls[...] = pack[16:17, :].reshape(width)
    gdb[...] = pack[17:18, :].reshape(width)
    rows = [pack[18 + i : 19 + i, :] for i in range(6)]
    ghb[...] = jnp.concatenate(rows[:3], 1)[:, : ghb.shape[0]].reshape(ghb.shape[0])
    gub[...] = jnp.concatenate(rows[3:], 1).reshape(gub.shape[0])


def edges(value, index):
    n = value.shape[1]
    return jnp.where(index == 0, value[:, n - 8 :], value[:, :8])


def to_chunks(wave):
    clips, samples = wave.shape
    return wave.reshape(clips, samples // LANES, LANES).transpose(1, 0, 2).reshape(-1, LANES)


def from_chunks(chunks, clips):
    rows = chunks.shape[0] // clips
    return chunks.reshape(rows, clips, LANES).transpose(1, 0, 2).reshape(clips, rows * LANES)


def body(
    inputs,
    band_ids,
    offsets,
    conv_weight,
    conv_bias,
    scale_table,
    shift_table,
    up_weight,
    up_bias,
    down_weight,
    down_bias,
    layer_scale,
    head_weight,
    head_bias,
    wave_cotangent,
):
    clips, frames, width = inputs.shape
    assert lax.axis_size("tm") == 2
    nfft = head_weight.shape[1] - 2
    half = nfft // 2
    hidden = up_weight.shape[1]
    tm = lax.axis_index("tm")
    core = lax.axis_index("clip") % 2
    swap = lambda v: lax.ppermute(v, "tm", [(0, 1), (1, 0)])
    transforms, windows, inverse, turns = tables(nfft)
    dft = [jnp.asarray(v) for pair in transforms for v in pair]
    consts = dft + [jnp.asarray(windows), jnp.asarray(inverse)]

    edge = swap(edges(inputs, tm))
    cot_edge = swap(jnp.pad(wave_cotangent[:, :nfft].reshape(clips, 2, half), ((0, 0), (0, 6), (0, 0))))
    weights = (
        conv_weight,
        conv_bias,
        scale_table,
        shift_table,
        up_weight,
        up_bias,
        down_weight,
        down_bias,
        layer_scale,
        head_weight.T,
        head_bias,
    )
    (
        norm, istd, adt_h, adt_l, act_h, act_l, slope, spec, gm, gb_h, gb_l, gbt_h, gbt_l, hg_keep, hg_send, small,
    ) = run_head(
        band_ids, offsets, inputs, edge, to_chunks(wave_cotangent), cot_edge, weights, jnp.asarray(turns), consts
    )

    keep, send = run_down((gbt_h, gbt_l), (act_h, act_l), hg_keep, hg_send)
    sums = Sums()
    first_total = sums.add(halves_steps(keep, send, True))
    blks = frames // ROWS
    gus, gubs, halves = [], [], ()
    for size, part in UP_PARTS:
        results = run_up((gb_h, gb_l), slope, (adt_h, adt_l), down_weight, size, part, halves, waits=sums.waits())
        *halves, gub, gu_h, gu_l = sums.advance(results)
        gus.append((gu_h, gu_l))
        gubs.append(gub)
    up_total = sums.add(halves_steps(*halves, False), {3: 2})
    normed, gh_edge = [], jnp.zeros(edge.shape, F32)
    for clip in range(clips):
        results = run_norm(band_ids, gus, up_weight, norm, istd, scale_table, gh_edge, clip, waits=sums.waits())
        gh_edge = results[1]
        normed.append(sums.advance(results))
    gh = [v[0][None] for v in normed]
    gh_edge = sums.add(one_step(normed[-1][1], ("tm", 1)))
    late = blks // 2
    carry = jnp.zeros((clips, 8, half), F32)
    wave, tail = run_wave(offsets, spec, consts, clips, late, blks - late, carry, waits=sums.waits())
    wave, tail = sums.advance((wave, tail))
    arrived = sums.add(one_step(tail, "next"))
    gh_edge = sums.finish(gh_edge)
    so_far = (None, jnp.zeros((8 * (KERNEL + 1), width), F32))
    gm = gm.reshape(clips, frames, width)
    for clip in range(clips):
        so_far = run_conv(
            offsets, inputs, edge, gh[clip], gh_edge, gm, conv_weight, clip, so_far, waits=sums.waits()
        )
        so_far = sums.advance(so_far)
    grad_inputs, acc = so_far
    pack = pl.pallas_call(pack_kernel, out_shape=SDS((32, width), F32), name="pack")(
        acc, small, *[v[2] for v in normed], *[v[3] for v in normed], *gubs
    )
    small_total = sums.add(whole_steps(pack))

    arrived = sums.finish(arrived)
    wave, over = run_wave(offsets, spec, consts, clips, 0, late, arrived, wave, waits=sums.waits())
    wave, over = sums.advance((wave, over))
    over = to_chunks(over[:, :2].reshape(clips, nfft))
    at = late * clips * PAIRS * half // LANES
    mended = lax.dynamic_slice_in_dim(wave, at, over.shape[0]) + over
    waveform = from_chunks(lax.dynamic_update_slice_in_dim(wave, mended, at, 0), clips)

    first_total = sums.finish(first_total)
    head_grad, down_grad = sums.advance(
        run_order(
            first_order_kernel,
            first_total,
            [SDS((nfft + 2, width), F32), SDS((hidden, width), F32)],
            waits=sums.waits(),
        )
    )
    up_total = sums.finish(up_total)
    (up_grad,) = sums.advance(
        run_order(
            up_order_kernel,
            up_total,
            [SDS((width, hidden), F32)],
            [pltpu.VMEM((hidden, width), F32)],
            waits=sums.waits(),
        )
    )
    pack = sums.finish(small_total)
    small_shapes = [(KERNEL, width), (width,), scale_table.shape, scale_table.shape]
    small_shapes += [(width,), (width,), (nfft + 2,), (hidden,)]
    gcw, gcb, gscale, gshift, gls, gdb, ghb, gub = pl.pallas_call(
        unpack_kernel, out_shape=[SDS(shape, F32) for shape in small_shapes], name="unpack"
    )(pack)
    return (
        waveform,
        grad_inputs,
        gcw,
        gcb,
        gscale,
        gshift,
        up_grad,
        gub,
        down_grad,
        gdb,
        gls,
        head_grad.T,
        ghb,
    )


def solution(mesh):
    in_specs = (P("clip", "tm", None), P("clip"), P("clip")) + (P(),) * 11 + (P("clip", "tm"),)
    out_specs = (P("clip", "tm"), P("clip", "tm", None)) + (P(),) * 11
    return jax.shard_map(body, mesh=mesh, in_specs=in_specs, out_specs=out_specs, check_vma=False)
```

```python
import functools

import jax
import jax.numpy as jnp
import ml_dtypes
import numpy as np
from jax import lax
from jax.experimental import pallas as pl
from jax.experimental.pallas import tpu as pltpu
from jax.sharding import PartitionSpec as P

KERNEL = 7
CLASSES = ((1, 4), (2, 3), (0,))
F32 = jnp.float32
BF16 = jnp.bfloat16
LANES = 128
PAIRS = 128
ROWS = 2 * PAIRS
VMEM = 60 * 2**20
UP_PARTS = ((1024, 0), (512, 2))
HEAD_ROWS = 704
SDS = jax.ShapeDtypeStruct

SIN_POLY = (0.999999996, -0.166666580, 8.33305023e-03, -1.98090119e-04, 2.60507821e-06)
COS_POLY = (1.0, -0.499999994, 4.16666361e-02, -1.38883598e-03, 2.47600798e-05, -2.60500270e-07)

NN = (((1,), (0,)), ((), ()))
NT = (((1,), (1,)), ((), ()))


def split(x):
    high = x.astype(BF16)
    return high, (x - high.astype(F32)).astype(BF16)


def dot(a, b, dims=NN):
    return lax.dot_general(a, b, dims, preferred_element_type=F32)


def dot3(a, b, dims=NN):
    return dot(a[0], b[0], dims) + (dot(a[0], b[1], dims) + dot(a[1], b[0], dims))


def fold8(x):
    return jnp.sum(x.reshape(x.shape[0] // 8, 8, x.shape[1]), axis=0)


def np_split(x):
    high = x.astype(np.float32).astype(ml_dtypes.bfloat16)
    return high, (x - high.astype(np.float64)).astype(ml_dtypes.bfloat16)


@functools.lru_cache(None)
def tables(nfft):
    fifth, half, hop = nfft // 5, nfft // 2, nfft // 4
    bins = np.arange(1, half)
    first, second = (np.concatenate([bins[bins % 5 == r] for r in rs]) for rs in CLASSES[:2])
    zero = np.arange(0, half, 5)
    n0 = np.arange(fifth)

    def paired(ks, residue):
        sign = np.where(ks % 5 == residue, 1.0, -1.0)[:, None]
        turn = 2 * np.pi * ((sign * ks[:, None] * n0[None]) % nfft) / nfft
        weight = 2.0 / nfft
        real = np.concatenate([weight * np.cos(turn), weight * np.sin(turn)], 1)
        imag = np.concatenate([-sign * weight * np.sin(turn), sign * weight * np.cos(turn)], 1)
        return np.concatenate([real, imag], 0)

    turn = 2 * np.pi * ((zero[:, None] * n0[None]) % nfft) / nfft
    weight = np.where(zero == 0, 1.0, 2.0)[:, None] / nfft
    real, imag = weight * np.cos(turn), -weight * np.sin(turn)
    imag[0] = np.cos(np.pi * n0) / nfft
    transforms = [np_split(t) for t in (paired(first, 1), paired(second, 2), np.concatenate([real, imag], 0))]
    n = np.arange(nfft)
    window = 0.5 - 0.5 * np.cos(2 * np.pi * n / nfft)
    windows = np.stack([window, np.roll(window, hop)]).astype(np.float32)
    squares = np.cumsum((window**2).reshape(4, hop), axis=0)
    inverse = np.tile(1.0 / np.maximum(squares, 1.0), (1, 2)).astype(np.float32)
    turns = np.zeros(nfft)
    place = 0
    for ks in (first, second, zero):
        turns[place + len(ks) : place + 2 * len(ks)] = -(np.pi / 2) * (ks % 4)
        place += 2 * len(ks)
    return transforms, windows, inverse, turns.astype(np.float32)[None]


def class_places(nfft):
    length, places, at = nfft // 10, [], 0
    for residues in CLASSES:
        for offset in (0, nfft // 2 + 1):
            for r in residues:
                places.append((at, offset + r))
                at += length
    return places


def sin_cos(x):
    turns = jnp.round(x * np.float32(0.5 / np.pi))
    h = x * 0.5 - turns * np.float32(3.140625)
    h = h - turns * np.float32(9.67502593994140625e-4)
    h = h - turns * np.float32(1.509957990978376432e-7)
    z = h * h
    s = np.float32(SIN_POLY[-1])
    for c in SIN_POLY[-2::-1]:
        s = s * z + np.float32(c)
    s = s * h
    cosine = np.float32(COS_POLY[-1])
    for c in COS_POLY[-2::-1]:
        cosine = cosine * z + np.float32(c)
    twice = s + s
    return twice * cosine, 1.0 - twice * s


def fifths():
    a = 2 * np.pi / 5
    return [np.float32(v) for v in (np.cos(a), np.cos(2 * a), np.sin(a), np.sin(2 * a))]


def inverse_envelope(first_pair, offset, table_ref, tile, rows):
    lane = tile * LANES + lax.broadcasted_iota(jnp.int32, (rows, LANES), 1)
    row = lax.broadcasted_iota(jnp.int32, (rows, LANES), 0)
    half = table_ref.shape[1] // 2
    since = 2 * (first_pair + row) + (lane >= half).astype(jnp.int32) - offset
    value = jnp.where(since < 0, 1.0, 1.0)
    for i in range(4):
        value = jnp.where(since >= i, table_ref[i : i + 1, tile * LANES : (tile + 1) * LANES], value)
    return value


def head_kernel(
    bands,
    offsets,
    x_ref,
    x_up,
    x_down,
    edge_ref,
    cot_ref,
    cot_down,
    cot_edge,
    conv_w,
    conv_b,
    scale_t,
    shift_t,
    up_w,
    up_b,
    down_w,
    down_b,
    layer_scale,
    head_wt,
    head_b,
    turns,
    t1h,
    t1l,
    t2h,
    t2l,
    t0h,
    t0l,
    windows,
    inverse,
    o_norm,
    o_istd,
    o_adt_h,
    o_adt_l,
    o_act_h,
    o_act_l,
    o_slope,
    o_spec,
    o_gm,
    o_gb_h,
    o_gb_l,
    o_gbt_h,
    o_gbt_l,
    o_keep,
    o_send,
    o_small,
    up_h,
    up_l,
    down_h,
    down_l,
    head_h,
    head_l,
    head_bias,
    ext_w,
    head4,
    bias4,
    pad4,
    nrm4,
    istd1,
    gs5,
    gm4,
    gl_h,
    gl_l,
    acc_ghw,
    acc_ghb,
    acc_ghwe,
    acc_ghbe,
    acc_gls,
    acc_gmb,
):
    clip, blk = pl.program_id(0), pl.program_id(1)
    clips, blks = pl.num_programs(0), pl.num_programs(1)
    width = x_ref.shape[2]
    frames = blks * ROWS
    tiles = width // LANES
    nfft = turns.shape[1]
    half = nfft // 2
    tm = lax.axis_index("tm")
    band = bands[clip]
    local = offsets[clip] - tm * frames
    rows8 = edge_ref.shape[1]
    places = class_places(nfft)

    @pl.when((clip == 0) & (blk == 0))
    def _():
        up_h[...], up_l[...] = split(up_w[...])
        down_h[...], down_l[...] = split(down_w[...])
        for t in range(tiles):
            head4[t, 0 : nfft + 2, :] = head_wt[:, t * LANES : (t + 1) * LANES]
        bias = head_b[...].reshape(1, nfft + 2)
        for c in range(0, nfft, LANES):
            bias4[c : c + LANES, :] = jnp.broadcast_to(bias[:, c : c + LANES], (LANES, LANES)).T
        for c in (nfft, nfft + 1):
            bias4[c : c + 1, :] = jnp.broadcast_to(bias[:, c : c + 1], (1, LANES))
        for at, first in places:
            rows = jnp.concatenate([head4[t, pl.ds(first, LANES, stride=5), :] for t in range(tiles)], 1)
            head_h[at : at + LANES, :], head_l[at : at + LANES, :] = split(rows)
            moved = bias4[pl.ds(first, LANES, stride=5), :].T[0:1, :]
            head_bias[0:1, at : at + LANES] = moved
            head_bias[1:2, at : at + LANES] = moved + turns[:, at : at + LANES]
        ext_w[0:1, :] = head_wt[half : half + 1, :]
        ext_w[1:2, :] = head_wt[nfft + 1 : nfft + 2, :]
        ext_w[2:8, :] = jnp.zeros((6, width), F32)
        for ref in (acc_ghw, acc_ghb, acc_ghwe, acc_ghbe, acc_gls, acc_gmb):
            ref[...] = jnp.zeros_like(ref)

    base = pl.multiple_of(blk * ROWS, ROWS)

    def masked(value, first):
        row = first + lax.broadcasted_iota(jnp.int32, value.shape, 0)
        return jnp.where(row >= local, value, 0.0)

    before = masked(jnp.where(blk == 0, jnp.where(tm > 0, edge_ref[0], 0.0), x_up[0]), base - rows8)
    after = masked(jnp.where(blk == blks - 1, jnp.where(tm > 0, 0.0, edge_ref[0]), x_down[0]), base + ROWS)
    middle = masked(x_ref[0], base)
    for t in range(tiles):
        lanes = slice(t * LANES, (t + 1) * LANES)
        pad4[t, 0:rows8, :] = before[:, lanes]
        pad4[t, rows8 : rows8 + ROWS, :] = middle[:, lanes]
        pad4[t, rows8 + ROWS :, :] = after[:, lanes]
    bias = conv_b[...].reshape(1, width)
    chunk = 64
    for r in range(0, ROWS, chunk):
        parts = []
        for t in range(tiles):
            lanes = slice(t * LANES, (t + 1) * LANES)
            total = bias[:, lanes]
            for k in range(KERNEL):
                first = r + rows8 - KERNEL // 2 + k
                total = total + pad4[t, first : first + chunk, :] * conv_w[k : k + 1, lanes]
            parts.append(total)
        mean = jnp.sum(sum(parts[1:], parts[0]), axis=1, keepdims=True) * (1.0 / width)
        parts = [p - mean for p in parts]
        squares = [p * p for p in parts]
        variance = jnp.sum(sum(squares[1:], squares[0]), axis=1, keepdims=True) * (1.0 / width)
        istd = lax.rsqrt(variance + 1e-6)
        for t in range(tiles):
            nrm4[t, r : r + chunk, :] = parts[t] * istd
        istd1[r : r + chunk, :] = jnp.broadcast_to(istd, (chunk, LANES))

    def by_parity(ref, first):
        return jnp.concatenate(
            [
                jnp.concatenate([ref[t, pl.ds(first + par, PAIRS, stride=2), :] for t in range(tiles)], 1)
                for par in range(2)
            ],
            0,
        )

    normed = by_parity(nrm4, 0)
    o_norm[...] = normed
    for par in range(2):
        o_istd[par * PAIRS : (par + 1) * PAIRS, :] = istd1[pl.ds(par, PAIRS, stride=2), :]
    adapted = normed * scale_t[pl.ds(band, 1), :] + shift_t[pl.ds(band, 1), :]
    ad = split(adapted)
    o_adt_h[...], o_adt_l[...] = ad[0].T, ad[1].T

    first_pair = pl.multiple_of(blk * PAIRS, PAIRS)
    wave_tiles = gs5.shape[0]
    for t in range(wave_tiles):
        lanes = slice(t * LANES, (t + 1) * LANES)
        stride = clips * wave_tiles
        value = cot_ref[pl.ds(clips * t + clip, PAIRS, stride=stride), :]
        gs5[t, 0:PAIRS, :] = value * inverse_envelope(first_pair, local, inverse, t, PAIRS)
        value = cot_down[pl.ds(clips * t + clip, 8, stride=stride), :]
        value = jnp.where(blk == blks - 1, jnp.where(tm > 0, 0.0, cot_edge[0, :, lanes]), value)
        gs5[t, PAIRS : PAIRS + 8, :] = value * inverse_envelope(first_pair + PAIRS, local, inverse, t, 8)
    now, one, two = ([gs5[t, d : d + PAIRS, :] for t in range(wave_tiles)] for d in range(3))
    mid = wave_tiles // 2
    right = lax.broadcasted_iota(jnp.int32, (PAIRS, LANES), 1) >= LANES // 2
    odd = two[:mid] + [jnp.where(right, now[mid], two[mid])] + now[mid + 1 :] + one
    c1, c2, s1, s2 = fifths()
    folded = []
    for par, segment in enumerate((now + one, odd)):
        seg = [v * windows[par : par + 1, t * LANES : (t + 1) * LANES] for t, v in enumerate(segment)]
        v = [jnp.concatenate(seg[2 * j : 2 * j + 2], 1) for j in range(5)]
        p14, m41, p23, m32 = v[1] + v[4], v[4] - v[1], v[2] + v[3], v[3] - v[2]
        folded.append(
            (
                v[0] + p14 + p23,
                v[0] + c1 * p14 + c2 * p23,
                s1 * m41 + s2 * m32,
                v[0] + c2 * p14 + c1 * p23,
                s2 * m41 - s1 * m32,
            )
        )
    f0, fa, fb, fc, fd = (jnp.concatenate([e, o], 0) for e, o in zip(*folded))
    spectrum_grads = (
        dot3(split(jnp.concatenate([fa, fb], 1)), (t1h[...], t1l[...]), NT),
        dot3(split(jnp.concatenate([fc, fd], 1)), (t2h[...], t2l[...]), NT),
        dot3(split(f0), (t0h[...], t0l[...]), NT),
    )

    hidden = up_h.shape[1]
    step = 256
    up_bias = up_b[...].reshape(1, hidden)
    for j in range(hidden // step):
        cols = slice(j * step, (j + 1) * step)
        upward = dot3(ad, (up_h[:, cols], up_l[:, cols])) + up_bias[:, cols]
        cdf = 0.5 + 0.5 * lax.erf(upward * np.float32(0.7071067811865476))
        density = jnp.exp(upward * upward * -0.5) * np.float32(0.3989422804014327)
        o_slope[:, cols] = cdf + upward * density
        o_act_h[:, cols], o_act_l[:, cols] = split(upward * cdf)
    branch = dot3((o_act_h[...], o_act_l[...]), (down_h[...], down_l[...])) + down_b[...].reshape(1, width)
    scale = layer_scale[...].reshape(1, width)
    residual = by_parity(pad4, rows8) + scale * branch
    res = split(residual)
    res_t = res[0].T, res[1].T

    bias = head_b[...].reshape(1, nfft + 2)
    ext = split(ext_w[...])
    ext_logits = dot3(ext, res, NT)
    lane = lax.broadcasted_iota(jnp.int32, (1, ROWS), 1)
    ext_frame = base + jnp.where(lane < PAIRS, 2 * lane, 2 * (lane - PAIRS) + 1)
    ext_present = ext_frame >= local

    def magnitudes(logits, present):
        raw = jnp.where(present, jnp.exp(logits), 0.0)
        squashed = jnp.tanh(raw * np.float32(0.01))
        return 100.0 * squashed, raw * (1.0 - squashed * squashed)

    ext_mag, ext_slope = magnitudes(ext_logits[0:1] + bias[:, half : half + 1], ext_present)
    ext_sin, ext_cos = sin_cos(ext_logits[1:2] + bias[:, nfft + 1 : nfft + 2])
    ext_real = ext_mag * ext_cos
    ext_imag = ext_mag * ext_sin
    ext_real_col = jnp.concatenate([ext_real, jnp.zeros((7, ROWS), F32)], 0).T[:, 0:1]

    row = lax.broadcasted_iota(jnp.int32, (PAIRS, 1), 0)
    at = 0
    for index, grads in enumerate(spectrum_grads):
        n = grads.shape[1] // 2
        cols = slice(at, at + 2 * n)
        logits = dot3(res, (head_h[cols, :], head_l[cols, :]), NT)
        for par in range(2):
            rows = slice(par * PAIRS, (par + 1) * PAIRS)
            present = base + 2 * row + par >= local
            value = logits[rows] + head_bias[par : par + 1, cols]
            magnitude, slope = magnitudes(value[:, :n], present)
            sine, cosine = sin_cos(value[:, n:])
            real, imag = magnitude * cosine, magnitude * sine
            g_real, g_imag = grads[rows, :n], grads[rows, n:]
            if index == 2:
                corner = lax.broadcasted_iota(jnp.int32, (PAIRS, n), 1) == 0
                shown = jnp.where(corner, ext_real_col[rows], imag)
                g_imag = jnp.where(corner, 0.0, g_imag)
            else:
                shown = imag
            o_spec[rows, at : at + n] = real
            o_spec[rows, at + n : at + 2 * n] = shown
            g_mag = slope * (g_real * cosine + g_imag * sine)
            g_ang = g_imag * real - g_real * imag
            gl = jnp.concatenate([g_mag, g_ang], 1)
            acc_ghb[:, cols] += fold8(gl)
            gl_h[rows, cols], gl_l[rows, cols] = split(gl)
        at += 2 * n

    corner_t = spectrum_grads[2][:, spectrum_grads[2].shape[1] // 2 :].T
    ext_g = corner_t[0:1, :]
    ext_grads = jnp.concatenate(
        [ext_slope * ext_g * ext_cos, -ext_g * ext_imag, jnp.zeros((6, ROWS), F32)], 0
    )
    acc_ghbe[...] += ext_grads
    acc_ghwe[...] += dot3(split(ext_grads), res)
    gl = (gl_h[...], gl_l[...])
    ext_cols = ext_grads.T
    grad_mixed = (
        dot3(gl, (head_h[...], head_l[...]))
        + ext_cols[:, 0:1] * ext_w[0:1, :]
        + ext_cols[:, 1:2] * ext_w[1:2, :]
    )
    acc_ghw[...] += dot3(res_t, gl)
    acc_gls[...] += fold8(grad_mixed * branch)
    acc_gmb[...] += fold8(grad_mixed)
    for par in range(2):
        rows = slice(par * PAIRS, (par + 1) * PAIRS)
        for t in range(tiles):
            gm4[t, pl.ds(par, PAIRS, stride=2), :] = grad_mixed[rows, t * LANES : (t + 1) * LANES]
    for t in range(tiles):
        o_gm[:, t * LANES : (t + 1) * LANES] = gm4[t]
    grad_branch = grad_mixed * scale
    gb = split(grad_branch)
    o_gb_h[...], o_gb_l[...] = gb
    o_gbt_h[...], o_gbt_l[...] = gb[0].T, gb[1].T

    @pl.when((clip == clips - 1) & (blk == blks - 1))
    def _():
        total = jnp.sum(acc_ghb[...], axis=0, keepdims=True)
        for at, first in places:
            for t in range(tiles):
                block = acc_ghw[t * LANES : (t + 1) * LANES, at : at + LANES]
                head4[t, pl.ds(first, LANES, stride=5), :] = block.T
            block = jnp.broadcast_to(total[:, at : at + LANES], (LANES, LANES))
            bias4[pl.ds(first, LANES, stride=5), :] = block.T
        ext_sums = jnp.sum(acc_ghbe[...], axis=1, keepdims=True)
        for i, c in enumerate((half, nfft + 1)):
            for t in range(tiles):
                head4[t, c : c + 1, :] = acc_ghwe[i : i + 1, t * LANES : (t + 1) * LANES]
            bias4[c : c + 1, :] = jnp.broadcast_to(ext_sums[i : i + 1], (1, LANES))
        core = lax.axis_index("clip") % 2
        for here, first in ((core == 0, 0), (core == 1, half + 1)):

            @pl.when(here)
            def _(first=first):
                for t in range(tiles):
                    lanes = slice(t * LANES, (t + 1) * LANES)
                    for ref, at in ((o_keep, first), (o_send, half + 1 - first)):
                        ref[0 : half + 1, lanes] = head4[t, at : at + half + 1, :]
                        ref[half + 1 :, lanes] = jnp.zeros((ref.shape[0] - half - 1, LANES), F32)

        o_small[...] = jnp.zeros_like(o_small)
        for c in range(0, nfft, LANES):
            o_small[0:1, c : c + LANES] = bias4[c : c + LANES, :].T[0:1, :]
        o_small[0:1, nfft : nfft + 2] = jnp.concatenate(
            [bias4[nfft : nfft + 1, 0:1], bias4[nfft + 1 : nfft + 2, 0:1]], 1
        )
        o_small[1:2, :width] = jnp.sum(acc_gls[...], axis=0, keepdims=True)
        o_small[2:3, :width] = jnp.sum(acc_gmb[...], axis=0, keepdims=True) * scale


def whole(shape):
    return pl.BlockSpec(shape, lambda *_: (0,) * len(shape))


def fixed(shape):
    return pl.BlockSpec(shape, lambda *_: (0,) * len(shape), pipeline_mode=pl.Buffered(1))


def row_halves(blks, rows, rows8, width, clip=None):
    per, last = rows // rows8, blks * rows // rows8 - 1
    places = [
        (rows, lambda j: j),
        (rows8, lambda j: jnp.maximum(j * per - 1, 0)),
        (rows8, lambda j: jnp.minimum(j * per + per, last)),
    ]
    if clip is None:
        return [pl.BlockSpec((1, n, width), lambda i, j, *_, f=f: (i, f(j), 0)) for n, f in places]
    return [pl.BlockSpec((1, n, width), lambda j, *_, f=f: (clip, f(j), 0)) for n, f in places]


def run_head(bands, offsets, x, edge, cot, cot_edge, weights, turns, consts):
    clips, frames, width = x.shape
    blks = frames // ROWS
    count = clips * frames
    hidden = weights[4].shape[1]
    nfft = turns.shape[1]
    block = lambda i, j, *_: (i * blks + j, 0)
    column = lambda i, j, *_: (0, i * blks + j)
    per_clip = lambda shape: pl.BlockSpec((1,) + shape, lambda i, j, *_: (i, 0, 0))
    in_specs = row_halves(blks, ROWS, edge.shape[1], width)
    in_specs += [per_clip(edge.shape[1:])]
    operands = list(weights) + [turns] + list(consts)
    rows = cot.shape[0] // blks
    few = rows * 8 // PAIRS
    per, last = rows // few, cot.shape[0] // few - 1
    in_specs += [
        pl.BlockSpec((rows, LANES), lambda i, j, *_: (j, 0)),
        pl.BlockSpec((few, LANES), lambda i, j, *_: (jnp.minimum(j * per + per, last), 0)),
        per_clip(cot_edge.shape[1:]),
    ]
    in_specs += [fixed(v.shape) for v in operands]
    row_out = lambda n, dtype: (SDS((count, n), dtype), pl.BlockSpec((ROWS, n), block))
    col_out = (SDS((width, count), BF16), pl.BlockSpec((width, ROWS), column))
    outs = [
        row_out(width, F32),
        row_out(LANES, F32),
        col_out,
        col_out,
        row_out(hidden, BF16),
        row_out(hidden, BF16),
        row_out(hidden, F32),
        row_out(nfft, F32),
        row_out(width, F32),
        row_out(width, BF16),
        row_out(width, BF16),
        col_out,
        col_out,
        (SDS((HEAD_ROWS + hidden // 2, width), F32), whole((HEAD_ROWS, width))),
        (SDS((HEAD_ROWS + hidden // 2, width), F32), whole((HEAD_ROWS, width))),
        (SDS((8, hidden), F32), whole((8, hidden))),
    ]
    wave_tiles = nfft // 2 // LANES
    tiles = width // LANES
    scratch = [pltpu.VMEM((width, hidden), BF16)] * 2 + [pltpu.VMEM((hidden, width), BF16)] * 2
    scratch += [
        pltpu.VMEM((nfft, width), BF16),
        pltpu.VMEM((nfft, width), BF16),
        pltpu.VMEM((2, nfft), F32),
        pltpu.VMEM((8, width), F32),
        pltpu.VMEM((tiles, nfft + 8, LANES), F32),
        pltpu.VMEM((nfft + 8, LANES), F32),
        pltpu.VMEM((tiles, ROWS + 2 * edge.shape[1], LANES), F32),
        pltpu.VMEM((tiles, ROWS, LANES), F32),
        pltpu.VMEM((ROWS, LANES), F32),
        pltpu.VMEM((wave_tiles, PAIRS + 8, LANES), F32),
        pltpu.VMEM((tiles, ROWS, LANES), F32),
        pltpu.VMEM((ROWS, nfft), BF16),
        pltpu.VMEM((ROWS, nfft), BF16),
        pltpu.VMEM((width, nfft), F32),
        pltpu.VMEM((8, nfft), F32),
        pltpu.VMEM((8, width), F32),
        pltpu.VMEM((8, ROWS), F32),
        pltpu.VMEM((8, width), F32),
        pltpu.VMEM((8, width), F32),
    ]
    return pl.pallas_call(
        head_kernel,
        grid_spec=pltpu.PrefetchScalarGridSpec(
            num_scalar_prefetch=2,
            grid=(clips, blks),
            in_specs=in_specs,
            out_specs=[s for _, s in outs],
            scratch_shapes=scratch,
        ),
        out_shape=[s for s, _ in outs],
        compiler_params=pltpu.CompilerParams(vmem_limit_bytes=VMEM),
        cost_estimate=pl.CostEstimate(flops=80_000_000_000, bytes_accessed=90_000_000, transcendentals=0),
        name="head",
    )(bands, offsets, x, x, x, edge, cot, cot, cot_edge, *operands)


def down_kernel(gbt_h, gbt_l, act_h, act_l, *refs):
    o_keep, o_send, acc, keep, send, sems = refs[-6:]
    step = pl.program_id(0)

    @pl.when(step == 0)
    def _():
        acc[...] = jnp.zeros_like(acc)

    acc[...] += dot3((gbt_h[...], gbt_l[...]), (act_h[...], act_l[...]))

    @pl.when(step == pl.num_programs(0) - 1)
    def _():
        core = lax.axis_index("clip") % 2
        rows = keep.shape[0]
        copies = []
        for i, (ref, out, half) in enumerate(((keep, o_keep, core), (send, o_send, 1 - core))):
            mine = pl.ds(pl.multiple_of(half * rows, rows), rows)
            ref[...] = acc[:, mine].T
            above = out.shape[0] - rows
            copies.append(pltpu.make_async_copy(ref, out.at[pl.ds(above, rows), :], sems.at[i]))
            copies[-1].start()
        for copy in copies:
            copy.wait()


def run_down(gbt, act, keep, send):
    width, count = gbt[0].shape
    hidden = act[0].shape[1]
    rows = 512
    any_spec = pl.BlockSpec(memory_space=pl.ANY)
    half = pltpu.VMEM((hidden // 2, width), F32)
    return pl.pallas_call(
        down_kernel,
        grid=(count // rows,),
        in_specs=[pl.BlockSpec((width, rows), lambda i: (0, i))] * 2
        + [pl.BlockSpec((rows, hidden), lambda i: (i, 0))] * 2
        + [any_spec] * 2,
        out_specs=[any_spec] * 2,
        out_shape=[SDS(keep.shape, F32), SDS(send.shape, F32)],
        input_output_aliases={4: 0, 5: 1},
        scratch_shapes=[pltpu.VMEM((width, hidden), F32), half, half, pltpu.SemaphoreType.DMA((2,))],
        compiler_params=pltpu.CompilerParams(vmem_limit_bytes=VMEM),
        cost_estimate=pl.CostEstimate(flops=10_000_000_000, bytes_accessed=20_000_000, transcendentals=0),
        name="down_grads",
    )(*gbt, *act, keep, send)


def up_kernel(gb_h, gb_l, slope, adt_h, adt_l, down_w, *refs):
    o_keep, o_send, o_gub, o_gu_h, o_gu_l, dw_h, dw_l, acc, acc_gub = refs[-9:]
    step = pl.program_id(0)
    hidden = slope.shape[1]

    @pl.when(step == 0)
    def _():
        dw_h[...], dw_l[...] = split(down_w[...])
        acc[...] = jnp.zeros_like(acc)
        acc_gub[...] = jnp.zeros_like(acc_gub)

    cols = 512
    for j in range(hidden // cols):
        part = slice(j * cols, (j + 1) * cols)
        gu = dot3((gb_h[...], gb_l[...]), (dw_h[part, :], dw_l[part, :]), NT) * slope[:, part]
        acc_gub[:, part] += fold8(gu)
        gs = split(gu)
        o_gu_h[:, part], o_gu_l[:, part] = gs
        acc[:, part] += dot3((adt_h[...], adt_l[...]), gs)

    @pl.when(step == pl.num_programs(0) - 1)
    def _():
        o_gub[...] = jnp.sum(acc_gub[...], axis=0, keepdims=True)
        core = lax.axis_index("clip") % 2
        rows = o_keep.shape[0]
        for ref, half in ((o_keep, core), (o_send, 1 - core)):
            ref[...] = acc[:, pl.ds(pl.multiple_of(half * rows, rows), rows)].T


def after(values, operand):
    return lax.optimization_barrier((operand, tuple(values)))[0] if values else operand


def run_up(gb, slope, adt, down_w, size, part, so_far, waits=()):
    count, width = gb[0].shape
    hidden = slope.shape[1]
    rows = 512
    row = lambda i: (i, 0)
    in_specs = [pl.BlockSpec((rows, width), row)] * 2 + [pl.BlockSpec((rows, size), lambda i: (i, part))]
    in_specs += [pl.BlockSpec((width, rows), lambda i: (0, i))] * 2
    in_specs += [pl.BlockSpec((size, width), lambda i: (part, 0), pipeline_mode=pl.Buffered(1))]
    so_far = list(so_far)
    return pl.pallas_call(
        up_kernel,
        grid=(count // rows,),
        in_specs=in_specs + [pl.BlockSpec(memory_space=pl.ANY)] * len(so_far),
        out_specs=[pl.BlockSpec((size // 2, width), lambda i: (part, 0))] * 2
        + [whole((1, size)), pl.BlockSpec((rows, size), row), pl.BlockSpec((rows, size), row)],
        out_shape=[
            SDS((hidden // 2, width), F32),
            SDS((hidden // 2, width), F32),
            SDS((1, size), F32),
            SDS((count, size), BF16),
            SDS((count, size), BF16),
        ],
        input_output_aliases={6 + i: i for i in range(len(so_far))},
        scratch_shapes=[pltpu.VMEM((size, width), BF16)] * 2
        + [pltpu.VMEM((width, size), F32), pltpu.VMEM((8, size), F32)],
        compiler_params=pltpu.CompilerParams(vmem_limit_bytes=VMEM),
        cost_estimate=pl.CostEstimate(flops=10_000_000_000, bytes_accessed=20_000_000, transcendentals=0),
        name="up_grads",
    )(*gb, after(waits, slope), *adt, down_w, *so_far)


def norm_kernel(sizes, clip, bands, *refs):
    gu = refs[: 2 * len(sizes)]
    up_w, norm, istd, scale_t = refs[2 * len(sizes) : 2 * len(sizes) + 4]
    edge_in = refs[2 * len(sizes) + 4] if clip else None
    o_gh, o_edge, o_scale, o_shift, up_h, up_l, nat4, acc_scale, acc_shift = refs[-9:]
    blk, blks = pl.program_id(0), pl.num_programs(0)
    band = bands[clip]
    width = norm.shape[1]
    tiles = width // LANES

    @pl.when(blk == 0)
    def _():
        up_h[...], up_l[...] = split(up_w[...])
        for ref in (o_scale, o_shift, acc_scale, acc_shift):
            ref[...] = jnp.zeros_like(ref)
        if edge_in is not None:
            o_edge[...] = edge_in[...]

    ga, at = None, 0
    for j, hidden in enumerate(sizes):
        cols = slice(at, at + hidden)
        term = dot3((gu[2 * j][...], gu[2 * j + 1][...]), (up_h[:, cols], up_l[:, cols]), NT)
        ga = term if ga is None else ga + term
        at += hidden
    normed = norm[...]
    acc_scale[...] += fold8(ga * normed)
    acc_shift[...] += fold8(ga)
    gn = ga * scale_t[pl.ds(band, 1), :]
    mean = jnp.sum(gn, axis=1, keepdims=True) * (1.0 / width)
    along = jnp.sum(gn * normed, axis=1, keepdims=True) * (1.0 / width)
    gh = istd[:, 0:1] * (gn - mean - normed * along)
    for par in range(2):
        for t in range(tiles):
            nat4[t, pl.ds(par, PAIRS, stride=2), :] = gh[par * PAIRS : (par + 1) * PAIRS, t * LANES : (t + 1) * LANES]
    for t in range(tiles):
        o_gh[:, t * LANES : (t + 1) * LANES] = nat4[t]
    tm = lax.axis_index("tm")
    for here, first in (((tm == 0) & (blk == blks - 1), ROWS - 8), ((tm == 1) & (blk == 0), 0)):

        @pl.when(here)
        def _(first=first):
            for t in range(tiles):
                o_edge[clip, :, t * LANES : (t + 1) * LANES] = nat4[t, first : first + 8, :]

    @pl.when(blk == blks - 1)
    def _():
        o_scale[pl.ds(band, 1), :] = jnp.sum(acc_scale[...], axis=0, keepdims=True)
        o_shift[pl.ds(band, 1), :] = jnp.sum(acc_shift[...], axis=0, keepdims=True)


def run_norm(bands, gus, up_w, norm, istd, scale_t, edge, clip, waits=()):
    clips = edge.shape[0]
    earlier = [edge] if clip else []
    count, width = norm.shape
    blks = count // clips // ROWS
    block = lambda j, *_: (clip * blks + j, 0)
    flat = [v for pair in gus for v in pair]
    in_specs = [pl.BlockSpec((ROWS, v.shape[1]), block) for v in flat]
    in_specs += [fixed(up_w.shape), pl.BlockSpec((ROWS, width), block)]
    in_specs += [pl.BlockSpec((ROWS, LANES), block), fixed(scale_t.shape)]
    in_specs += [fixed(v.shape) for v in earlier]
    return pl.pallas_call(
        functools.partial(norm_kernel, [pair[0].shape[1] for pair in gus], clip),
        grid_spec=pltpu.PrefetchScalarGridSpec(
            num_scalar_prefetch=1,
            grid=(blks,),
            in_specs=in_specs,
            out_specs=[pl.BlockSpec((ROWS, width), lambda j, *_: (j, 0)), whole(edge.shape)] + [whole(scale_t.shape)] * 2,
            scratch_shapes=[pltpu.VMEM(up_w.shape, BF16)] * 2
            + [pltpu.VMEM((width // LANES, ROWS, LANES), F32)]
            + [pltpu.VMEM((8, width), F32)] * 2,
        ),
        out_shape=[SDS((count // clips, width), F32), SDS(edge.shape, F32)] + [SDS(scale_t.shape, F32)] * 2,
        compiler_params=pltpu.CompilerParams(vmem_limit_bytes=VMEM),
        cost_estimate=pl.CostEstimate(flops=5_000_000_000, bytes_accessed=12_000_000, transcendentals=0),
        name="norm_grads",
    )(bands, *flat, up_w, after(waits, norm), istd, scale_t, *earlier)


def conv_kernel(
    clip, offsets, x_ref, x_up, x_down, edge_ref, gh_ref, gh_up, gh_down, gh_edge, gm_ref, conv_w, *refs
):
    o_gi, o_acc, pad4, gh4 = refs[-4:]
    blk, blks = pl.program_id(0), pl.num_programs(0)
    rows, width = x_ref.shape[1], x_ref.shape[2]
    tiles = width // LANES
    tm = lax.axis_index("tm")
    local = offsets[clip] - tm * blks * rows
    rows8 = edge_ref.shape[1]
    base = blk * rows

    @pl.when(blk == 0)
    def _():
        o_acc[...] = refs[0][...] if clip else jnp.zeros_like(o_acc)

    def masked(value, first):
        row = first + lax.broadcasted_iota(jnp.int32, value.shape, 0)
        return jnp.where(row >= local, value, 0.0)

    def above(edge, up):
        return jnp.where(blk == 0, jnp.where(tm > 0, edge[0], 0.0), up[0])

    def below(edge, down):
        return jnp.where(blk == blks - 1, jnp.where(tm > 0, 0.0, edge[0]), down[0])

    before, after = masked(above(edge_ref, x_up), base - rows8), masked(below(edge_ref, x_down), base + rows)
    g_before, g_after = above(gh_edge, gh_up), below(gh_edge, gh_down)
    middle = masked(x_ref[0], base)
    for t in range(tiles):
        lanes = slice(t * LANES, (t + 1) * LANES)
        pad4[t, 0:rows8, :] = before[:, lanes]
        pad4[t, rows8 : rows8 + rows, :] = middle[:, lanes]
        pad4[t, rows8 + rows :, :] = after[:, lanes]
        gh4[t, 0:rows8, :] = g_before[:, lanes]
        gh4[t, rows8 : rows8 + rows, :] = gh_ref[0, :, lanes]
        gh4[t, rows8 + rows :, :] = g_after[:, lanes]
    chunk = 64
    for r in range(0, rows, chunk):
        shown = base + r + lax.broadcasted_iota(jnp.int32, (chunk, LANES), 0) >= local
        for t in range(tiles):
            lanes = slice(t * LANES, (t + 1) * LANES)
            gh = gh4[t, rows8 + r : rows8 + r + chunk, :]
            o_acc[8 * KERNEL :, lanes] += fold8(gh)
            total = gm_ref[0, r : r + chunk, lanes]
            for k in range(KERNEL):
                first = r + rows8 + KERNEL // 2 - k
                total = total + conv_w[k : k + 1, lanes] * gh4[t, first : first + chunk, :]
                first = r + rows8 - KERNEL // 2 + k
                o_acc[8 * k : 8 * k + 8, lanes] += fold8(gh * pad4[t, first : first + chunk, :])
            o_gi[0, r : r + chunk, lanes] = jnp.where(shown, total, 0.0)


def run_conv(offsets, x, edge, gh, gh_edge, gm, conv_w, clip, so_far, waits=()):
    clips, frames, width = x.shape
    blks = frames // ROWS
    rows8 = edge.shape[1]
    mine = pl.BlockSpec((1, rows8, width), lambda j, *_: (clip, 0, 0))
    padded = pltpu.VMEM((width // LANES, ROWS + 2 * rows8, LANES), F32)
    blocks = row_halves(blks, ROWS, rows8, width, clip)
    in_specs = blocks + [mine] + row_halves(blks, ROWS, rows8, width, 0) + [mine] + blocks[:1]
    in_specs += [fixed(conv_w.shape)]
    operands = [x, x, x, edge, gh, gh, gh, gh_edge, after(waits, gm), conv_w]
    aliases = {}
    sums = (8 * (KERNEL + 1), width)
    if so_far:
        grads, acc = so_far
        operands.append(acc)
        in_specs.append(fixed(acc.shape))
        aliases = {1 + len(operands): 0}
        operands.append(grads)
        in_specs.append(pl.BlockSpec(memory_space=pl.ANY))
    return pl.pallas_call(
        functools.partial(conv_kernel, clip),
        grid_spec=pltpu.PrefetchScalarGridSpec(
            num_scalar_prefetch=1,
            grid=(blks,),
            in_specs=in_specs,
            out_specs=[blocks[0], whole(sums)],
            scratch_shapes=[padded, padded],
        ),
        out_shape=[SDS(x.shape, F32), SDS(sums, F32)],
        input_output_aliases=aliases,
        compiler_params=pltpu.CompilerParams(vmem_limit_bytes=VMEM),
        cost_estimate=pl.CostEstimate(flops=5_000_000_000, bytes_accessed=17_000_000, transcendentals=0),
        name="conv_grads",
    )(offsets, *operands)


def pack_kernel(acc, small, scales0, scales1, shifts0, shifts1, *refs):
    gubs, o_pack = refs[:-1], refs[-1]
    width = acc.shape[1]
    for k in range(KERNEL + 1):
        o_pack[k : k + 1, :] = jnp.sum(acc[8 * k : 8 * k + 8, :], axis=0, keepdims=True)
    o_pack[8:12, :] = scales0[...] + scales1[...]
    o_pack[12:16, :] = shifts0[...] + shifts1[...]
    o_pack[16:18, :] = small[1:3, :width]
    for i in range(3):
        o_pack[18 + i : 19 + i, :] = small[0:1, i * width : (i + 1) * width]
        gub = jnp.concatenate([v[...] for v in gubs], 1)
        o_pack[21 + i : 22 + i, :] = gub[:, i * width : (i + 1) * width]
    o_pack[24:, :] = jnp.zeros((o_pack.shape[0] - 24, width), F32)


def wave_kernel(
    first_blk, frames, scaled, offsets, spec, t1h, t1l, t2h, t2l, t0h, t0l, windows, inverse, *refs
):
    o_wave, o_tail, accs = refs[-3:]
    blk, clip = pl.program_id(0), pl.program_id(1)
    blks, clips = pl.num_programs(0), pl.num_programs(1)
    tiles = accs.shape[1]
    first = (first_blk + blk) * PAIRS
    local = offsets[clip] - lax.axis_index("tm") * frames
    acc5 = accs.at[clip]

    @pl.when(blk == 0)
    def _():
        for t in range(tiles):
            lanes = slice(t * LANES, (t + 1) * LANES)
            acc5[t, 0:8, :] = refs[0][0, :, lanes] if scaled else jnp.zeros((8, LANES), F32)

    @pl.when(blk > 0)
    def _():
        for t in range(tiles):
            acc5[t, 0:8, :] = acc5[t, PAIRS : PAIRS + 8, :]

    for t in range(tiles):
        acc5[t, 8:, :] = jnp.zeros((PAIRS, LANES), F32)

    n1, n2 = t1h.shape[0], t2h.shape[0]
    ab = dot3(split(spec[:, :n1]), (t1h[...], t1l[...]))
    cd = dot3(split(spec[:, n1 : n1 + n2]), (t2h[...], t2l[...]))
    p0 = dot3(split(spec[:, n1 + n2 :]), (t0h[...], t0l[...]))
    c1, c2, s1, s2 = fifths()
    sides = []
    for par in range(2):
        rows = slice(par * PAIRS, (par + 1) * PAIRS)
        w = p0.shape[1]
        a, b, c, d, p = ab[rows, :w], ab[rows, w:], cd[rows, :w], cd[rows, w:], p0[rows]
        e1, o1 = p + c1 * a + c2 * c, s1 * b + s2 * d
        e2, o2 = p + c2 * a + c1 * c, s2 * b - s1 * d
        v = [p + a + c, e1 - o1, e2 - o2, e2 + o2, e1 + o1]
        seg = []
        for t in range(2 * tiles):
            part = v[t // 2][:, (t % 2) * LANES : (t % 2 + 1) * LANES]
            seg.append(part * windows[par : par + 1, t * LANES : (t + 1) * LANES])
        sides.append(seg)
    even, odd = sides
    mid = tiles // 2
    right = lax.broadcasted_iota(jnp.int32, (PAIRS, LANES), 1) >= LANES // 2
    for t in range(tiles):
        here = even[t]
        if t > mid:
            here = here + odd[t]
        if t == mid:
            here = here + jnp.where(right, odd[t], 0.0)
        acc5[t, 0:PAIRS, :] += here
        acc5[t, 1 : PAIRS + 1, :] += even[tiles + t] + odd[tiles + t]
        if t < mid:
            acc5[t, 2 : PAIRS + 2, :] += odd[t]
        if t == mid:
            acc5[t, 2 : PAIRS + 2, :] += jnp.where(right, 0.0, odd[t])
        value = acc5[t, 0:PAIRS, :] * inverse_envelope(first, local, inverse, t, PAIRS)
        o_wave[pl.ds(clips * t + clip, PAIRS, stride=clips * tiles), :] = value

    @pl.when(blk == blks - 1)
    def _():
        for t in range(tiles):
            value = acc5[t, PAIRS : PAIRS + 8, :]
            if scaled:
                value = value * inverse_envelope(first + PAIRS, local, inverse, t, 8)
            o_tail[0, :, t * LANES : (t + 1) * LANES] = value


def run_wave(offsets, spec, consts, clips, first_blk, blks, earlier=(), waits=()):
    count, nfft = spec.shape
    all_blks = count // clips // ROWS
    tiles = nfft // 2 // LANES
    rows = clips * PAIRS * tiles
    in_specs = [pl.BlockSpec((ROWS, nfft), lambda j, i, *_: (i * all_blks + first_blk + j, 0))]
    in_specs += [fixed(v.shape) for v in consts]
    operands = [after(waits, spec), *consts]
    aliases = {}
    if earlier:
        carry, wave = earlier
        operands.append(carry)
        in_specs.append(pl.BlockSpec((1, 8, nfft // 2), lambda j, i, *_: (i, 0, 0)))
        aliases = {1 + len(operands): 0}
        operands.append(wave)
        in_specs.append(pl.BlockSpec(memory_space=pl.ANY))
    return pl.pallas_call(
        functools.partial(wave_kernel, first_blk, count // clips, first_blk == 0),
        grid_spec=pltpu.PrefetchScalarGridSpec(
            num_scalar_prefetch=1,
            grid=(blks, clips),
            in_specs=in_specs,
            out_specs=[
                pl.BlockSpec((rows, LANES), lambda j, i, *_: (first_blk + j, 0)),
                pl.BlockSpec((1, 8, nfft // 2), lambda j, i, *_: (i, 0, 0)),
            ],
            scratch_shapes=[pltpu.VMEM((clips, tiles, PAIRS + 8, LANES), F32)],
        ),
        out_shape=[SDS((rows * all_blks, LANES), F32), SDS((clips, 8, nfft // 2), F32)],
        input_output_aliases=aliases,
        compiler_params=pltpu.CompilerParams(vmem_limit_bytes=VMEM),
        cost_estimate=pl.CostEstimate(flops=5_000_000_000, bytes_accessed=8_000_000, transcendentals=0),
        name="wave",
    )(offsets, *operands)


def levels():
    clip = [("clip", 1 << i) for i in range((lax.axis_size("clip") - 1).bit_length())]
    tm = [("tm", 1 << i) for i in range((lax.axis_size("tm") - 1).bit_length())]
    return clip[:1] + clip[1:2] + tm + clip[2:]


def exchange(value, level):
    if level == "next":
        return lax.ppermute(value, "tm", [(i, i + 1) for i in range(lax.axis_size("tm") - 1)])
    across = {"clip": 0, "tm": 0}
    for axis, distance in level if isinstance(level, list) else [level]:
        across[axis] += distance
    if not across["tm"]:
        return lax.ppermute(value, "clip", [(i, i ^ across["clip"]) for i in range(lax.axis_size("clip"))])
    if not across["clip"]:
        return lax.ppermute(value, "tm", [(i, i ^ across["tm"]) for i in range(lax.axis_size("tm"))])
    n, m = lax.axis_size("clip"), lax.axis_size("tm")
    pairs = [(i * m + j, (i ^ across["clip"]) * m + (j ^ across["tm"])) for i in range(n) for j in range(m)]
    return lax.ppermute(value, ("clip", "tm"), pairs)


def side(level):
    axis, distance = level
    return lax.axis_index(axis) // distance % 2


class Sums:
    def __init__(self):
        self.running = []

    def add(self, steps, holds=()):
        entry = {"steps": steps, "holds": holds, "count": 0, "sent": None, "came": None, "left": 0, "sum": None}
        self.step(entry, None)
        self.running.append(entry)
        return entry

    def step(self, entry, values):
        try:
            entry["sent"] = entry["steps"].send(values)
            while entry["sent"][0][1] == levels()[0]:
                entry["sent"] = entry["steps"].send([exchange(*pair) for pair in entry["sent"]])
        except StopIteration as stop:
            entry["sent"], entry["sum"] = None, stop.value

    def waits(self):
        sent = []
        for entry in self.running:
            if entry["came"] is None and entry["sent"] is not None:
                entry["came"] = [exchange(*pair) for pair in entry["sent"]]
                entry["left"] = dict(entry["holds"]).get(entry["count"], 1)
                entry["count"] += 1
                sent += [pair[0] for pair in entry["sent"]]
        return sent

    def advance(self, results):
        done = []
        for entry in self.running:
            if entry["came"] is not None:
                entry["left"] -= 1
                if entry["left"] <= 0:
                    done.append(entry)
        if done:
            came, results = lax.optimization_barrier(([entry["came"] for entry in done], results))
            for entry, values in zip(done, came):
                entry["came"] = None
                self.step(entry, values)
        return results

    def finish(self, entry):
        while entry["sum"] is None:
            self.waits()
            self.advance(())
        return entry["sum"]


def halves_steps(keep, send, narrow):
    core, one, two, *last = levels()
    orders = ((one, two), (two, one))
    (came,) = yield [(send, core)]
    cols = keep.shape[1] // 2
    parts = [[(v, 0, c) for v in (keep, came)] for c in (0, cols)]

    def cut(terms, first):
        return [(v, row + first, col) for v, row, col in terms]

    def added(terms, rows):
        return sum(lax.dynamic_slice(v, (row, col), (rows, cols)) for v, row, col in terms)

    rows = keep.shape[0]
    for i in range(2):
        rows //= 2
        sides = [side(order[i]) for order in orders]
        came = yield [(added(cut(t, (1 - s) * rows), rows), o[i]) for t, s, o in zip(parts, sides, orders)]
        parts = [cut(t, s * rows) + [(c, 0, 0)] for t, s, c in zip(parts, sides, came)]
    value = jnp.concatenate([added(t, rows) for t in parts])
    halved = last if narrow and rows % (4 << len(last)) == 0 else []
    n, terms = value.shape[0], [(value, 0, 0)]
    for level in halved:
        n, s = n // 2, side(level)
        (came,) = yield [(added(cut(terms, (1 - s) * n), n), level)]
        terms = cut(terms, s * n) + [(came, 0, 0)]
    value = added(terms, n) if halved else value
    for level in last[len(halved) :]:
        (came,) = yield [(value, level)]
        value = value + came
    for level in halved[::-1]:
        s = side(level)
        (came,) = yield [(value, level)]
        value = jnp.concatenate([jnp.where(s == 0, value, came), jnp.where(s == 0, came, value)])
    parts = [value[:rows], value[rows:]]
    for i in (1, 0):
        came = yield [(part, order[i]) for part, order in zip(parts, orders)]
        parts = [jnp.concatenate(pair) for pair in zip(parts, came)]
    others = yield [(part, core) for part in parts]
    return parts, others, orders


def whole_steps(value):
    core, *rest = levels()
    (came,) = yield [(value, core)]
    value = value + came
    for pair in [rest[:1]] + [rest[i : i + 2] for i in range(1, len(rest), 2)]:
        came = yield [(value, [level]) for level in pair] + ([(value, pair)] if len(pair) == 2 else [])
        for other in came:
            value = value + other
    return value


def one_step(value, level):
    (came,) = yield [(value, level)]
    return came


def natural_blocks(orders, refs, copy):
    core = side(levels()[0])
    cols = refs[0].shape[1]
    rows = refs[0].shape[0] // 4
    for half in range(2):
        for here, pair in ((core == half, refs[:2]), (core != half, refs[2:])):

            @pl.when(here)
            def _(pair=pair, half=half):
                for i, (ref, order) in enumerate(zip(pair, orders)):
                    a, b = (side(level) for level in order)
                    for block in range(4):
                        first = (2 * jnp.bitwise_xor(block // 2, a) + jnp.bitwise_xor(block % 2, b)) * rows
                        value = ref[pl.ds(pl.multiple_of(first, 8), rows), :]
                        copy(half, slice(i * cols, (i + 1) * cols), block * rows, value)


def to_runs(runs):
    def copy(half, cols, first, value):
        for start, out, place, rows in runs:
            low, high = max(first, start), min(first + value.shape[0], start + rows)
            if low < high:
                at = place(half) + low - start
                out[at : at + high - low, cols] = value[low - first : high - first]

    return copy


def first_order_kernel(orders, *refs):
    o_head, o_down = refs[-2:]
    copy = to_runs(
        (
            (0, o_head, lambda half: half * (o_head.shape[0] // 2), o_head.shape[0] // 2),
            (HEAD_ROWS, o_down, lambda half: half * (o_down.shape[0] // 2), o_down.shape[0] // 2),
        )
    )
    natural_blocks(orders, refs[:4], copy)


def up_order_kernel(orders, *refs):
    o_up, up_t = refs[-2:]

    runs, at = [], 0
    for size, part in UP_PARTS:
        runs.append((at, up_t, lambda half, size=size, part=part: size * part + half * (size // 2), size // 2))
        at += size // 2
    copy = to_runs(runs)
    natural_blocks(orders, refs[:4], copy)
    for c in range(0, up_t.shape[0], LANES):
        o_up[:, c : c + LANES] = up_t[c : c + LANES, :].T


def run_order(kernel, total, out_shape, scratch=(), waits=()):
    parts, others, orders = total
    parts = after(waits, parts)
    return pl.pallas_call(
        functools.partial(kernel, orders),
        in_specs=[pl.BlockSpec(memory_space=pltpu.VMEM)] * 4,
        out_shape=out_shape,
        scratch_shapes=list(scratch),
        compiler_params=pltpu.CompilerParams(vmem_limit_bytes=VMEM),
        name="in_order",
    )(*parts, *others)


def unpack_kernel(pack, gcw, gcb, gscale, gshift, gls, gdb, ghb, gub):
    width = pack.shape[1]
    gcw[...] = pack[0:KERNEL, :]
    gcb[...] = pack[KERNEL : KERNEL + 1, :].reshape(width)
    gscale[...] = pack[8:12, :]
    gshift[...] = pack[12:16, :]
    gls[...] = pack[16:17, :].reshape(width)
    gdb[...] = pack[17:18, :].reshape(width)
    rows = [pack[18 + i : 19 + i, :] for i in range(6)]
    ghb[...] = jnp.concatenate(rows[:3], 1)[:, : ghb.shape[0]].reshape(ghb.shape[0])
    gub[...] = jnp.concatenate(rows[3:], 1).reshape(gub.shape[0])


def edges(value, index):
    n = value.shape[1]
    return jnp.where(index == 0, value[:, n - 8 :], value[:, :8])


def to_chunks(wave):
    clips, samples = wave.shape
    return wave.reshape(clips, samples // LANES, LANES).transpose(1, 0, 2).reshape(-1, LANES)


def from_chunks(chunks, clips):
    rows = chunks.shape[0] // clips
    return chunks.reshape(rows, clips, LANES).transpose(1, 0, 2).reshape(clips, rows * LANES)


def body(
    inputs,
    band_ids,
    offsets,
    conv_weight,
    conv_bias,
    scale_table,
    shift_table,
    up_weight,
    up_bias,
    down_weight,
    down_bias,
    layer_scale,
    head_weight,
    head_bias,
    wave_cotangent,
):
    clips, frames, width = inputs.shape
    assert lax.axis_size("tm") == 2
    nfft = head_weight.shape[1] - 2
    half = nfft // 2
    hidden = up_weight.shape[1]
    tm = lax.axis_index("tm")
    core = lax.axis_index("clip") % 2
    swap = lambda v: lax.ppermute(v, "tm", [(0, 1), (1, 0)])
    transforms, windows, inverse, turns = tables(nfft)
    dft = [jnp.asarray(v) for pair in transforms for v in pair]
    consts = dft + [jnp.asarray(windows), jnp.asarray(inverse)]

    edge = swap(edges(inputs, tm))
    cot_edge = swap(jnp.pad(wave_cotangent[:, :nfft].reshape(clips, 2, half), ((0, 0), (0, 6), (0, 0))))
    weights = (
        conv_weight,
        conv_bias,
        scale_table,
        shift_table,
        up_weight,
        up_bias,
        down_weight,
        down_bias,
        layer_scale,
        head_weight.T,
        head_bias,
    )
    (
        norm, istd, adt_h, adt_l, act_h, act_l, slope, spec, gm, gb_h, gb_l, gbt_h, gbt_l, hg_keep, hg_send, small,
    ) = run_head(
        band_ids, offsets, inputs, edge, to_chunks(wave_cotangent), cot_edge, weights, jnp.asarray(turns), consts
    )

    keep, send = run_down((gbt_h, gbt_l), (act_h, act_l), hg_keep, hg_send)
    sums = Sums()
    first_total = sums.add(halves_steps(keep, send, True))
    blks = frames // ROWS
    gus, gubs, halves = [], [], ()
    for size, part in UP_PARTS:
        results = run_up((gb_h, gb_l), slope, (adt_h, adt_l), down_weight, size, part, halves, waits=sums.waits())
        *halves, gub, gu_h, gu_l = sums.advance(results)
        gus.append((gu_h, gu_l))
        gubs.append(gub)
    up_total = sums.add(halves_steps(*halves, False), {3: 2})
    normed, gh_edge = [], edge
    for clip in range(clips):
        results = run_norm(band_ids, gus, up_weight, norm, istd, scale_table, gh_edge, clip, waits=sums.waits())
        gh_edge = results[1]
        normed.append(sums.advance(results))
    gh = [v[0][None] for v in normed]
    gh_edge = sums.add(one_step(normed[-1][1], ("tm", 1)))
    late = blks // 2
    wave, tail = run_wave(offsets, spec, consts, clips, late, blks - late, waits=sums.waits())
    wave, tail = sums.advance((wave, tail))
    arrived = sums.add(one_step(tail, "next"))
    gh_edge = sums.finish(gh_edge)
    so_far = ()
    gm = gm.reshape(clips, frames, width)
    for clip in range(clips):
        so_far = run_conv(
            offsets, inputs, edge, gh[clip], gh_edge, gm, conv_weight, clip, so_far, waits=sums.waits()
        )
        so_far = sums.advance(so_far)
    grad_inputs, acc = so_far
    pack = pl.pallas_call(pack_kernel, out_shape=SDS((32, width), F32), name="pack")(
        acc, small, *[v[2] for v in normed], *[v[3] for v in normed], *gubs
    )
    small_total = sums.add(whole_steps(pack))

    arrived = sums.finish(arrived)
    wave, over = run_wave(offsets, spec, consts, clips, 0, late, (arrived, wave), waits=sums.waits())
    wave, over = sums.advance((wave, over))
    over = to_chunks(over[:, :2].reshape(clips, nfft))
    at = late * clips * PAIRS * half // LANES
    mended = lax.dynamic_slice_in_dim(wave, at, over.shape[0]) + over
    waveform = from_chunks(lax.dynamic_update_slice_in_dim(wave, mended, at, 0), clips)

    first_total = sums.finish(first_total)
    head_grad, down_grad = sums.advance(
        run_order(
            first_order_kernel,
            first_total,
            [SDS((nfft + 2, width), F32), SDS((hidden, width), F32)],
            waits=sums.waits(),
        )
    )
    up_total = sums.finish(up_total)
    (up_grad,) = sums.advance(
        run_order(
            up_order_kernel,
            up_total,
            [SDS((width, hidden), F32)],
            [pltpu.VMEM((hidden, width), F32)],
            waits=sums.waits(),
        )
    )
    pack = sums.finish(small_total)
    small_shapes = [(KERNEL, width), (width,), scale_table.shape, scale_table.shape]
    small_shapes += [(width,), (width,), (nfft + 2,), (hidden,)]
    gcw, gcb, gscale, gshift, gls, gdb, ghb, gub = pl.pallas_call(
        unpack_kernel, out_shape=[SDS(shape, F32) for shape in small_shapes], name="unpack"
    )(pack)
    return (
        waveform,
        grad_inputs,
        gcw,
        gcb,
        gscale,
        gshift,
        up_grad,
        gub,
        down_grad,
        gdb,
        gls,
        head_grad.T,
        ghb,
    )


def solution(mesh):
    in_specs = (P("clip", "tm", None), P("clip"), P("clip")) + (P(),) * 11 + (P("clip", "tm"),)
    out_specs = (P("clip", "tm"), P("clip", "tm", None)) + (P(),) * 11
    return jax.shard_map(body, mesh=mesh, in_specs=in_specs, out_specs=out_specs, check_vma=False)
```

```python
import functools

import jax
import jax.numpy as jnp
import ml_dtypes
import numpy as np
from jax import lax
from jax.experimental import pallas as pl
from jax.experimental.pallas import tpu as pltpu
from jax.sharding import PartitionSpec as P

KERNEL = 7
CLASSES = ((1, 4), (2, 3), (0,))
F32 = jnp.float32
BF16 = jnp.bfloat16
LANES = 128
PAIRS = 128
ROWS = 2 * PAIRS
VMEM = 60 * 2**20
UP_PARTS = ((1024, 0), (512, 2))
HEAD_ROWS = 704
SDS = jax.ShapeDtypeStruct

SIN_POLY = (0.999999996, -0.166666580, 8.33305023e-03, -1.98090119e-04, 2.60507821e-06)
COS_POLY = (1.0, -0.499999994, 4.16666361e-02, -1.38883598e-03, 2.47600798e-05, -2.60500270e-07)

NN = (((1,), (0,)), ((), ()))
NT = (((1,), (1,)), ((), ()))


def split(x):
    high = x.astype(BF16)
    return high, (x - high.astype(F32)).astype(BF16)


def dot(a, b, dims=NN):
    return lax.dot_general(a, b, dims, preferred_element_type=F32)


def dot3(a, b, dims=NN):
    return dot(a[0], b[0], dims) + (dot(a[0], b[1], dims) + dot(a[1], b[0], dims))


def fold8(x):
    return jnp.sum(x.reshape(x.shape[0] // 8, 8, x.shape[1]), axis=0)


def np_split(x):
    high = x.astype(np.float32).astype(ml_dtypes.bfloat16)
    return high, (x - high.astype(np.float64)).astype(ml_dtypes.bfloat16)


@functools.lru_cache(None)
def tables(nfft):
    fifth, half, hop = nfft // 5, nfft // 2, nfft // 4
    bins = np.arange(1, half)
    first, second = (np.concatenate([bins[bins % 5 == r] for r in rs]) for rs in CLASSES[:2])
    zero = np.arange(0, half, 5)
    n0 = np.arange(fifth)

    def paired(ks, residue):
        sign = np.where(ks % 5 == residue, 1.0, -1.0)[:, None]
        turn = 2 * np.pi * ((sign * ks[:, None] * n0[None]) % nfft) / nfft
        weight = 2.0 / nfft
        real = np.concatenate([weight * np.cos(turn), weight * np.sin(turn)], 1)
        imag = np.concatenate([-sign * weight * np.sin(turn), sign * weight * np.cos(turn)], 1)
        return np.concatenate([real, imag], 0)

    turn = 2 * np.pi * ((zero[:, None] * n0[None]) % nfft) / nfft
    weight = np.where(zero == 0, 1.0, 2.0)[:, None] / nfft
    real, imag = weight * np.cos(turn), -weight * np.sin(turn)
    imag[0] = np.cos(np.pi * n0) / nfft
    transforms = [np_split(t) for t in (paired(first, 1), paired(second, 2), np.concatenate([real, imag], 0))]
    n = np.arange(nfft)
    window = 0.5 - 0.5 * np.cos(2 * np.pi * n / nfft)
    windows = np.stack([window, np.roll(window, hop)]).astype(np.float32)
    squares = np.cumsum((window**2).reshape(4, hop), axis=0)
    inverse = np.tile(1.0 / np.maximum(squares, 1.0), (1, 2)).astype(np.float32)
    turns = np.zeros(nfft)
    place = 0
    for ks in (first, second, zero):
        turns[place + len(ks) : place + 2 * len(ks)] = -(np.pi / 2) * (ks % 4)
        place += 2 * len(ks)
    return transforms, windows, inverse, turns.astype(np.float32)[None]


def class_places(nfft):
    length, places, at = nfft // 10, [], 0
    for residues in CLASSES:
        for offset in (0, nfft // 2 + 1):
            for r in residues:
                places.append((at, offset + r))
                at += length
    return places


def sin_cos(x):
    turns = jnp.round(x * np.float32(0.5 / np.pi))
    h = x * 0.5 - turns * np.float32(3.140625)
    h = h - turns * np.float32(9.67502593994140625e-4)
    h = h - turns * np.float32(1.509957990978376432e-7)
    z = h * h
    s = np.float32(SIN_POLY[-1])
    for c in SIN_POLY[-2::-1]:
        s = s * z + np.float32(c)
    s = s * h
    cosine = np.float32(COS_POLY[-1])
    for c in COS_POLY[-2::-1]:
        cosine = cosine * z + np.float32(c)
    twice = s + s
    return twice * cosine, 1.0 - twice * s


def fifths():
    a = 2 * np.pi / 5
    return [np.float32(v) for v in (np.cos(a), np.cos(2 * a), np.sin(a), np.sin(2 * a))]


def inverse_envelope(first_pair, offset, table_ref, tile, rows):
    lane = tile * LANES + lax.broadcasted_iota(jnp.int32, (rows, LANES), 1)
    row = lax.broadcasted_iota(jnp.int32, (rows, LANES), 0)
    half = table_ref.shape[1] // 2
    since = 2 * (first_pair + row) + (lane >= half).astype(jnp.int32) - offset
    value = jnp.where(since < 0, 1.0, 1.0)
    for i in range(4):
        value = jnp.where(since >= i, table_ref[i : i + 1, tile * LANES : (tile + 1) * LANES], value)
    return value


def head_kernel(
    bands,
    offsets,
    x_ref,
    x_up,
    x_down,
    edge_ref,
    cot_ref,
    cot_down,
    cot_edge,
    conv_w,
    conv_b,
    scale_t,
    shift_t,
    up_w,
    up_b,
    down_w,
    down_b,
    layer_scale,
    head_wt,
    head_b,
    turns,
    t1h,
    t1l,
    t2h,
    t2l,
    t0h,
    t0l,
    windows,
    inverse,
    o_norm,
    o_istd,
    o_adt_h,
    o_adt_l,
    o_slope,
    o_spec,
    o_gm,
    o_gb_h,
    o_gb_l,
    o_keep,
    o_send,
    o_small,
    up_h,
    up_l,
    down_h,
    down_l,
    head_h,
    head_l,
    head_bias,
    ext_w,
    head4,
    bias4,
    pad4,
    nrm4,
    istd1,
    gs5,
    gm4,
    gl_h,
    gl_l,
    act_h,
    act_l,
    acc_gdn,
    acc_ghw,
    acc_ghb,
    acc_ghwe,
    acc_ghbe,
    acc_gls,
    acc_gmb,
):
    clip, blk = pl.program_id(0), pl.program_id(1)
    clips, blks = pl.num_programs(0), pl.num_programs(1)
    width = x_ref.shape[2]
    frames = blks * ROWS
    tiles = width // LANES
    nfft = turns.shape[1]
    half = nfft // 2
    tm = lax.axis_index("tm")
    band = bands[clip]
    local = offsets[clip] - tm * frames
    rows8 = edge_ref.shape[1]
    places = class_places(nfft)

    @pl.when((clip == 0) & (blk == 0))
    def _():
        up_h[...], up_l[...] = split(up_w[...])
        down_h[...], down_l[...] = split(down_w[...])
        for t in range(tiles):
            head4[t, 0 : nfft + 2, :] = head_wt[:, t * LANES : (t + 1) * LANES]
        bias = head_b[...].reshape(1, nfft + 2)
        for c in range(0, nfft, LANES):
            bias4[c : c + LANES, :] = jnp.broadcast_to(bias[:, c : c + LANES], (LANES, LANES)).T
        for c in (nfft, nfft + 1):
            bias4[c : c + 1, :] = jnp.broadcast_to(bias[:, c : c + 1], (1, LANES))
        for at, first in places:
            rows = jnp.concatenate([head4[t, pl.ds(first, LANES, stride=5), :] for t in range(tiles)], 1)
            head_h[at : at + LANES, :], head_l[at : at + LANES, :] = split(rows)
            moved = bias4[pl.ds(first, LANES, stride=5), :].T[0:1, :]
            head_bias[0:1, at : at + LANES] = moved
            head_bias[1:2, at : at + LANES] = moved + turns[:, at : at + LANES]
        ext_w[0:1, :] = head_wt[half : half + 1, :]
        ext_w[1:2, :] = head_wt[nfft + 1 : nfft + 2, :]
        ext_w[2:8, :] = jnp.zeros((6, width), F32)
        for ref in (acc_gdn, acc_ghw, acc_ghb, acc_ghwe, acc_ghbe, acc_gls, acc_gmb):
            ref[...] = jnp.zeros_like(ref)

    base = pl.multiple_of(blk * ROWS, ROWS)

    def masked(value, first):
        row = first + lax.broadcasted_iota(jnp.int32, value.shape, 0)
        return jnp.where(row >= local, value, 0.0)

    before = masked(jnp.where(blk == 0, jnp.where(tm > 0, edge_ref[0], 0.0), x_up[0]), base - rows8)
    after = masked(jnp.where(blk == blks - 1, jnp.where(tm > 0, 0.0, edge_ref[0]), x_down[0]), base + ROWS)
    middle = masked(x_ref[0], base)
    for t in range(tiles):
        lanes = slice(t * LANES, (t + 1) * LANES)
        pad4[t, 0:rows8, :] = before[:, lanes]
        pad4[t, rows8 : rows8 + ROWS, :] = middle[:, lanes]
        pad4[t, rows8 + ROWS :, :] = after[:, lanes]
    bias = conv_b[...].reshape(1, width)
    chunk = 64
    for r in range(0, ROWS, chunk):
        parts = []
        for t in range(tiles):
            lanes = slice(t * LANES, (t + 1) * LANES)
            total = bias[:, lanes]
            for k in range(KERNEL):
                first = r + rows8 - KERNEL // 2 + k
                total = total + pad4[t, first : first + chunk, :] * conv_w[k : k + 1, lanes]
            parts.append(total)
        mean = jnp.sum(sum(parts[1:], parts[0]), axis=1, keepdims=True) * (1.0 / width)
        parts = [p - mean for p in parts]
        squares = [p * p for p in parts]
        variance = jnp.sum(sum(squares[1:], squares[0]), axis=1, keepdims=True) * (1.0 / width)
        istd = lax.rsqrt(variance + 1e-6)
        for t in range(tiles):
            nrm4[t, r : r + chunk, :] = parts[t] * istd
        istd1[r : r + chunk, :] = jnp.broadcast_to(istd, (chunk, LANES))

    def by_parity(ref, first):
        return jnp.concatenate(
            [
                jnp.concatenate([ref[t, pl.ds(first + par, PAIRS, stride=2), :] for t in range(tiles)], 1)
                for par in range(2)
            ],
            0,
        )

    normed = by_parity(nrm4, 0)
    o_norm[...] = normed
    for par in range(2):
        o_istd[par * PAIRS : (par + 1) * PAIRS, :] = istd1[pl.ds(par, PAIRS, stride=2), :]
    adapted = normed * scale_t[pl.ds(band, 1), :] + shift_t[pl.ds(band, 1), :]
    ad = split(adapted)
    o_adt_h[...], o_adt_l[...] = ad[0].T, ad[1].T

    first_pair = pl.multiple_of(blk * PAIRS, PAIRS)
    wave_tiles = gs5.shape[0]
    for t in range(wave_tiles):
        lanes = slice(t * LANES, (t + 1) * LANES)
        stride = clips * wave_tiles
        value = cot_ref[pl.ds(clips * t + clip, PAIRS, stride=stride), :]
        gs5[t, 0:PAIRS, :] = value * inverse_envelope(first_pair, local, inverse, t, PAIRS)
        value = cot_down[pl.ds(clips * t + clip, 8, stride=stride), :]
        value = jnp.where(blk == blks - 1, jnp.where(tm > 0, 0.0, cot_edge[0, :, lanes]), value)
        gs5[t, PAIRS : PAIRS + 8, :] = value * inverse_envelope(first_pair + PAIRS, local, inverse, t, 8)
    now, one, two = ([gs5[t, d : d + PAIRS, :] for t in range(wave_tiles)] for d in range(3))
    mid = wave_tiles // 2
    right = lax.broadcasted_iota(jnp.int32, (PAIRS, LANES), 1) >= LANES // 2
    odd = two[:mid] + [jnp.where(right, now[mid], two[mid])] + now[mid + 1 :] + one
    c1, c2, s1, s2 = fifths()
    folded = []
    for par, segment in enumerate((now + one, odd)):
        seg = [v * windows[par : par + 1, t * LANES : (t + 1) * LANES] for t, v in enumerate(segment)]
        v = [jnp.concatenate(seg[2 * j : 2 * j + 2], 1) for j in range(5)]
        p14, m41, p23, m32 = v[1] + v[4], v[4] - v[1], v[2] + v[3], v[3] - v[2]
        folded.append(
            (
                v[0] + p14 + p23,
                v[0] + c1 * p14 + c2 * p23,
                s1 * m41 + s2 * m32,
                v[0] + c2 * p14 + c1 * p23,
                s2 * m41 - s1 * m32,
            )
        )
    f0, fa, fb, fc, fd = (jnp.concatenate([e, o], 0) for e, o in zip(*folded))
    spectrum_grads = (
        dot3(split(jnp.concatenate([fa, fb], 1)), (t1h[...], t1l[...]), NT),
        dot3(split(jnp.concatenate([fc, fd], 1)), (t2h[...], t2l[...]), NT),
        dot3(split(f0), (t0h[...], t0l[...]), NT),
    )

    hidden = up_h.shape[1]
    step = 256
    up_bias = up_b[...].reshape(1, hidden)
    for j in range(hidden // step):
        cols = slice(j * step, (j + 1) * step)
        upward = dot3(ad, (up_h[:, cols], up_l[:, cols])) + up_bias[:, cols]
        cdf = 0.5 + 0.5 * lax.erf(upward * np.float32(0.7071067811865476))
        density = jnp.exp(upward * upward * -0.5) * np.float32(0.3989422804014327)
        o_slope[:, cols] = cdf + upward * density
        act_h[:, cols], act_l[:, cols] = split(upward * cdf)
    branch = dot3((act_h[...], act_l[...]), (down_h[...], down_l[...])) + down_b[...].reshape(1, width)
    scale = layer_scale[...].reshape(1, width)
    residual = by_parity(pad4, rows8) + scale * branch
    res = split(residual)
    res_t = res[0].T, res[1].T

    bias = head_b[...].reshape(1, nfft + 2)
    ext = split(ext_w[...])
    ext_logits = dot3(ext, res, NT)
    lane = lax.broadcasted_iota(jnp.int32, (1, ROWS), 1)
    ext_frame = base + jnp.where(lane < PAIRS, 2 * lane, 2 * (lane - PAIRS) + 1)
    ext_present = ext_frame >= local

    def magnitudes(logits, present):
        raw = jnp.where(present, jnp.exp(logits), 0.0)
        squashed = jnp.tanh(raw * np.float32(0.01))
        return 100.0 * squashed, raw * (1.0 - squashed * squashed)

    ext_mag, ext_slope = magnitudes(ext_logits[0:1] + bias[:, half : half + 1], ext_present)
    ext_sin, ext_cos = sin_cos(ext_logits[1:2] + bias[:, nfft + 1 : nfft + 2])
    ext_real = ext_mag * ext_cos
    ext_imag = ext_mag * ext_sin
    ext_real_col = jnp.concatenate([ext_real, jnp.zeros((7, ROWS), F32)], 0).T[:, 0:1]

    row = lax.broadcasted_iota(jnp.int32, (PAIRS, 1), 0)
    at = 0
    for index, grads in enumerate(spectrum_grads):
        n = grads.shape[1] // 2
        cols = slice(at, at + 2 * n)
        logits = dot3(res, (head_h[cols, :], head_l[cols, :]), NT)
        for par in range(2):
            rows = slice(par * PAIRS, (par + 1) * PAIRS)
            present = base + 2 * row + par >= local
            value = logits[rows] + head_bias[par : par + 1, cols]
            magnitude, slope = magnitudes(value[:, :n], present)
            sine, cosine = sin_cos(value[:, n:])
            real, imag = magnitude * cosine, magnitude * sine
            g_real, g_imag = grads[rows, :n], grads[rows, n:]
            if index == 2:
                corner = lax.broadcasted_iota(jnp.int32, (PAIRS, n), 1) == 0
                shown = jnp.where(corner, ext_real_col[rows], imag)
                g_imag = jnp.where(corner, 0.0, g_imag)
            else:
                shown = imag
            o_spec[rows, at : at + n] = real
            o_spec[rows, at + n : at + 2 * n] = shown
            g_mag = slope * (g_real * cosine + g_imag * sine)
            g_ang = g_imag * real - g_real * imag
            gl = jnp.concatenate([g_mag, g_ang], 1)
            acc_ghb[:, cols] += fold8(gl)
            gl_h[rows, cols], gl_l[rows, cols] = split(gl)
        at += 2 * n

    corner_t = spectrum_grads[2][:, spectrum_grads[2].shape[1] // 2 :].T
    ext_g = corner_t[0:1, :]
    ext_grads = jnp.concatenate(
        [ext_slope * ext_g * ext_cos, -ext_g * ext_imag, jnp.zeros((6, ROWS), F32)], 0
    )
    acc_ghbe[...] += ext_grads
    acc_ghwe[...] += dot3(split(ext_grads), res)
    gl = (gl_h[...], gl_l[...])
    ext_cols = ext_grads.T
    grad_mixed = (
        dot3(gl, (head_h[...], head_l[...]))
        + ext_cols[:, 0:1] * ext_w[0:1, :]
        + ext_cols[:, 1:2] * ext_w[1:2, :]
    )
    acc_ghw[...] += dot3(res_t, gl)
    acc_gls[...] += fold8(grad_mixed * branch)
    acc_gmb[...] += fold8(grad_mixed)
    for par in range(2):
        rows = slice(par * PAIRS, (par + 1) * PAIRS)
        for t in range(tiles):
            gm4[t, pl.ds(par, PAIRS, stride=2), :] = grad_mixed[rows, t * LANES : (t + 1) * LANES]
    for t in range(tiles):
        o_gm[:, t * LANES : (t + 1) * LANES] = gm4[t]
    grad_branch = grad_mixed * scale
    gb = split(grad_branch)
    o_gb_h[...], o_gb_l[...] = gb
    acc_gdn[...] += dot3((gb[0].T, gb[1].T), (act_h[...], act_l[...]))

    @pl.when((clip == clips - 1) & (blk == blks - 1))
    def _():
        total = jnp.sum(acc_ghb[...], axis=0, keepdims=True)
        for at, first in places:
            for t in range(tiles):
                block = acc_ghw[t * LANES : (t + 1) * LANES, at : at + LANES]
                head4[t, pl.ds(first, LANES, stride=5), :] = block.T
            block = jnp.broadcast_to(total[:, at : at + LANES], (LANES, LANES))
            bias4[pl.ds(first, LANES, stride=5), :] = block.T
        ext_sums = jnp.sum(acc_ghbe[...], axis=1, keepdims=True)
        for i, c in enumerate((half, nfft + 1)):
            for t in range(tiles):
                head4[t, c : c + 1, :] = acc_ghwe[i : i + 1, t * LANES : (t + 1) * LANES]
            bias4[c : c + 1, :] = jnp.broadcast_to(ext_sums[i : i + 1], (1, LANES))
        core = lax.axis_index("clip") % 2
        for here, first in ((core == 0, 0), (core == 1, half + 1)):

            @pl.when(here)
            def _(first=first):
                for t in range(tiles):
                    lanes = slice(t * LANES, (t + 1) * LANES)
                    for ref, at in ((o_keep, first), (o_send, half + 1 - first)):
                        ref[0 : half + 1, lanes] = head4[t, at : at + half + 1, :]
                        ref[half + 1 : HEAD_ROWS, lanes] = jnp.zeros((HEAD_ROWS - half - 1, LANES), F32)

        rows = hidden // 2
        for ref, part in ((o_keep, core), (o_send, 1 - core)):
            ref[HEAD_ROWS:, :] = acc_gdn[:, pl.ds(pl.multiple_of(part * rows, rows), rows)].T
        o_small[...] = jnp.zeros_like(o_small)
        for c in range(0, nfft, LANES):
            o_small[0:1, c : c + LANES] = bias4[c : c + LANES, :].T[0:1, :]
        o_small[0:1, nfft : nfft + 2] = jnp.concatenate(
            [bias4[nfft : nfft + 1, 0:1], bias4[nfft + 1 : nfft + 2, 0:1]], 1
        )
        o_small[1:2, :width] = jnp.sum(acc_gls[...], axis=0, keepdims=True)
        o_small[2:3, :width] = jnp.sum(acc_gmb[...], axis=0, keepdims=True) * scale


def whole(shape):
    return pl.BlockSpec(shape, lambda *_: (0,) * len(shape))


def fixed(shape):
    return pl.BlockSpec(shape, lambda *_: (0,) * len(shape), pipeline_mode=pl.Buffered(1))


def row_halves(blks, rows, rows8, width, clip=None):
    per, last = rows // rows8, blks * rows // rows8 - 1
    places = [
        (rows, lambda j: j),
        (rows8, lambda j: jnp.maximum(j * per - 1, 0)),
        (rows8, lambda j: jnp.minimum(j * per + per, last)),
    ]
    if clip is None:
        return [pl.BlockSpec((1, n, width), lambda i, j, *_, f=f: (i, f(j), 0)) for n, f in places]
    return [pl.BlockSpec((1, n, width), lambda j, *_, f=f: (clip, f(j), 0)) for n, f in places]


def run_head(bands, offsets, x, edge, cot, cot_edge, weights, turns, consts):
    clips, frames, width = x.shape
    blks = frames // ROWS
    count = clips * frames
    hidden = weights[4].shape[1]
    nfft = turns.shape[1]
    block = lambda i, j, *_: (i * blks + j, 0)
    column = lambda i, j, *_: (0, i * blks + j)
    per_clip = lambda shape: pl.BlockSpec((1,) + shape, lambda i, j, *_: (i, 0, 0))
    in_specs = row_halves(blks, ROWS, edge.shape[1], width)
    in_specs += [per_clip(edge.shape[1:])]
    operands = list(weights) + [turns] + list(consts)
    rows = cot.shape[0] // blks
    few = rows * 8 // PAIRS
    per, last = rows // few, cot.shape[0] // few - 1
    in_specs += [
        pl.BlockSpec((rows, LANES), lambda i, j, *_: (j, 0)),
        pl.BlockSpec((few, LANES), lambda i, j, *_: (jnp.minimum(j * per + per, last), 0)),
        per_clip(cot_edge.shape[1:]),
    ]
    in_specs += [fixed(v.shape) for v in operands]
    row_out = lambda n, dtype: (SDS((count, n), dtype), pl.BlockSpec((ROWS, n), block))
    col_out = (SDS((width, count), BF16), pl.BlockSpec((width, ROWS), column))
    outs = [
        row_out(width, F32),
        row_out(LANES, F32),
        col_out,
        col_out,
        row_out(hidden, F32),
        row_out(nfft, F32),
        row_out(width, F32),
        row_out(width, BF16),
        row_out(width, BF16),
        (SDS((HEAD_ROWS + hidden // 2, width), F32), fixed((HEAD_ROWS + hidden // 2, width))),
        (SDS((HEAD_ROWS + hidden // 2, width), F32), fixed((HEAD_ROWS + hidden // 2, width))),
        (SDS((8, hidden), F32), whole((8, hidden))),
    ]
    wave_tiles = nfft // 2 // LANES
    tiles = width // LANES
    scratch = [pltpu.VMEM((width, hidden), BF16)] * 2 + [pltpu.VMEM((hidden, width), BF16)] * 2
    scratch += [
        pltpu.VMEM((nfft, width), BF16),
        pltpu.VMEM((nfft, width), BF16),
        pltpu.VMEM((2, nfft), F32),
        pltpu.VMEM((8, width), F32),
        pltpu.VMEM((tiles, nfft + 8, LANES), F32),
        pltpu.VMEM((nfft + 8, LANES), F32),
        pltpu.VMEM((tiles, ROWS + 2 * edge.shape[1], LANES), F32),
        pltpu.VMEM((tiles, ROWS, LANES), F32),
        pltpu.VMEM((ROWS, LANES), F32),
        pltpu.VMEM((wave_tiles, PAIRS + 8, LANES), F32),
        pltpu.VMEM((tiles, ROWS, LANES), F32),
        pltpu.VMEM((ROWS, nfft), BF16),
        pltpu.VMEM((ROWS, nfft), BF16),
        pltpu.VMEM((ROWS, hidden), BF16),
        pltpu.VMEM((ROWS, hidden), BF16),
        pltpu.VMEM((width, hidden), F32),
        pltpu.VMEM((width, nfft), F32),
        pltpu.VMEM((8, nfft), F32),
        pltpu.VMEM((8, width), F32),
        pltpu.VMEM((8, ROWS), F32),
        pltpu.VMEM((8, width), F32),
        pltpu.VMEM((8, width), F32),
    ]
    return pl.pallas_call(
        head_kernel,
        grid_spec=pltpu.PrefetchScalarGridSpec(
            num_scalar_prefetch=2,
            grid=(clips, blks),
            in_specs=in_specs,
            out_specs=[s for _, s in outs],
            scratch_shapes=scratch,
        ),
        out_shape=[s for s, _ in outs],
        compiler_params=pltpu.CompilerParams(vmem_limit_bytes=VMEM),
        cost_estimate=pl.CostEstimate(flops=80_000_000_000, bytes_accessed=90_000_000, transcendentals=0),
        name="head",
    )(bands, offsets, x, x, x, edge, cot, cot, cot_edge, *operands)


def up_kernel(gb_h, gb_l, slope, adt_h, adt_l, down_w, *refs):
    o_keep, o_send, o_gub, o_gu_h, o_gu_l, dw_h, dw_l, acc, acc_gub = refs[-9:]
    step = pl.program_id(0)
    hidden = slope.shape[1]

    @pl.when(step == 0)
    def _():
        dw_h[...], dw_l[...] = split(down_w[...])
        acc[...] = jnp.zeros_like(acc)
        acc_gub[...] = jnp.zeros_like(acc_gub)

    cols = 512
    for j in range(hidden // cols):
        part = slice(j * cols, (j + 1) * cols)
        gu = dot3((gb_h[...], gb_l[...]), (dw_h[part, :], dw_l[part, :]), NT) * slope[:, part]
        acc_gub[:, part] += fold8(gu)
        gs = split(gu)
        o_gu_h[:, part], o_gu_l[:, part] = gs
        acc[:, part] += dot3((adt_h[...], adt_l[...]), gs)

    @pl.when(step == pl.num_programs(0) - 1)
    def _():
        o_gub[...] = jnp.sum(acc_gub[...], axis=0, keepdims=True)
        core = lax.axis_index("clip") % 2
        rows = o_keep.shape[0]
        for ref, half in ((o_keep, core), (o_send, 1 - core)):
            ref[...] = acc[:, pl.ds(pl.multiple_of(half * rows, rows), rows)].T


def after(values, operand):
    return lax.optimization_barrier((operand, tuple(values)))[0] if values else operand


def run_up(gb, slope, adt, down_w, size, part, so_far, waits=()):
    count, width = gb[0].shape
    hidden = slope.shape[1]
    rows = 512
    row = lambda i: (i, 0)
    in_specs = [pl.BlockSpec((rows, width), row)] * 2 + [pl.BlockSpec((rows, size), lambda i: (i, part))]
    in_specs += [pl.BlockSpec((width, rows), lambda i: (0, i))] * 2
    in_specs += [pl.BlockSpec((size, width), lambda i: (part, 0), pipeline_mode=pl.Buffered(1))]
    so_far = list(so_far)
    return pl.pallas_call(
        up_kernel,
        grid=(count // rows,),
        in_specs=in_specs + [pl.BlockSpec(memory_space=pl.ANY)] * len(so_far),
        out_specs=[pl.BlockSpec((size // 2, width), lambda i: (part, 0))] * 2
        + [whole((1, size)), pl.BlockSpec((rows, size), row), pl.BlockSpec((rows, size), row)],
        out_shape=[
            SDS((hidden // 2, width), F32),
            SDS((hidden // 2, width), F32),
            SDS((1, size), F32),
            SDS((count, size), BF16),
            SDS((count, size), BF16),
        ],
        input_output_aliases={6 + i: i for i in range(len(so_far))},
        scratch_shapes=[pltpu.VMEM((size, width), BF16)] * 2
        + [pltpu.VMEM((width, size), F32), pltpu.VMEM((8, size), F32)],
        compiler_params=pltpu.CompilerParams(vmem_limit_bytes=VMEM),
        cost_estimate=pl.CostEstimate(flops=10_000_000_000, bytes_accessed=20_000_000, transcendentals=0),
        name="up_grads",
    )(*gb, after(waits, slope), *adt, down_w, *so_far)


def norm_kernel(sizes, clip, bands, *refs):
    gu = refs[: 2 * len(sizes)]
    up_w, norm, istd, scale_t = refs[2 * len(sizes) : 2 * len(sizes) + 4]
    edge_in = refs[2 * len(sizes) + 4] if clip else None
    o_gh, o_edge, o_scale, o_shift, up_h, up_l, nat4, acc_scale, acc_shift = refs[-9:]
    blk, blks = pl.program_id(0), pl.num_programs(0)
    band = bands[clip]
    width = norm.shape[1]
    tiles = width // LANES

    @pl.when(blk == 0)
    def _():
        up_h[...], up_l[...] = split(up_w[...])
        for ref in (o_scale, o_shift, acc_scale, acc_shift):
            ref[...] = jnp.zeros_like(ref)
        if edge_in is not None:
            o_edge[...] = edge_in[...]

    ga, at = None, 0
    for j, hidden in enumerate(sizes):
        cols = slice(at, at + hidden)
        term = dot3((gu[2 * j][...], gu[2 * j + 1][...]), (up_h[:, cols], up_l[:, cols]), NT)
        ga = term if ga is None else ga + term
        at += hidden
    normed = norm[...]
    acc_scale[...] += fold8(ga * normed)
    acc_shift[...] += fold8(ga)
    gn = ga * scale_t[pl.ds(band, 1), :]
    mean = jnp.sum(gn, axis=1, keepdims=True) * (1.0 / width)
    along = jnp.sum(gn * normed, axis=1, keepdims=True) * (1.0 / width)
    gh = istd[:, 0:1] * (gn - mean - normed * along)
    for par in range(2):
        for t in range(tiles):
            nat4[t, pl.ds(par, PAIRS, stride=2), :] = gh[par * PAIRS : (par + 1) * PAIRS, t * LANES : (t + 1) * LANES]
    for t in range(tiles):
        o_gh[:, t * LANES : (t + 1) * LANES] = nat4[t]
    tm = lax.axis_index("tm")
    for here, first in (((tm == 0) & (blk == blks - 1), ROWS - 8), ((tm == 1) & (blk == 0), 0)):

        @pl.when(here)
        def _(first=first):
            for t in range(tiles):
                o_edge[clip, :, t * LANES : (t + 1) * LANES] = nat4[t, first : first + 8, :]

    @pl.when(blk == blks - 1)
    def _():
        o_scale[pl.ds(band, 1), :] = jnp.sum(acc_scale[...], axis=0, keepdims=True)
        o_shift[pl.ds(band, 1), :] = jnp.sum(acc_shift[...], axis=0, keepdims=True)


def run_norm(bands, gus, up_w, norm, istd, scale_t, edge, clip, waits=()):
    clips = edge.shape[0]
    earlier = [edge] if clip else []
    count, width = norm.shape
    blks = count // clips // ROWS
    block = lambda j, *_: (clip * blks + j, 0)
    flat = [v for pair in gus for v in pair]
    in_specs = [pl.BlockSpec((ROWS, v.shape[1]), block) for v in flat]
    in_specs += [fixed(up_w.shape), pl.BlockSpec((ROWS, width), block)]
    in_specs += [pl.BlockSpec((ROWS, LANES), block), fixed(scale_t.shape)]
    in_specs += [fixed(v.shape) for v in earlier]
    return pl.pallas_call(
        functools.partial(norm_kernel, [pair[0].shape[1] for pair in gus], clip),
        grid_spec=pltpu.PrefetchScalarGridSpec(
            num_scalar_prefetch=1,
            grid=(blks,),
            in_specs=in_specs,
            out_specs=[pl.BlockSpec((ROWS, width), lambda j, *_: (j, 0)), whole(edge.shape)] + [whole(scale_t.shape)] * 2,
            scratch_shapes=[pltpu.VMEM(up_w.shape, BF16)] * 2
            + [pltpu.VMEM((width // LANES, ROWS, LANES), F32)]
            + [pltpu.VMEM((8, width), F32)] * 2,
        ),
        out_shape=[SDS((count // clips, width), F32), SDS(edge.shape, F32)] + [SDS(scale_t.shape, F32)] * 2,
        compiler_params=pltpu.CompilerParams(vmem_limit_bytes=VMEM),
        cost_estimate=pl.CostEstimate(flops=5_000_000_000, bytes_accessed=12_000_000, transcendentals=0),
        name="norm_grads",
    )(bands, *flat, up_w, after(waits, norm), istd, scale_t, *earlier)


def conv_kernel(
    clip, offsets, x_ref, x_up, x_down, edge_ref, gh_ref, gh_up, gh_down, gh_edge, gm_ref, conv_w, *refs
):
    o_gi, o_acc, pad4, gh4 = refs[-4:]
    blk, blks = pl.program_id(0), pl.num_programs(0)
    rows, width = x_ref.shape[1], x_ref.shape[2]
    tiles = width // LANES
    tm = lax.axis_index("tm")
    local = offsets[clip] - tm * blks * rows
    rows8 = edge_ref.shape[1]
    base = blk * rows

    @pl.when(blk == 0)
    def _():
        o_acc[...] = refs[0][...] if clip else jnp.zeros_like(o_acc)

    def masked(value, first):
        row = first + lax.broadcasted_iota(jnp.int32, value.shape, 0)
        return jnp.where(row >= local, value, 0.0)

    def above(edge, up):
        return jnp.where(blk == 0, jnp.where(tm > 0, edge[0], 0.0), up[0])

    def below(edge, down):
        return jnp.where(blk == blks - 1, jnp.where(tm > 0, 0.0, edge[0]), down[0])

    before, after = masked(above(edge_ref, x_up), base - rows8), masked(below(edge_ref, x_down), base + rows)
    g_before, g_after = above(gh_edge, gh_up), below(gh_edge, gh_down)
    middle = masked(x_ref[0], base)
    for t in range(tiles):
        lanes = slice(t * LANES, (t + 1) * LANES)
        pad4[t, 0:rows8, :] = before[:, lanes]
        pad4[t, rows8 : rows8 + rows, :] = middle[:, lanes]
        pad4[t, rows8 + rows :, :] = after[:, lanes]
        gh4[t, 0:rows8, :] = g_before[:, lanes]
        gh4[t, rows8 : rows8 + rows, :] = gh_ref[0, :, lanes]
        gh4[t, rows8 + rows :, :] = g_after[:, lanes]
    chunk = 64
    for r in range(0, rows, chunk):
        shown = base + r + lax.broadcasted_iota(jnp.int32, (chunk, LANES), 0) >= local
        for t in range(tiles):
            lanes = slice(t * LANES, (t + 1) * LANES)
            gh = gh4[t, rows8 + r : rows8 + r + chunk, :]
            o_acc[8 * KERNEL :, lanes] += fold8(gh)
            total = gm_ref[0, r : r + chunk, lanes]
            for k in range(KERNEL):
                first = r + rows8 + KERNEL // 2 - k
                total = total + conv_w[k : k + 1, lanes] * gh4[t, first : first + chunk, :]
                first = r + rows8 - KERNEL // 2 + k
                o_acc[8 * k : 8 * k + 8, lanes] += fold8(gh * pad4[t, first : first + chunk, :])
            o_gi[0, r : r + chunk, lanes] = jnp.where(shown, total, 0.0)


def run_conv(offsets, x, edge, gh, gh_edge, gm, conv_w, clip, so_far, waits=()):
    clips, frames, width = x.shape
    blks = frames // ROWS
    rows8 = edge.shape[1]
    mine = pl.BlockSpec((1, rows8, width), lambda j, *_: (clip, 0, 0))
    padded = pltpu.VMEM((width // LANES, ROWS + 2 * rows8, LANES), F32)
    blocks = row_halves(blks, ROWS, rows8, width, clip)
    in_specs = blocks + [mine] + row_halves(blks, ROWS, rows8, width, 0) + [mine] + blocks[:1]
    in_specs += [fixed(conv_w.shape)]
    operands = [x, x, x, edge, gh, gh, gh, gh_edge, after(waits, gm), conv_w]
    aliases = {}
    sums = (8 * (KERNEL + 1), width)
    if so_far:
        grads, acc = so_far
        operands.append(acc)
        in_specs.append(fixed(acc.shape))
        aliases = {1 + len(operands): 0}
        operands.append(grads)
        in_specs.append(pl.BlockSpec(memory_space=pl.ANY))
    return pl.pallas_call(
        functools.partial(conv_kernel, clip),
        grid_spec=pltpu.PrefetchScalarGridSpec(
            num_scalar_prefetch=1,
            grid=(blks,),
            in_specs=in_specs,
            out_specs=[blocks[0], whole(sums)],
            scratch_shapes=[padded, padded],
        ),
        out_shape=[SDS(x.shape, F32), SDS(sums, F32)],
        input_output_aliases=aliases,
        compiler_params=pltpu.CompilerParams(vmem_limit_bytes=VMEM),
        cost_estimate=pl.CostEstimate(flops=5_000_000_000, bytes_accessed=17_000_000, transcendentals=0),
        name="conv_grads",
    )(offsets, *operands)


def pack_kernel(acc, small, scales0, scales1, shifts0, shifts1, *refs):
    gubs, o_pack = refs[:-1], refs[-1]
    width = acc.shape[1]
    for k in range(KERNEL + 1):
        o_pack[k : k + 1, :] = jnp.sum(acc[8 * k : 8 * k + 8, :], axis=0, keepdims=True)
    o_pack[8:12, :] = scales0[...] + scales1[...]
    o_pack[12:16, :] = shifts0[...] + shifts1[...]
    o_pack[16:18, :] = small[1:3, :width]
    for i in range(3):
        o_pack[18 + i : 19 + i, :] = small[0:1, i * width : (i + 1) * width]
        gub = jnp.concatenate([v[...] for v in gubs], 1)
        o_pack[21 + i : 22 + i, :] = gub[:, i * width : (i + 1) * width]
    o_pack[24:, :] = jnp.zeros((o_pack.shape[0] - 24, width), F32)


def wave_kernel(
    first_blk, frames, scaled, offsets, spec, t1h, t1l, t2h, t2l, t0h, t0l, windows, inverse, *refs
):
    o_wave, o_tail, accs = refs[-3:]
    blk, clip = pl.program_id(0), pl.program_id(1)
    blks, clips = pl.num_programs(0), pl.num_programs(1)
    tiles = accs.shape[1]
    first = (first_blk + blk) * PAIRS
    local = offsets[clip] - lax.axis_index("tm") * frames
    acc5 = accs.at[clip]

    @pl.when(blk == 0)
    def _():
        for t in range(tiles):
            lanes = slice(t * LANES, (t + 1) * LANES)
            acc5[t, 0:8, :] = refs[0][0, :, lanes] if scaled else jnp.zeros((8, LANES), F32)

    @pl.when(blk > 0)
    def _():
        for t in range(tiles):
            acc5[t, 0:8, :] = acc5[t, PAIRS : PAIRS + 8, :]

    for t in range(tiles):
        acc5[t, 8:, :] = jnp.zeros((PAIRS, LANES), F32)

    n1, n2 = t1h.shape[0], t2h.shape[0]
    ab = dot3(split(spec[:, :n1]), (t1h[...], t1l[...]))
    cd = dot3(split(spec[:, n1 : n1 + n2]), (t2h[...], t2l[...]))
    p0 = dot3(split(spec[:, n1 + n2 :]), (t0h[...], t0l[...]))
    c1, c2, s1, s2 = fifths()
    sides = []
    for par in range(2):
        rows = slice(par * PAIRS, (par + 1) * PAIRS)
        w = p0.shape[1]
        a, b, c, d, p = ab[rows, :w], ab[rows, w:], cd[rows, :w], cd[rows, w:], p0[rows]
        e1, o1 = p + c1 * a + c2 * c, s1 * b + s2 * d
        e2, o2 = p + c2 * a + c1 * c, s2 * b - s1 * d
        v = [p + a + c, e1 - o1, e2 - o2, e2 + o2, e1 + o1]
        seg = []
        for t in range(2 * tiles):
            part = v[t // 2][:, (t % 2) * LANES : (t % 2 + 1) * LANES]
            seg.append(part * windows[par : par + 1, t * LANES : (t + 1) * LANES])
        sides.append(seg)
    even, odd = sides
    mid = tiles // 2
    right = lax.broadcasted_iota(jnp.int32, (PAIRS, LANES), 1) >= LANES // 2
    for t in range(tiles):
        here = even[t]
        if t > mid:
            here = here + odd[t]
        if t == mid:
            here = here + jnp.where(right, odd[t], 0.0)
        acc5[t, 0:PAIRS, :] += here
        acc5[t, 1 : PAIRS + 1, :] += even[tiles + t] + odd[tiles + t]
        if t < mid:
            acc5[t, 2 : PAIRS + 2, :] += odd[t]
        if t == mid:
            acc5[t, 2 : PAIRS + 2, :] += jnp.where(right, 0.0, odd[t])
        value = acc5[t, 0:PAIRS, :] * inverse_envelope(first, local, inverse, t, PAIRS)
        o_wave[pl.ds(clips * t + clip, PAIRS, stride=clips * tiles), :] = value

    @pl.when(blk == blks - 1)
    def _():
        for t in range(tiles):
            value = acc5[t, PAIRS : PAIRS + 8, :]
            if scaled:
                value = value * inverse_envelope(first + PAIRS, local, inverse, t, 8)
            o_tail[0, :, t * LANES : (t + 1) * LANES] = value


def run_wave(offsets, spec, consts, clips, first_blk, blks, earlier=(), waits=()):
    count, nfft = spec.shape
    all_blks = count // clips // ROWS
    tiles = nfft // 2 // LANES
    rows = clips * PAIRS * tiles
    in_specs = [pl.BlockSpec((ROWS, nfft), lambda j, i, *_: (i * all_blks + first_blk + j, 0))]
    in_specs += [fixed(v.shape) for v in consts]
    operands = [after(waits, spec), *consts]
    aliases = {}
    if earlier:
        carry, wave = earlier
        operands.append(carry)
        in_specs.append(pl.BlockSpec((1, 8, nfft // 2), lambda j, i, *_: (i, 0, 0)))
        aliases = {1 + len(operands): 0}
        operands.append(wave)
        in_specs.append(pl.BlockSpec(memory_space=pl.ANY))
    return pl.pallas_call(
        functools.partial(wave_kernel, first_blk, count // clips, first_blk == 0),
        grid_spec=pltpu.PrefetchScalarGridSpec(
            num_scalar_prefetch=1,
            grid=(blks, clips),
            in_specs=in_specs,
            out_specs=[
                pl.BlockSpec((rows, LANES), lambda j, i, *_: (first_blk + j, 0)),
                pl.BlockSpec((1, 8, nfft // 2), lambda j, i, *_: (i, 0, 0)),
            ],
            scratch_shapes=[pltpu.VMEM((clips, tiles, PAIRS + 8, LANES), F32)],
        ),
        out_shape=[SDS((rows * all_blks, LANES), F32), SDS((clips, 8, nfft // 2), F32)],
        input_output_aliases=aliases,
        compiler_params=pltpu.CompilerParams(vmem_limit_bytes=VMEM),
        cost_estimate=pl.CostEstimate(flops=5_000_000_000, bytes_accessed=8_000_000, transcendentals=0),
        name="wave",
    )(offsets, *operands)


def levels():
    clip = [("clip", 1 << i) for i in range((lax.axis_size("clip") - 1).bit_length())]
    tm = [("tm", 1 << i) for i in range((lax.axis_size("tm") - 1).bit_length())]
    return clip[:1] + clip[1:2] + tm + clip[2:]


def exchange(value, level):
    if level == "next":
        return lax.ppermute(value, "tm", [(i, i + 1) for i in range(lax.axis_size("tm") - 1)])
    across = {"clip": 0, "tm": 0}
    for axis, distance in level if isinstance(level, list) else [level]:
        across[axis] += distance
    if not across["tm"]:
        return lax.ppermute(value, "clip", [(i, i ^ across["clip"]) for i in range(lax.axis_size("clip"))])
    if not across["clip"]:
        return lax.ppermute(value, "tm", [(i, i ^ across["tm"]) for i in range(lax.axis_size("tm"))])
    n, m = lax.axis_size("clip"), lax.axis_size("tm")
    pairs = [(i * m + j, (i ^ across["clip"]) * m + (j ^ across["tm"])) for i in range(n) for j in range(m)]
    return lax.ppermute(value, ("clip", "tm"), pairs)


def side(level):
    axis, distance = level
    return lax.axis_index(axis) // distance % 2


class Sums:
    def __init__(self):
        self.running = []

    def add(self, steps, holds=()):
        entry = {"steps": steps, "holds": holds, "count": 0, "sent": None, "came": None, "left": 0, "sum": None}
        self.step(entry, None)
        self.running.append(entry)
        return entry

    def step(self, entry, values):
        try:
            entry["sent"] = entry["steps"].send(values)
            while entry["sent"][0][1] == levels()[0]:
                entry["sent"] = entry["steps"].send([exchange(*pair) for pair in entry["sent"]])
        except StopIteration as stop:
            entry["sent"], entry["sum"] = None, stop.value

    def waits(self):
        sent = []
        for entry in self.running:
            if entry["came"] is None and entry["sent"] is not None:
                entry["came"] = [exchange(*pair) for pair in entry["sent"]]
                entry["left"] = dict(entry["holds"]).get(entry["count"], 1)
                entry["count"] += 1
                sent += [pair[0] for pair in entry["sent"]]
        return sent

    def advance(self, results):
        done = []
        for entry in self.running:
            if entry["came"] is not None:
                entry["left"] -= 1
                if entry["left"] <= 0:
                    done.append(entry)
        if done:
            came, results = lax.optimization_barrier(([entry["came"] for entry in done], results))
            for entry, values in zip(done, came):
                entry["came"] = None
                self.step(entry, values)
        return results

    def finish(self, entry):
        while entry["sum"] is None:
            self.waits()
            self.advance(())
        return entry["sum"]


def halves_steps(keep, send, narrow):
    core, one, two, *last = levels()
    orders = ((one, two), (two, one))
    (came,) = yield [(send, core)]
    cols = keep.shape[1] // 2
    parts = [[(v, 0, c) for v in (keep, came)] for c in (0, cols)]

    def cut(terms, first):
        return [(v, row + first, col) for v, row, col in terms]

    def added(terms, rows):
        return sum(lax.dynamic_slice(v, (row, col), (rows, cols)) for v, row, col in terms)

    rows = keep.shape[0]
    for i in range(2):
        rows //= 2
        sides = [side(order[i]) for order in orders]
        came = yield [(added(cut(t, (1 - s) * rows), rows), o[i]) for t, s, o in zip(parts, sides, orders)]
        parts = [cut(t, s * rows) + [(c, 0, 0)] for t, s, c in zip(parts, sides, came)]
    value = jnp.concatenate([added(t, rows) for t in parts])
    halved = last if narrow and rows % (4 << len(last)) == 0 else []
    n, terms = value.shape[0], [(value, 0, 0)]
    for level in halved:
        n, s = n // 2, side(level)
        (came,) = yield [(added(cut(terms, (1 - s) * n), n), level)]
        terms = cut(terms, s * n) + [(came, 0, 0)]
    value = added(terms, n) if halved else value
    for level in last[len(halved) :]:
        (came,) = yield [(value, level)]
        value = value + came
    for level in halved[::-1]:
        s = side(level)
        (came,) = yield [(value, level)]
        value = jnp.concatenate([jnp.where(s == 0, value, came), jnp.where(s == 0, came, value)])
    parts = [value[:rows], value[rows:]]
    came = yield [(part, order[1]) for part, order in zip(parts, orders)]
    parts = [jnp.concatenate(pair) for pair in zip(parts, came)]
    came = yield [(part, order[0]) for part, order in zip(parts, orders)]
    parts, came = lax.optimization_barrier((parts, came))
    parts = [piece for pair in zip(parts, came) for piece in pair]
    others = yield [(part, core) for part in parts]
    return parts, others, orders


def whole_steps(value):
    core, *rest = levels()
    (came,) = yield [(value, core)]
    value = value + came
    for pair in [rest[:1]] + [rest[i : i + 2] for i in range(1, len(rest), 2)]:
        came = yield [(value, [level]) for level in pair] + ([(value, pair)] if len(pair) == 2 else [])
        for other in came:
            value = value + other
    return value


def one_step(value, level):
    (came,) = yield [(value, level)]
    return came


def natural_blocks(orders, refs, copy):
    core = side(levels()[0])
    cols = refs[0].shape[1]
    rows = refs[0].shape[0] // 2
    for half in range(2):
        for here, four in ((core == half, refs[:4]), (core != half, refs[4:])):
            for i, order in enumerate(orders):
                a, b = (side(level) for level in order)
                for top in range(2):
                    for piece in range(2):

                        @pl.when(here & (jnp.bitwise_xor(top, a) == piece))
                        def _(ref=four[2 * i + piece], half=half, i=i, top=top, b=b):
                            for low in range(2):
                                first = pl.multiple_of(jnp.bitwise_xor(low, b) * rows, 8)
                                value = ref[pl.ds(first, rows), :]
                                copy(half, slice(i * cols, (i + 1) * cols), (2 * top + low) * rows, value)


def to_runs(runs):
    def copy(half, cols, first, value):
        for start, out, place, rows in runs:
            low, high = max(first, start), min(first + value.shape[0], start + rows)
            if low < high:
                at = place(half) + low - start
                out[at : at + high - low, cols] = value[low - first : high - first]

    return copy


def first_order_kernel(orders, *refs):
    o_head, o_down = refs[-2:]
    copy = to_runs(
        (
            (0, o_head, lambda half: half * (o_head.shape[0] // 2), o_head.shape[0] // 2),
            (HEAD_ROWS, o_down, lambda half: half * (o_down.shape[0] // 2), o_down.shape[0] // 2),
        )
    )
    natural_blocks(orders, refs[:8], copy)


def up_order_kernel(orders, *refs):
    o_up, up_t = refs[-2:]

    runs, at = [], 0
    for size, part in UP_PARTS:
        runs.append((at, up_t, lambda half, size=size, part=part: size * part + half * (size // 2), size // 2))
        at += size // 2
    copy = to_runs(runs)
    natural_blocks(orders, refs[:8], copy)
    for c in range(0, up_t.shape[0], LANES):
        o_up[:, c : c + LANES] = up_t[c : c + LANES, :].T


def run_order(kernel, total, out_shape, scratch=(), waits=()):
    parts, others, orders = total
    parts = after(waits, parts)
    return pl.pallas_call(
        functools.partial(kernel, orders),
        in_specs=[pl.BlockSpec(memory_space=pltpu.VMEM)] * 8,
        out_shape=out_shape,
        scratch_shapes=list(scratch),
        compiler_params=pltpu.CompilerParams(vmem_limit_bytes=VMEM),
        name="in_order",
    )(*parts, *others)


def unpack_kernel(pack, gcw, gcb, gscale, gshift, gls, gdb, ghb, gub):
    width = pack.shape[1]
    gcw[...] = pack[0:KERNEL, :]
    gcb[...] = pack[KERNEL : KERNEL + 1, :].reshape(width)
    gscale[...] = pack[8:12, :]
    gshift[...] = pack[12:16, :]
    gls[...] = pack[16:17, :].reshape(width)
    gdb[...] = pack[17:18, :].reshape(width)
    rows = [pack[18 + i : 19 + i, :] for i in range(6)]
    ghb[...] = jnp.concatenate(rows[:3], 1)[:, : ghb.shape[0]].reshape(ghb.shape[0])
    gub[...] = jnp.concatenate(rows[3:], 1).reshape(gub.shape[0])


def edges(value, index):
    n = value.shape[1]
    return jnp.where(index == 0, value[:, n - 8 :], value[:, :8])


def to_chunks(wave):
    clips, samples = wave.shape
    return wave.reshape(clips, samples // LANES, LANES).transpose(1, 0, 2).reshape(-1, LANES)


def from_chunks(chunks, clips):
    rows = chunks.shape[0] // clips
    return chunks.reshape(rows, clips, LANES).transpose(1, 0, 2).reshape(clips, rows * LANES)


def body(
    inputs,
    band_ids,
    offsets,
    conv_weight,
    conv_bias,
    scale_table,
    shift_table,
    up_weight,
    up_bias,
    down_weight,
    down_bias,
    layer_scale,
    head_weight,
    head_bias,
    wave_cotangent,
):
    clips, frames, width = inputs.shape
    assert lax.axis_size("tm") == 2
    nfft = head_weight.shape[1] - 2
    half = nfft // 2
    hidden = up_weight.shape[1]
    tm = lax.axis_index("tm")
    core = lax.axis_index("clip") % 2
    swap = lambda v: lax.ppermute(v, "tm", [(0, 1), (1, 0)])
    transforms, windows, inverse, turns = tables(nfft)
    dft = [jnp.asarray(v) for pair in transforms for v in pair]
    consts = dft + [jnp.asarray(windows), jnp.asarray(inverse)]

    edge = swap(edges(inputs, tm))
    cot_edge = swap(jnp.pad(wave_cotangent[:, :nfft].reshape(clips, 2, half), ((0, 0), (0, 6), (0, 0))))
    weights = (
        conv_weight,
        conv_bias,
        scale_table,
        shift_table,
        up_weight,
        up_bias,
        down_weight,
        down_bias,
        layer_scale,
        head_weight.T,
        head_bias,
    )
    (
        norm, istd, adt_h, adt_l, slope, spec, gm, gb_h, gb_l, keep, send, small,
    ) = run_head(
        band_ids, offsets, inputs, edge, to_chunks(wave_cotangent), cot_edge, weights, jnp.asarray(turns), consts
    )

    sums = Sums()
    first_total = sums.add(halves_steps(keep, send, True))
    blks = frames // ROWS
    gus, gubs, halves = [], [], ()
    for size, part in UP_PARTS:
        results = run_up((gb_h, gb_l), slope, (adt_h, adt_l), down_weight, size, part, halves, waits=sums.waits())
        *halves, gub, gu_h, gu_l = sums.advance(results)
        gus.append((gu_h, gu_l))
        gubs.append(gub)
    up_total = sums.add(halves_steps(*halves, False), {3: 2})
    normed, gh_edge = [], edge
    for clip in range(clips):
        results = run_norm(band_ids, gus, up_weight, norm, istd, scale_table, gh_edge, clip, waits=sums.waits())
        gh_edge = results[1]
        normed.append(sums.advance(results))
    gh = [v[0][None] for v in normed]
    gh_edge = sums.add(one_step(normed[-1][1], ("tm", 1)))
    late = blks // 2
    wave, tail = run_wave(offsets, spec, consts, clips, late, blks - late, waits=sums.waits())
    wave, tail = sums.advance((wave, tail))
    arrived = sums.add(one_step(tail, "next"))
    gh_edge = sums.finish(gh_edge)
    so_far = ()
    gm = gm.reshape(clips, frames, width)
    for clip in range(clips):
        so_far = run_conv(
            offsets, inputs, edge, gh[clip], gh_edge, gm, conv_weight, clip, so_far, waits=sums.waits()
        )
        so_far = sums.advance(so_far)
    grad_inputs, acc = so_far
    pack = pl.pallas_call(pack_kernel, out_shape=SDS((32, width), F32), name="pack")(
        acc, small, *[v[2] for v in normed], *[v[3] for v in normed], *gubs
    )
    small_total = sums.add(whole_steps(pack))

    arrived = sums.finish(arrived)
    wave, over = run_wave(offsets, spec, consts, clips, 0, late, (arrived, wave), waits=sums.waits())
    wave, over = sums.advance((wave, over))
    over = to_chunks(over[:, :2].reshape(clips, nfft))
    at = late * clips * PAIRS * half // LANES
    mended = lax.dynamic_slice_in_dim(wave, at, over.shape[0]) + over
    waveform = from_chunks(lax.dynamic_update_slice_in_dim(wave, mended, at, 0), clips)

    first_total = sums.finish(first_total)
    head_grad, down_grad = sums.advance(
        run_order(
            first_order_kernel,
            first_total,
            [SDS((nfft + 2, width), F32), SDS((hidden, width), F32)],
            waits=sums.waits(),
        )
    )
    up_total = sums.finish(up_total)
    (up_grad,) = sums.advance(
        run_order(
            up_order_kernel,
            up_total,
            [SDS((width, hidden), F32)],
            [pltpu.VMEM((hidden, width), F32)],
            waits=sums.waits(),
        )
    )
    pack = sums.finish(small_total)
    small_shapes = [(KERNEL, width), (width,), scale_table.shape, scale_table.shape]
    small_shapes += [(width,), (width,), (nfft + 2,), (hidden,)]
    gcw, gcb, gscale, gshift, gls, gdb, ghb, gub = pl.pallas_call(
        unpack_kernel, out_shape=[SDS(shape, F32) for shape in small_shapes], name="unpack"
    )(pack)
    return (
        waveform,
        grad_inputs,
        gcw,
        gcb,
        gscale,
        gshift,
        up_grad,
        gub,
        down_grad,
        gdb,
        gls,
        head_grad.T,
        ghb,
    )


def solution(mesh):
    in_specs = (P("clip", "tm", None), P("clip"), P("clip")) + (P(),) * 11 + (P("clip", "tm"),)
    out_specs = (P("clip", "tm"), P("clip", "tm", None)) + (P(),) * 11
    return jax.shard_map(body, mesh=mesh, in_specs=in_specs, out_specs=out_specs, check_vma=False)
```

```python
import functools

import jax
import jax.numpy as jnp
import ml_dtypes
import numpy as np
from jax import lax
from jax.experimental import pallas as pl
from jax.experimental.pallas import tpu as pltpu
from jax.sharding import PartitionSpec as P

KERNEL = 7
CLASSES = ((1, 4), (2, 3), (0,))
F32 = jnp.float32
BF16 = jnp.bfloat16
LANES = 128
PAIRS = 128
ROWS = 2 * PAIRS
VMEM = 60 * 2**20
UP_PARTS = ((1024, 0), (512, 2))
HEAD_ROWS = 704
SDS = jax.ShapeDtypeStruct

SIN_POLY = (0.999999996, -0.166666580, 8.33305023e-03, -1.98090119e-04, 2.60507821e-06)
COS_POLY = (1.0, -0.499999994, 4.16666361e-02, -1.38883598e-03, 2.47600798e-05, -2.60500270e-07)

NN = (((1,), (0,)), ((), ()))
NT = (((1,), (1,)), ((), ()))


def split(x):
    high = x.astype(BF16)
    return high, (x - high.astype(F32)).astype(BF16)


def dot(a, b, dims=NN):
    return lax.dot_general(a, b, dims, preferred_element_type=F32)


def dot3(a, b, dims=NN):
    return dot(a[0], b[0], dims) + (dot(a[0], b[1], dims) + dot(a[1], b[0], dims))


def dot3_few(a, b, dims=NN):
    n = a.shape[0]
    high = a.astype(BF16).astype(F32)
    both = dot(jnp.concatenate([high, a - high], 0).astype(BF16), b[0], dims)
    return both[:n] + (both[n:] + dot(high.astype(BF16), b[1], dims))


def fold8(x):
    return jnp.sum(x.reshape(x.shape[0] // 8, 8, x.shape[1]), axis=0)


def np_split(x):
    high = x.astype(np.float32).astype(ml_dtypes.bfloat16)
    return high, (x - high.astype(np.float64)).astype(ml_dtypes.bfloat16)


@functools.lru_cache(None)
def tables(nfft):
    fifth, half, hop = nfft // 5, nfft // 2, nfft // 4
    bins = np.arange(1, half)
    first, second = (np.concatenate([bins[bins % 5 == r] for r in rs]) for rs in CLASSES[:2])
    zero = np.arange(0, half, 5)
    n0 = np.arange(fifth)

    def paired(ks, residue):
        sign = np.where(ks % 5 == residue, 1.0, -1.0)[:, None]
        turn = 2 * np.pi * ((sign * ks[:, None] * n0[None]) % nfft) / nfft
        weight = 2.0 / nfft
        real = np.concatenate([weight * np.cos(turn), weight * np.sin(turn)], 1)
        imag = np.concatenate([-sign * weight * np.sin(turn), sign * weight * np.cos(turn)], 1)
        return np.concatenate([real, imag], 0)

    turn = 2 * np.pi * ((zero[:, None] * n0[None]) % nfft) / nfft
    weight = np.where(zero == 0, 1.0, 2.0)[:, None] / nfft
    real, imag = weight * np.cos(turn), -weight * np.sin(turn)
    imag[0] = np.cos(np.pi * n0) / nfft
    transforms = [np_split(t) for t in (paired(first, 1), paired(second, 2), np.concatenate([real, imag], 0))]
    n = np.arange(nfft)
    window = 0.5 - 0.5 * np.cos(2 * np.pi * n / nfft)
    windows = np.stack([window, np.roll(window, hop)]).astype(np.float32)
    squares = np.cumsum((window**2).reshape(4, hop), axis=0)
    inverse = np.tile(1.0 / np.maximum(squares, 1.0), (1, 2)).astype(np.float32)
    turns = np.zeros(nfft)
    place = 0
    for ks in (first, second, zero):
        turns[place + len(ks) : place + 2 * len(ks)] = -(np.pi / 2) * (ks % 4)
        place += 2 * len(ks)
    return transforms, windows, inverse, turns.astype(np.float32)[None]


def class_places(nfft):
    length, places, at = nfft // 10, [], 0
    for residues in CLASSES:
        for offset in (0, nfft // 2 + 1):
            for r in residues:
                places.append((at, offset + r))
                at += length
    return places


def sin_cos(x):
    turns = jnp.round(x * np.float32(0.5 / np.pi))
    h = x * 0.5 - turns * np.float32(3.140625)
    h = h - turns * np.float32(9.67502593994140625e-4)
    h = h - turns * np.float32(1.509957990978376432e-7)
    z = h * h
    s = np.float32(SIN_POLY[-1])
    for c in SIN_POLY[-2::-1]:
        s = s * z + np.float32(c)
    s = s * h
    cosine = np.float32(COS_POLY[-1])
    for c in COS_POLY[-2::-1]:
        cosine = cosine * z + np.float32(c)
    twice = s + s
    return twice * cosine, 1.0 - twice * s


def fifths():
    a = 2 * np.pi / 5
    return [np.float32(v) for v in (np.cos(a), np.cos(2 * a), np.sin(a), np.sin(2 * a))]


def inverse_envelope(first_pair, offset, table_ref, tile, rows):
    lane = tile * LANES + lax.broadcasted_iota(jnp.int32, (rows, LANES), 1)
    row = lax.broadcasted_iota(jnp.int32, (rows, LANES), 0)
    half = table_ref.shape[1] // 2
    since = 2 * (first_pair + row) + (lane >= half).astype(jnp.int32) - offset
    value = jnp.where(since < 0, 1.0, 1.0)
    for i in range(4):
        value = jnp.where(since >= i, table_ref[i : i + 1, tile * LANES : (tile + 1) * LANES], value)
    return value


def head_kernel(
    bands,
    offsets,
    x_ref,
    x_up,
    x_down,
    edge_ref,
    cot_ref,
    cot_down,
    cot_edge,
    conv_w,
    conv_b,
    scale_t,
    shift_t,
    up_w,
    up_b,
    down_w,
    down_b,
    layer_scale,
    head_wt,
    head_b,
    turns,
    t1h,
    t1l,
    t2h,
    t2l,
    t0h,
    t0l,
    windows,
    inverse,
    o_norm,
    o_istd,
    o_adt_h,
    o_adt_l,
    o_slope,
    o_spec,
    o_gm,
    o_gb_h,
    o_gb_l,
    o_keep,
    o_send,
    o_small,
    up_h,
    up_l,
    down_h,
    down_l,
    head_h,
    head_l,
    head_bias,
    ext_w,
    head4,
    bias4,
    pad4,
    nrm4,
    istd1,
    gs5,
    gm4,
    gl_h,
    gl_l,
    act_h,
    act_l,
    acc_gdn,
    acc_ghw,
    acc_ghb,
    acc_ghwe,
    acc_ghbe,
    acc_gls,
    acc_gmb,
):
    clip, blk = pl.program_id(0), pl.program_id(1)
    clips, blks = pl.num_programs(0), pl.num_programs(1)
    width = x_ref.shape[2]
    frames = blks * ROWS
    tiles = width // LANES
    nfft = turns.shape[1]
    half = nfft // 2
    tm = lax.axis_index("tm")
    band = bands[clip]
    local = offsets[clip] - tm * frames
    rows8 = edge_ref.shape[1]
    places = class_places(nfft)

    @pl.when((clip == 0) & (blk == 0))
    def _():
        up_h[...], up_l[...] = split(up_w[...])
        down_h[...], down_l[...] = split(down_w[...])
        for t in range(tiles):
            head4[t, 0 : nfft + 2, :] = head_wt[:, t * LANES : (t + 1) * LANES]
        bias = head_b[...].reshape(1, nfft + 2)
        for c in range(0, nfft, LANES):
            bias4[c : c + LANES, :] = jnp.broadcast_to(bias[:, c : c + LANES], (LANES, LANES)).T
        for c in (nfft, nfft + 1):
            bias4[c : c + 1, :] = jnp.broadcast_to(bias[:, c : c + 1], (1, LANES))
        for at, first in places:
            rows = jnp.concatenate([head4[t, pl.ds(first, LANES, stride=5), :] for t in range(tiles)], 1)
            head_h[at : at + LANES, :], head_l[at : at + LANES, :] = split(rows)
            moved = bias4[pl.ds(first, LANES, stride=5), :].T[0:1, :]
            head_bias[0:1, at : at + LANES] = moved
            head_bias[1:2, at : at + LANES] = moved + turns[:, at : at + LANES]
        ext_w[0:1, :] = head_wt[half : half + 1, :]
        ext_w[1:2, :] = head_wt[nfft + 1 : nfft + 2, :]
        ext_w[2:8, :] = jnp.zeros((6, width), F32)
        for ref in (acc_gdn, acc_ghw, acc_ghb, acc_ghwe, acc_ghbe, acc_gls, acc_gmb):
            ref[...] = jnp.zeros_like(ref)

    base = pl.multiple_of(blk * ROWS, ROWS)

    def masked(value, first):
        row = first + lax.broadcasted_iota(jnp.int32, value.shape, 0)
        return jnp.where(row >= local, value, 0.0)

    before = masked(jnp.where(blk == 0, jnp.where(tm > 0, edge_ref[0], 0.0), x_up[0]), base - rows8)
    after = masked(jnp.where(blk == blks - 1, jnp.where(tm > 0, 0.0, edge_ref[0]), x_down[0]), base + ROWS)
    middle = masked(x_ref[0], base)
    for t in range(tiles):
        lanes = slice(t * LANES, (t + 1) * LANES)
        pad4[t, 0:rows8, :] = before[:, lanes]
        pad4[t, rows8 : rows8 + ROWS, :] = middle[:, lanes]
        pad4[t, rows8 + ROWS :, :] = after[:, lanes]
    bias = conv_b[...].reshape(1, width)
    chunk = 64
    for r in range(0, ROWS, chunk):
        parts = []
        for t in range(tiles):
            lanes = slice(t * LANES, (t + 1) * LANES)
            total = bias[:, lanes]
            for k in range(KERNEL):
                first = r + rows8 - KERNEL // 2 + k
                total = total + pad4[t, first : first + chunk, :] * conv_w[k : k + 1, lanes]
            parts.append(total)
        mean = jnp.sum(sum(parts[1:], parts[0]), axis=1, keepdims=True) * (1.0 / width)
        parts = [p - mean for p in parts]
        squares = [p * p for p in parts]
        variance = jnp.sum(sum(squares[1:], squares[0]), axis=1, keepdims=True) * (1.0 / width)
        istd = lax.rsqrt(variance + 1e-6)
        for t in range(tiles):
            nrm4[t, r : r + chunk, :] = parts[t] * istd
        istd1[r : r + chunk, :] = jnp.broadcast_to(istd, (chunk, LANES))

    def by_parity(ref, first):
        return jnp.concatenate(
            [
                jnp.concatenate([ref[t, pl.ds(first + par, PAIRS, stride=2), :] for t in range(tiles)], 1)
                for par in range(2)
            ],
            0,
        )

    normed = by_parity(nrm4, 0)
    o_norm[...] = normed
    for par in range(2):
        o_istd[par * PAIRS : (par + 1) * PAIRS, :] = istd1[pl.ds(par, PAIRS, stride=2), :]
    adapted = normed * scale_t[pl.ds(band, 1), :] + shift_t[pl.ds(band, 1), :]
    ad = split(adapted)
    o_adt_h[...], o_adt_l[...] = ad[0].T, ad[1].T

    first_pair = pl.multiple_of(blk * PAIRS, PAIRS)
    wave_tiles = gs5.shape[0]
    for t in range(wave_tiles):
        lanes = slice(t * LANES, (t + 1) * LANES)
        stride = clips * wave_tiles
        value = cot_ref[pl.ds(clips * t + clip, PAIRS, stride=stride), :]
        gs5[t, 0:PAIRS, :] = value * inverse_envelope(first_pair, local, inverse, t, PAIRS)
        value = cot_down[pl.ds(clips * t + clip, 8, stride=stride), :]
        value = jnp.where(blk == blks - 1, jnp.where(tm > 0, 0.0, cot_edge[0, :, lanes]), value)
        gs5[t, PAIRS : PAIRS + 8, :] = value * inverse_envelope(first_pair + PAIRS, local, inverse, t, 8)
    now, one, two = ([gs5[t, d : d + PAIRS, :] for t in range(wave_tiles)] for d in range(3))
    mid = wave_tiles // 2
    right = lax.broadcasted_iota(jnp.int32, (PAIRS, LANES), 1) >= LANES // 2
    odd = two[:mid] + [jnp.where(right, now[mid], two[mid])] + now[mid + 1 :] + one
    c1, c2, s1, s2 = fifths()
    folded = []
    for par, segment in enumerate((now + one, odd)):
        seg = [v * windows[par : par + 1, t * LANES : (t + 1) * LANES] for t, v in enumerate(segment)]
        v = [jnp.concatenate(seg[2 * j : 2 * j + 2], 1) for j in range(5)]
        p14, m41, p23, m32 = v[1] + v[4], v[4] - v[1], v[2] + v[3], v[3] - v[2]
        folded.append(
            (
                v[0] + p14 + p23,
                v[0] + c1 * p14 + c2 * p23,
                s1 * m41 + s2 * m32,
                v[0] + c2 * p14 + c1 * p23,
                s2 * m41 - s1 * m32,
            )
        )
    f0, fa, fb, fc, fd = (jnp.concatenate([e, o], 0) for e, o in zip(*folded))
    spectrum_grads = (
        dot3(split(jnp.concatenate([fa, fb], 1)), (t1h[...], t1l[...]), NT),
        dot3(split(jnp.concatenate([fc, fd], 1)), (t2h[...], t2l[...]), NT),
        dot3(split(f0), (t0h[...], t0l[...]), NT),
    )

    hidden = up_h.shape[1]
    step = 256
    up_bias = up_b[...].reshape(1, hidden)
    for j in range(hidden // step):
        cols = slice(j * step, (j + 1) * step)
        upward = dot3(ad, (up_h[:, cols], up_l[:, cols])) + up_bias[:, cols]
        cdf = 0.5 + 0.5 * lax.erf(upward * np.float32(0.7071067811865476))
        density = jnp.exp(upward * upward * -0.5) * np.float32(0.3989422804014327)
        o_slope[:, cols] = cdf + upward * density
        act_h[:, cols], act_l[:, cols] = split(upward * cdf)
    branch = dot3((act_h[...], act_l[...]), (down_h[...], down_l[...])) + down_b[...].reshape(1, width)
    scale = layer_scale[...].reshape(1, width)
    residual = by_parity(pad4, rows8) + scale * branch
    res = split(residual)
    res_t = res[0].T, res[1].T

    bias = head_b[...].reshape(1, nfft + 2)
    ext_logits = dot3_few(ext_w[...], res, NT)
    lane = lax.broadcasted_iota(jnp.int32, (1, ROWS), 1)
    ext_frame = base + jnp.where(lane < PAIRS, 2 * lane, 2 * (lane - PAIRS) + 1)
    ext_present = ext_frame >= local

    def magnitudes(logits, present):
        raw = jnp.where(present, jnp.exp(logits), 0.0)
        squashed = jnp.tanh(raw * np.float32(0.01))
        return 100.0 * squashed, raw * (1.0 - squashed * squashed)

    ext_mag, ext_slope = magnitudes(ext_logits[0:1] + bias[:, half : half + 1], ext_present)
    ext_sin, ext_cos = sin_cos(ext_logits[1:2] + bias[:, nfft + 1 : nfft + 2])
    ext_real = ext_mag * ext_cos
    ext_imag = ext_mag * ext_sin
    ext_real_col = jnp.concatenate([ext_real, jnp.zeros((7, ROWS), F32)], 0).T[:, 0:1]

    row = lax.broadcasted_iota(jnp.int32, (PAIRS, 1), 0)
    at = 0
    for index, grads in enumerate(spectrum_grads):
        n = grads.shape[1] // 2
        cols = slice(at, at + 2 * n)
        logits = dot3(res, (head_h[cols, :], head_l[cols, :]), NT)
        for par in range(2):
            rows = slice(par * PAIRS, (par + 1) * PAIRS)
            present = base + 2 * row + par >= local
            value = logits[rows] + head_bias[par : par + 1, cols]
            magnitude, slope = magnitudes(value[:, :n], present)
            sine, cosine = sin_cos(value[:, n:])
            real, imag = magnitude * cosine, magnitude * sine
            g_real, g_imag = grads[rows, :n], grads[rows, n:]
            if index == 2:
                corner = lax.broadcasted_iota(jnp.int32, (PAIRS, n), 1) == 0
                shown = jnp.where(corner, ext_real_col[rows], imag)
                g_imag = jnp.where(corner, 0.0, g_imag)
            else:
                shown = imag
            o_spec[rows, at : at + n] = real
            o_spec[rows, at + n : at + 2 * n] = shown
            g_mag = slope * (g_real * cosine + g_imag * sine)
            g_ang = g_imag * real - g_real * imag
            gl = jnp.concatenate([g_mag, g_ang], 1)
            acc_ghb[:, cols] += fold8(gl)
            gl_h[rows, cols], gl_l[rows, cols] = split(gl)
        at += 2 * n

    corner_t = spectrum_grads[2][:, spectrum_grads[2].shape[1] // 2 :].T
    ext_g = corner_t[0:1, :]
    ext_grads = jnp.concatenate(
        [ext_slope * ext_g * ext_cos, -ext_g * ext_imag, jnp.zeros((6, ROWS), F32)], 0
    )
    acc_ghbe[...] += ext_grads
    acc_ghwe[...] += dot3_few(ext_grads, res)
    gl = (gl_h[...], gl_l[...])
    ext_cols = ext_grads.T
    grad_mixed = (
        dot3(gl, (head_h[...], head_l[...]))
        + ext_cols[:, 0:1] * ext_w[0:1, :]
        + ext_cols[:, 1:2] * ext_w[1:2, :]
    )
    acc_ghw[...] += dot3(res_t, gl)
    acc_gls[...] += fold8(grad_mixed * branch)
    acc_gmb[...] += fold8(grad_mixed)
    for par in range(2):
        rows = slice(par * PAIRS, (par + 1) * PAIRS)
        for t in range(tiles):
            gm4[t, pl.ds(par, PAIRS, stride=2), :] = grad_mixed[rows, t * LANES : (t + 1) * LANES]
    for t in range(tiles):
        o_gm[:, t * LANES : (t + 1) * LANES] = gm4[t]
    grad_branch = grad_mixed * scale
    gb = split(grad_branch)
    o_gb_h[...], o_gb_l[...] = gb
    acc_gdn[...] += dot3((gb[0].T, gb[1].T), (act_h[...], act_l[...]))

    @pl.when((clip == clips - 1) & (blk == blks - 1))
    def _():
        total = jnp.sum(acc_ghb[...], axis=0, keepdims=True)
        for at, first in places:
            for t in range(tiles):
                block = acc_ghw[t * LANES : (t + 1) * LANES, at : at + LANES]
                head4[t, pl.ds(first, LANES, stride=5), :] = block.T
            block = jnp.broadcast_to(total[:, at : at + LANES], (LANES, LANES))
            bias4[pl.ds(first, LANES, stride=5), :] = block.T
        ext_sums = jnp.sum(acc_ghbe[...], axis=1, keepdims=True)
        for i, c in enumerate((half, nfft + 1)):
            for t in range(tiles):
                head4[t, c : c + 1, :] = acc_ghwe[i : i + 1, t * LANES : (t + 1) * LANES]
            bias4[c : c + 1, :] = jnp.broadcast_to(ext_sums[i : i + 1], (1, LANES))
        core = lax.axis_index("clip") % 2
        for here, first in ((core == 0, 0), (core == 1, half + 1)):

            @pl.when(here)
            def _(first=first):
                for t in range(tiles):
                    lanes = slice(t * LANES, (t + 1) * LANES)
                    for ref, at in ((o_keep, first), (o_send, half + 1 - first)):
                        ref[0 : half + 1, lanes] = head4[t, at : at + half + 1, :]
                        ref[half + 1 : HEAD_ROWS, lanes] = jnp.zeros((HEAD_ROWS - half - 1, LANES), F32)

        rows = hidden // 2
        for ref, part in ((o_keep, core), (o_send, 1 - core)):
            ref[HEAD_ROWS:, :] = acc_gdn[:, pl.ds(pl.multiple_of(part * rows, rows), rows)].T
        o_small[...] = jnp.zeros_like(o_small)
        for c in range(0, nfft, LANES):
            o_small[0:1, c : c + LANES] = bias4[c : c + LANES, :].T[0:1, :]
        o_small[0:1, nfft : nfft + 2] = jnp.concatenate(
            [bias4[nfft : nfft + 1, 0:1], bias4[nfft + 1 : nfft + 2, 0:1]], 1
        )
        o_small[1:2, :width] = jnp.sum(acc_gls[...], axis=0, keepdims=True)
        o_small[2:3, :width] = jnp.sum(acc_gmb[...], axis=0, keepdims=True) * scale


def whole(shape):
    return pl.BlockSpec(shape, lambda *_: (0,) * len(shape))


def fixed(shape):
    return pl.BlockSpec(shape, lambda *_: (0,) * len(shape), pipeline_mode=pl.Buffered(1))


def row_halves(blks, rows, rows8, width, clip=None):
    per, last = rows // rows8, blks * rows // rows8 - 1
    places = [
        (rows, lambda j: j),
        (rows8, lambda j: jnp.maximum(j * per - 1, 0)),
        (rows8, lambda j: jnp.minimum(j * per + per, last)),
    ]
    if clip is None:
        return [pl.BlockSpec((1, n, width), lambda i, j, *_, f=f: (i, f(j), 0)) for n, f in places]
    return [pl.BlockSpec((1, n, width), lambda j, *_, f=f: (clip, f(j), 0)) for n, f in places]


def run_head(bands, offsets, x, edge, cot, cot_edge, weights, turns, consts):
    clips, frames, width = x.shape
    blks = frames // ROWS
    count = clips * frames
    hidden = weights[4].shape[1]
    nfft = turns.shape[1]
    block = lambda i, j, *_: (i * blks + j, 0)
    column = lambda i, j, *_: (0, i * blks + j)
    per_clip = lambda shape: pl.BlockSpec((1,) + shape, lambda i, j, *_: (i, 0, 0))
    in_specs = row_halves(blks, ROWS, edge.shape[1], width)
    in_specs += [per_clip(edge.shape[1:])]
    operands = list(weights) + [turns] + list(consts)
    rows = cot.shape[0] // blks
    few = rows * 8 // PAIRS
    per, last = rows // few, cot.shape[0] // few - 1
    in_specs += [
        pl.BlockSpec((rows, LANES), lambda i, j, *_: (j, 0)),
        pl.BlockSpec((few, LANES), lambda i, j, *_: (jnp.minimum(j * per + per, last), 0)),
        per_clip(cot_edge.shape[1:]),
    ]
    in_specs += [fixed(v.shape) for v in operands]
    row_out = lambda n, dtype: (SDS((count, n), dtype), pl.BlockSpec((ROWS, n), block))
    col_out = (SDS((width, count), BF16), pl.BlockSpec((width, ROWS), column))
    outs = [
        row_out(width, F32),
        row_out(LANES, F32),
        col_out,
        col_out,
        row_out(hidden, F32),
        row_out(nfft, F32),
        row_out(width, F32),
        row_out(width, BF16),
        row_out(width, BF16),
        (SDS((HEAD_ROWS + hidden // 2, width), F32), fixed((HEAD_ROWS + hidden // 2, width))),
        (SDS((HEAD_ROWS + hidden // 2, width), F32), fixed((HEAD_ROWS + hidden // 2, width))),
        (SDS((8, hidden), F32), whole((8, hidden))),
    ]
    wave_tiles = nfft // 2 // LANES
    tiles = width // LANES
    scratch = [pltpu.VMEM((width, hidden), BF16)] * 2 + [pltpu.VMEM((hidden, width), BF16)] * 2
    scratch += [
        pltpu.VMEM((nfft, width), BF16),
        pltpu.VMEM((nfft, width), BF16),
        pltpu.VMEM((2, nfft), F32),
        pltpu.VMEM((8, width), F32),
        pltpu.VMEM((tiles, nfft + 8, LANES), F32),
        pltpu.VMEM((nfft + 8, LANES), F32),
        pltpu.VMEM((tiles, ROWS + 2 * edge.shape[1], LANES), F32),
        pltpu.VMEM((tiles, ROWS, LANES), F32),
        pltpu.VMEM((ROWS, LANES), F32),
        pltpu.VMEM((wave_tiles, PAIRS + 8, LANES), F32),
        pltpu.VMEM((tiles, ROWS, LANES), F32),
        pltpu.VMEM((ROWS, nfft), BF16),
        pltpu.VMEM((ROWS, nfft), BF16),
        pltpu.VMEM((ROWS, hidden), BF16),
        pltpu.VMEM((ROWS, hidden), BF16),
        pltpu.VMEM((width, hidden), F32),
        pltpu.VMEM((width, nfft), F32),
        pltpu.VMEM((8, nfft), F32),
        pltpu.VMEM((8, width), F32),
        pltpu.VMEM((8, ROWS), F32),
        pltpu.VMEM((8, width), F32),
        pltpu.VMEM((8, width), F32),
    ]
    return pl.pallas_call(
        head_kernel,
        grid_spec=pltpu.PrefetchScalarGridSpec(
            num_scalar_prefetch=2,
            grid=(clips, blks),
            in_specs=in_specs,
            out_specs=[s for _, s in outs],
            scratch_shapes=scratch,
        ),
        out_shape=[s for s, _ in outs],
        compiler_params=pltpu.CompilerParams(vmem_limit_bytes=VMEM),
        cost_estimate=pl.CostEstimate(flops=80_000_000_000, bytes_accessed=90_000_000, transcendentals=0),
        name="head",
    )(bands, offsets, x, x, x, edge, cot, cot, cot_edge, *operands)


def up_kernel(gb_h, gb_l, slope, adt_h, adt_l, down_w, *refs):
    o_keep, o_send, o_gub, o_gu_h, o_gu_l, dw_h, dw_l, acc, acc_gub = refs[-9:]
    step = pl.program_id(0)
    hidden = slope.shape[1]

    @pl.when(step == 0)
    def _():
        dw_h[...], dw_l[...] = split(down_w[...])
        acc[...] = jnp.zeros_like(acc)
        acc_gub[...] = jnp.zeros_like(acc_gub)

    cols = 512
    for j in range(hidden // cols):
        part = slice(j * cols, (j + 1) * cols)
        gu = dot3((gb_h[...], gb_l[...]), (dw_h[part, :], dw_l[part, :]), NT) * slope[:, part]
        acc_gub[:, part] += fold8(gu)
        gs = split(gu)
        o_gu_h[:, part], o_gu_l[:, part] = gs
        acc[:, part] += dot3((adt_h[...], adt_l[...]), gs)

    @pl.when(step == pl.num_programs(0) - 1)
    def _():
        o_gub[...] = jnp.sum(acc_gub[...], axis=0, keepdims=True)
        core = lax.axis_index("clip") % 2
        rows = o_keep.shape[0]
        for ref, half in ((o_keep, core), (o_send, 1 - core)):
            ref[...] = acc[:, pl.ds(pl.multiple_of(half * rows, rows), rows)].T


def after(values, operand):
    return lax.optimization_barrier((operand, tuple(values)))[0] if values else operand


def run_up(gb, slope, adt, down_w, size, part, so_far, waits=()):
    count, width = gb[0].shape
    hidden = slope.shape[1]
    rows = 512
    row = lambda i: (i, 0)
    in_specs = [pl.BlockSpec((rows, width), row)] * 2 + [pl.BlockSpec((rows, size), lambda i: (i, part))]
    in_specs += [pl.BlockSpec((width, rows), lambda i: (0, i))] * 2
    in_specs += [pl.BlockSpec((size, width), lambda i: (part, 0), pipeline_mode=pl.Buffered(1))]
    so_far = list(so_far)
    return pl.pallas_call(
        up_kernel,
        grid=(count // rows,),
        in_specs=in_specs + [pl.BlockSpec(memory_space=pl.ANY)] * len(so_far),
        out_specs=[pl.BlockSpec((size // 2, width), lambda i: (part, 0))] * 2
        + [whole((1, size)), pl.BlockSpec((rows, size), row), pl.BlockSpec((rows, size), row)],
        out_shape=[
            SDS((hidden // 2, width), F32),
            SDS((hidden // 2, width), F32),
            SDS((1, size), F32),
            SDS((count, size), BF16),
            SDS((count, size), BF16),
        ],
        input_output_aliases={6 + i: i for i in range(len(so_far))},
        scratch_shapes=[pltpu.VMEM((size, width), BF16)] * 2
        + [pltpu.VMEM((width, size), F32), pltpu.VMEM((8, size), F32)],
        compiler_params=pltpu.CompilerParams(vmem_limit_bytes=VMEM),
        cost_estimate=pl.CostEstimate(flops=10_000_000_000, bytes_accessed=20_000_000, transcendentals=0),
        name="up_grads",
    )(*gb, after(waits, slope), *adt, down_w, *so_far)


def norm_kernel(sizes, clip, bands, *refs):
    gu = refs[: 2 * len(sizes)]
    up_w, norm, istd, scale_t = refs[2 * len(sizes) : 2 * len(sizes) + 4]
    edge_in = refs[2 * len(sizes) + 4] if clip else None
    o_gh, o_edge, o_scale, o_shift, up_h, up_l, nat4, acc_scale, acc_shift = refs[-9:]
    blk, blks = pl.program_id(0), pl.num_programs(0)
    band = bands[clip]
    width = norm.shape[1]
    tiles = width // LANES

    @pl.when(blk == 0)
    def _():
        up_h[...], up_l[...] = split(up_w[...])
        for ref in (o_scale, o_shift, acc_scale, acc_shift):
            ref[...] = jnp.zeros_like(ref)
        if edge_in is not None:
            o_edge[...] = edge_in[...]

    ga, at = None, 0
    for j, hidden in enumerate(sizes):
        cols = slice(at, at + hidden)
        term = dot3((gu[2 * j][...], gu[2 * j + 1][...]), (up_h[:, cols], up_l[:, cols]), NT)
        ga = term if ga is None else ga + term
        at += hidden
    normed = norm[...]
    acc_scale[...] += fold8(ga * normed)
    acc_shift[...] += fold8(ga)
    gn = ga * scale_t[pl.ds(band, 1), :]
    mean = jnp.sum(gn, axis=1, keepdims=True) * (1.0 / width)
    along = jnp.sum(gn * normed, axis=1, keepdims=True) * (1.0 / width)
    gh = istd[:, 0:1] * (gn - mean - normed * along)
    for par in range(2):
        for t in range(tiles):
            nat4[t, pl.ds(par, PAIRS, stride=2), :] = gh[par * PAIRS : (par + 1) * PAIRS, t * LANES : (t + 1) * LANES]
    for t in range(tiles):
        o_gh[:, t * LANES : (t + 1) * LANES] = nat4[t]
    tm = lax.axis_index("tm")
    for here, first in (((tm == 0) & (blk == blks - 1), ROWS - 8), ((tm == 1) & (blk == 0), 0)):

        @pl.when(here)
        def _(first=first):
            for t in range(tiles):
                o_edge[clip, :, t * LANES : (t + 1) * LANES] = nat4[t, first : first + 8, :]

    @pl.when(blk == blks - 1)
    def _():
        o_scale[pl.ds(band, 1), :] = jnp.sum(acc_scale[...], axis=0, keepdims=True)
        o_shift[pl.ds(band, 1), :] = jnp.sum(acc_shift[...], axis=0, keepdims=True)


def run_norm(bands, gus, up_w, norm, istd, scale_t, edge, clip, waits=()):
    clips = edge.shape[0]
    earlier = [edge] if clip else []
    count, width = norm.shape
    blks = count // clips // ROWS
    block = lambda j, *_: (clip * blks + j, 0)
    flat = [v for pair in gus for v in pair]
    in_specs = [pl.BlockSpec((ROWS, v.shape[1]), block) for v in flat]
    in_specs += [fixed(up_w.shape), pl.BlockSpec((ROWS, width), block)]
    in_specs += [pl.BlockSpec((ROWS, LANES), block), fixed(scale_t.shape)]
    in_specs += [fixed(v.shape) for v in earlier]
    return pl.pallas_call(
        functools.partial(norm_kernel, [pair[0].shape[1] for pair in gus], clip),
        grid_spec=pltpu.PrefetchScalarGridSpec(
            num_scalar_prefetch=1,
            grid=(blks,),
            in_specs=in_specs,
            out_specs=[pl.BlockSpec((ROWS, width), lambda j, *_: (j, 0)), whole(edge.shape)] + [whole(scale_t.shape)] * 2,
            scratch_shapes=[pltpu.VMEM(up_w.shape, BF16)] * 2
            + [pltpu.VMEM((width // LANES, ROWS, LANES), F32)]
            + [pltpu.VMEM((8, width), F32)] * 2,
        ),
        out_shape=[SDS((count // clips, width), F32), SDS(edge.shape, F32)] + [SDS(scale_t.shape, F32)] * 2,
        compiler_params=pltpu.CompilerParams(vmem_limit_bytes=VMEM),
        cost_estimate=pl.CostEstimate(flops=5_000_000_000, bytes_accessed=12_000_000, transcendentals=0),
        name="norm_grads",
    )(bands, *flat, up_w, after(waits, norm), istd, scale_t, *earlier)


def conv_kernel(
    clip, offsets, x_ref, x_up, x_down, edge_ref, gh_ref, gh_up, gh_down, gh_edge, gm_ref, conv_w, *refs
):
    o_gi, o_acc, pad4, gh4 = refs[-4:]
    blk, blks = pl.program_id(0), pl.num_programs(0)
    rows, width = x_ref.shape[1], x_ref.shape[2]
    tiles = width // LANES
    tm = lax.axis_index("tm")
    local = offsets[clip] - tm * blks * rows
    rows8 = edge_ref.shape[1]
    base = blk * rows

    @pl.when(blk == 0)
    def _():
        o_acc[...] = refs[0][...] if clip else jnp.zeros_like(o_acc)

    def masked(value, first):
        row = first + lax.broadcasted_iota(jnp.int32, value.shape, 0)
        return jnp.where(row >= local, value, 0.0)

    def above(edge, up):
        return jnp.where(blk == 0, jnp.where(tm > 0, edge[0], 0.0), up[0])

    def below(edge, down):
        return jnp.where(blk == blks - 1, jnp.where(tm > 0, 0.0, edge[0]), down[0])

    before, after = masked(above(edge_ref, x_up), base - rows8), masked(below(edge_ref, x_down), base + rows)
    g_before, g_after = above(gh_edge, gh_up), below(gh_edge, gh_down)
    middle = masked(x_ref[0], base)
    for t in range(tiles):
        lanes = slice(t * LANES, (t + 1) * LANES)
        pad4[t, 0:rows8, :] = before[:, lanes]
        pad4[t, rows8 : rows8 + rows, :] = middle[:, lanes]
        pad4[t, rows8 + rows :, :] = after[:, lanes]
        gh4[t, 0:rows8, :] = g_before[:, lanes]
        gh4[t, rows8 : rows8 + rows, :] = gh_ref[0, :, lanes]
        gh4[t, rows8 + rows :, :] = g_after[:, lanes]
    chunk = 64
    for r in range(0, rows, chunk):
        shown = base + r + lax.broadcasted_iota(jnp.int32, (chunk, LANES), 0) >= local
        for t in range(tiles):
            lanes = slice(t * LANES, (t + 1) * LANES)
            gh = gh4[t, rows8 + r : rows8 + r + chunk, :]
            o_acc[8 * KERNEL :, lanes] += fold8(gh)
            total = gm_ref[0, r : r + chunk, lanes]
            for k in range(KERNEL):
                first = r + rows8 + KERNEL // 2 - k
                total = total + conv_w[k : k + 1, lanes] * gh4[t, first : first + chunk, :]
                first = r + rows8 - KERNEL // 2 + k
                o_acc[8 * k : 8 * k + 8, lanes] += fold8(gh * pad4[t, first : first + chunk, :])
            o_gi[0, r : r + chunk, lanes] = jnp.where(shown, total, 0.0)


def run_conv(offsets, x, edge, gh, gh_edge, gm, conv_w, clip, so_far, waits=()):
    clips, frames, width = x.shape
    blks = frames // ROWS
    rows8 = edge.shape[1]
    mine = pl.BlockSpec((1, rows8, width), lambda j, *_: (clip, 0, 0))
    padded = pltpu.VMEM((width // LANES, ROWS + 2 * rows8, LANES), F32)
    blocks = row_halves(blks, ROWS, rows8, width, clip)
    in_specs = blocks + [mine] + row_halves(blks, ROWS, rows8, width, 0) + [mine] + blocks[:1]
    in_specs += [fixed(conv_w.shape)]
    operands = [x, x, x, edge, gh, gh, gh, gh_edge, after(waits, gm), conv_w]
    aliases = {}
    sums = (8 * (KERNEL + 1), width)
    if so_far:
        grads, acc = so_far
        operands.append(acc)
        in_specs.append(fixed(acc.shape))
        aliases = {1 + len(operands): 0}
        operands.append(grads)
        in_specs.append(pl.BlockSpec(memory_space=pl.ANY))
    return pl.pallas_call(
        functools.partial(conv_kernel, clip),
        grid_spec=pltpu.PrefetchScalarGridSpec(
            num_scalar_prefetch=1,
            grid=(blks,),
            in_specs=in_specs,
            out_specs=[blocks[0], whole(sums)],
            scratch_shapes=[padded, padded],
        ),
        out_shape=[SDS(x.shape, F32), SDS(sums, F32)],
        input_output_aliases=aliases,
        compiler_params=pltpu.CompilerParams(vmem_limit_bytes=VMEM),
        cost_estimate=pl.CostEstimate(flops=5_000_000_000, bytes_accessed=17_000_000, transcendentals=0),
        name="conv_grads",
    )(offsets, *operands)


def pack_kernel(acc, small, scales0, scales1, shifts0, shifts1, *refs):
    gubs, o_pack = refs[:-1], refs[-1]
    width = acc.shape[1]
    for k in range(KERNEL + 1):
        o_pack[k : k + 1, :] = jnp.sum(acc[8 * k : 8 * k + 8, :], axis=0, keepdims=True)
    o_pack[8:12, :] = scales0[...] + scales1[...]
    o_pack[12:16, :] = shifts0[...] + shifts1[...]
    o_pack[16:18, :] = small[1:3, :width]
    for i in range(3):
        o_pack[18 + i : 19 + i, :] = small[0:1, i * width : (i + 1) * width]
        gub = jnp.concatenate([v[...] for v in gubs], 1)
        o_pack[21 + i : 22 + i, :] = gub[:, i * width : (i + 1) * width]
    o_pack[24:, :] = jnp.zeros((o_pack.shape[0] - 24, width), F32)


def wave_kernel(
    first_blk, frames, scaled, offsets, spec, t1h, t1l, t2h, t2l, t0h, t0l, windows, inverse, *refs
):
    o_wave, o_tail, accs = refs[-3:]
    blk, clip = pl.program_id(0), pl.program_id(1)
    blks, clips = pl.num_programs(0), pl.num_programs(1)
    tiles = accs.shape[1]
    first = (first_blk + blk) * PAIRS
    local = offsets[clip] - lax.axis_index("tm") * frames
    acc5 = accs.at[clip]

    @pl.when(blk == 0)
    def _():
        for t in range(tiles):
            lanes = slice(t * LANES, (t + 1) * LANES)
            acc5[t, 0:8, :] = refs[0][0, :, lanes] if scaled else jnp.zeros((8, LANES), F32)

    @pl.when(blk > 0)
    def _():
        for t in range(tiles):
            acc5[t, 0:8, :] = acc5[t, PAIRS : PAIRS + 8, :]

    for t in range(tiles):
        acc5[t, 8:, :] = jnp.zeros((PAIRS, LANES), F32)

    n1, n2 = t1h.shape[0], t2h.shape[0]
    ab = dot3(split(spec[:, :n1]), (t1h[...], t1l[...]))
    cd = dot3(split(spec[:, n1 : n1 + n2]), (t2h[...], t2l[...]))
    p0 = dot3(split(spec[:, n1 + n2 :]), (t0h[...], t0l[...]))
    c1, c2, s1, s2 = fifths()
    sides = []
    for par in range(2):
        rows = slice(par * PAIRS, (par + 1) * PAIRS)
        w = p0.shape[1]
        a, b, c, d, p = ab[rows, :w], ab[rows, w:], cd[rows, :w], cd[rows, w:], p0[rows]
        e1, o1 = p + c1 * a + c2 * c, s1 * b + s2 * d
        e2, o2 = p + c2 * a + c1 * c, s2 * b - s1 * d
        v = [p + a + c, e1 - o1, e2 - o2, e2 + o2, e1 + o1]
        seg = []
        for t in range(2 * tiles):
            part = v[t // 2][:, (t % 2) * LANES : (t % 2 + 1) * LANES]
            seg.append(part * windows[par : par + 1, t * LANES : (t + 1) * LANES])
        sides.append(seg)
    even, odd = sides
    mid = tiles // 2
    right = lax.broadcasted_iota(jnp.int32, (PAIRS, LANES), 1) >= LANES // 2
    for t in range(tiles):
        here = even[t]
        if t > mid:
            here = here + odd[t]
        if t == mid:
            here = here + jnp.where(right, odd[t], 0.0)
        acc5[t, 0:PAIRS, :] += here
        acc5[t, 1 : PAIRS + 1, :] += even[tiles + t] + odd[tiles + t]
        if t < mid:
            acc5[t, 2 : PAIRS + 2, :] += odd[t]
        if t == mid:
            acc5[t, 2 : PAIRS + 2, :] += jnp.where(right, 0.0, odd[t])
        value = acc5[t, 0:PAIRS, :] * inverse_envelope(first, local, inverse, t, PAIRS)
        o_wave[pl.ds(clips * t + clip, PAIRS, stride=clips * tiles), :] = value

    @pl.when(blk == blks - 1)
    def _():
        for t in range(tiles):
            value = acc5[t, PAIRS : PAIRS + 8, :]
            if scaled:
                value = value * inverse_envelope(first + PAIRS, local, inverse, t, 8)
            o_tail[0, :, t * LANES : (t + 1) * LANES] = value


def run_wave(offsets, spec, consts, clips, first_blk, blks, earlier=(), waits=()):
    count, nfft = spec.shape
    all_blks = count // clips // ROWS
    tiles = nfft // 2 // LANES
    rows = clips * PAIRS * tiles
    in_specs = [pl.BlockSpec((ROWS, nfft), lambda j, i, *_: (i * all_blks + first_blk + j, 0))]
    in_specs += [fixed(v.shape) for v in consts]
    operands = [after(waits, spec), *consts]
    aliases = {}
    if earlier:
        carry, wave = earlier
        operands.append(carry)
        in_specs.append(pl.BlockSpec((1, 8, nfft // 2), lambda j, i, *_: (i, 0, 0)))
        aliases = {1 + len(operands): 0}
        operands.append(wave)
        in_specs.append(pl.BlockSpec(memory_space=pl.ANY))
    return pl.pallas_call(
        functools.partial(wave_kernel, first_blk, count // clips, first_blk == 0),
        grid_spec=pltpu.PrefetchScalarGridSpec(
            num_scalar_prefetch=1,
            grid=(blks, clips),
            in_specs=in_specs,
            out_specs=[
                pl.BlockSpec((rows, LANES), lambda j, i, *_: (first_blk + j, 0)),
                pl.BlockSpec((1, 8, nfft // 2), lambda j, i, *_: (i, 0, 0)),
            ],
            scratch_shapes=[pltpu.VMEM((clips, tiles, PAIRS + 8, LANES), F32)],
        ),
        out_shape=[SDS((rows * all_blks, LANES), F32), SDS((clips, 8, nfft // 2), F32)],
        input_output_aliases=aliases,
        compiler_params=pltpu.CompilerParams(vmem_limit_bytes=VMEM),
        cost_estimate=pl.CostEstimate(flops=5_000_000_000, bytes_accessed=8_000_000, transcendentals=0),
        name="wave",
    )(offsets, *operands)


def levels():
    clip = [("clip", 1 << i) for i in range((lax.axis_size("clip") - 1).bit_length())]
    tm = [("tm", 1 << i) for i in range((lax.axis_size("tm") - 1).bit_length())]
    return clip[:1] + clip[1:2] + tm + clip[2:]


def exchange(value, level):
    if level == "next":
        return lax.ppermute(value, "tm", [(i, i + 1) for i in range(lax.axis_size("tm") - 1)])
    across = {"clip": 0, "tm": 0}
    for axis, distance in level if isinstance(level, list) else [level]:
        across[axis] += distance
    if not across["tm"]:
        return lax.ppermute(value, "clip", [(i, i ^ across["clip"]) for i in range(lax.axis_size("clip"))])
    if not across["clip"]:
        return lax.ppermute(value, "tm", [(i, i ^ across["tm"]) for i in range(lax.axis_size("tm"))])
    n, m = lax.axis_size("clip"), lax.axis_size("tm")
    pairs = [(i * m + j, (i ^ across["clip"]) * m + (j ^ across["tm"])) for i in range(n) for j in range(m)]
    return lax.ppermute(value, ("clip", "tm"), pairs)


def side(level):
    axis, distance = level
    return lax.axis_index(axis) // distance % 2


class Sums:
    def __init__(self):
        self.running = []

    def add(self, steps, holds=()):
        entry = {"steps": steps, "holds": holds, "count": 0, "sent": None, "came": None, "left": 0, "sum": None}
        self.step(entry, None)
        self.running.append(entry)
        return entry

    def step(self, entry, values):
        try:
            entry["sent"] = entry["steps"].send(values)
            while entry["sent"][0][1] == levels()[0]:
                entry["sent"] = entry["steps"].send([exchange(*pair) for pair in entry["sent"]])
        except StopIteration as stop:
            entry["sent"], entry["sum"] = None, stop.value

    def waits(self):
        sent = []
        for entry in self.running:
            if entry["came"] is None and entry["sent"] is not None:
                entry["came"] = [exchange(*pair) for pair in entry["sent"]]
                entry["left"] = dict(entry["holds"]).get(entry["count"], 1)
                entry["count"] += 1
                sent += [pair[0] for pair in entry["sent"]]
        return sent

    def advance(self, results):
        done = []
        for entry in self.running:
            if entry["came"] is not None:
                entry["left"] -= 1
                if entry["left"] <= 0:
                    done.append(entry)
        if done:
            came, results = lax.optimization_barrier(([entry["came"] for entry in done], results))
            for entry, values in zip(done, came):
                entry["came"] = None
                self.step(entry, values)
        return results

    def finish(self, entry):
        while entry["sum"] is None:
            self.waits()
            self.advance(())
        return entry["sum"]


def halves_steps(keep, send, narrow):
    core, one, two, *last = levels()
    orders = ((one, two), (two, one))
    (came,) = yield [(send, core)]
    cols = keep.shape[1] // 2
    parts = [[(v, 0, c) for v in (keep, came)] for c in (0, cols)]

    def cut(terms, first):
        return [(v, row + first, col) for v, row, col in terms]

    def added(terms, rows):
        return sum(lax.dynamic_slice(v, (row, col), (rows, cols)) for v, row, col in terms)

    rows = keep.shape[0]
    for i in range(2):
        rows //= 2
        sides = [side(order[i]) for order in orders]
        came = yield [(added(cut(t, (1 - s) * rows), rows), o[i]) for t, s, o in zip(parts, sides, orders)]
        parts = [cut(t, s * rows) + [(c, 0, 0)] for t, s, c in zip(parts, sides, came)]
    value = jnp.concatenate([added(t, rows) for t in parts])
    halved = last if narrow and rows % (4 << len(last)) == 0 else []
    n, terms = value.shape[0], [(value, 0, 0)]
    for level in halved:
        n, s = n // 2, side(level)
        (came,) = yield [(added(cut(terms, (1 - s) * n), n), level)]
        terms = cut(terms, s * n) + [(came, 0, 0)]
    value = added(terms, n) if halved else value
    for level in last[len(halved) :]:
        (came,) = yield [(value, level)]
        value = value + came
    for level in halved[::-1]:
        s = side(level)
        (came,) = yield [(value, level)]
        value = jnp.concatenate([jnp.where(s == 0, value, came), jnp.where(s == 0, came, value)])
    parts = [value[:rows], value[rows:]]
    came = yield [(part, order[1]) for part, order in zip(parts, orders)]
    parts = [jnp.concatenate(pair) for pair in zip(parts, came)]
    came = yield [(part, order[0]) for part, order in zip(parts, orders)]
    parts, came = lax.optimization_barrier((parts, came))
    parts = [piece for pair in zip(parts, came) for piece in pair]
    others = yield [(part, core) for part in parts]
    return parts, others, orders


def whole_steps(value):
    core, *rest = levels()
    (came,) = yield [(value, core)]
    value = value + came
    for pair in [rest[:1]] + [rest[i : i + 2] for i in range(1, len(rest), 2)]:
        came = yield [(value, [level]) for level in pair] + ([(value, pair)] if len(pair) == 2 else [])
        for other in came:
            value = value + other
    return value


def one_step(value, level):
    (came,) = yield [(value, level)]
    return came


def natural_blocks(orders, refs, copy):
    core = side(levels()[0])
    cols = refs[0].shape[1]
    rows = refs[0].shape[0] // 2
    for half in range(2):
        for here, four in ((core == half, refs[:4]), (core != half, refs[4:])):
            for i, order in enumerate(orders):
                a, b = (side(level) for level in order)
                for top in range(2):
                    for piece in range(2):

                        @pl.when(here & (jnp.bitwise_xor(top, a) == piece))
                        def _(ref=four[2 * i + piece], half=half, i=i, top=top, b=b):
                            for low in range(2):
                                first = pl.multiple_of(jnp.bitwise_xor(low, b) * rows, 8)
                                value = ref[pl.ds(first, rows), :]
                                copy(half, slice(i * cols, (i + 1) * cols), (2 * top + low) * rows, value)


def to_runs(runs):
    def copy(half, cols, first, value):
        for start, out, place, rows in runs:
            low, high = max(first, start), min(first + value.shape[0], start + rows)
            if low < high:
                at = place(half) + low - start
                out[at : at + high - low, cols] = value[low - first : high - first]

    return copy


def first_order_kernel(orders, *refs):
    o_head, o_down = refs[-2:]
    copy = to_runs(
        (
            (0, o_head, lambda half: half * (o_head.shape[0] // 2), o_head.shape[0] // 2),
            (HEAD_ROWS, o_down, lambda half: half * (o_down.shape[0] // 2), o_down.shape[0] // 2),
        )
    )
    natural_blocks(orders, refs[:8], copy)


def up_order_kernel(orders, *refs):
    o_up, up_t = refs[-2:]

    runs, at = [], 0
    for size, part in UP_PARTS:
        runs.append((at, up_t, lambda half, size=size, part=part: size * part + half * (size // 2), size // 2))
        at += size // 2
    copy = to_runs(runs)
    natural_blocks(orders, refs[:8], copy)
    for c in range(0, up_t.shape[0], LANES):
        o_up[:, c : c + LANES] = up_t[c : c + LANES, :].T


def run_order(kernel, total, out_shape, scratch=(), waits=()):
    parts, others, orders = total
    parts = after(waits, parts)
    return pl.pallas_call(
        functools.partial(kernel, orders),
        in_specs=[pl.BlockSpec(memory_space=pltpu.VMEM)] * 8,
        out_shape=out_shape,
        scratch_shapes=list(scratch),
        compiler_params=pltpu.CompilerParams(vmem_limit_bytes=VMEM),
        name="in_order",
    )(*parts, *others)


def unpack_kernel(pack, gcw, gcb, gscale, gshift, gls, gdb, ghb, gub):
    width = pack.shape[1]
    gcw[...] = pack[0:KERNEL, :]
    gcb[...] = pack[KERNEL : KERNEL + 1, :].reshape(width)
    gscale[...] = pack[8:12, :]
    gshift[...] = pack[12:16, :]
    gls[...] = pack[16:17, :].reshape(width)
    gdb[...] = pack[17:18, :].reshape(width)
    rows = [pack[18 + i : 19 + i, :] for i in range(6)]
    ghb[...] = jnp.concatenate(rows[:3], 1)[:, : ghb.shape[0]].reshape(ghb.shape[0])
    gub[...] = jnp.concatenate(rows[3:], 1).reshape(gub.shape[0])


def edges(value, index):
    n = value.shape[1]
    return jnp.where(index == 0, value[:, n - 8 :], value[:, :8])


def to_chunks(wave):
    clips, samples = wave.shape
    return wave.reshape(clips, samples // LANES, LANES).transpose(1, 0, 2).reshape(-1, LANES)


def from_chunks(chunks, clips):
    rows = chunks.shape[0] // clips
    return chunks.reshape(rows, clips, LANES).transpose(1, 0, 2).reshape(clips, rows * LANES)


def body(
    inputs,
    band_ids,
    offsets,
    conv_weight,
    conv_bias,
    scale_table,
    shift_table,
    up_weight,
    up_bias,
    down_weight,
    down_bias,
    layer_scale,
    head_weight,
    head_bias,
    wave_cotangent,
):
    clips, frames, width = inputs.shape
    assert lax.axis_size("tm") == 2
    nfft = head_weight.shape[1] - 2
    half = nfft // 2
    hidden = up_weight.shape[1]
    tm = lax.axis_index("tm")
    core = lax.axis_index("clip") % 2
    swap = lambda v: lax.ppermute(v, "tm", [(0, 1), (1, 0)])
    transforms, windows, inverse, turns = tables(nfft)
    dft = [jnp.asarray(v) for pair in transforms for v in pair]
    consts = dft + [jnp.asarray(windows), jnp.asarray(inverse)]

    edge = swap(edges(inputs, tm))
    cot_edge = swap(jnp.pad(wave_cotangent[:, :nfft].reshape(clips, 2, half), ((0, 0), (0, 6), (0, 0))))
    weights = (
        conv_weight,
        conv_bias,
        scale_table,
        shift_table,
        up_weight,
        up_bias,
        down_weight,
        down_bias,
        layer_scale,
        head_weight.T,
        head_bias,
    )
    (
        norm, istd, adt_h, adt_l, slope, spec, gm, gb_h, gb_l, keep, send, small,
    ) = run_head(
        band_ids, offsets, inputs, edge, to_chunks(wave_cotangent), cot_edge, weights, jnp.asarray(turns), consts
    )

    sums = Sums()
    first_total = sums.add(halves_steps(keep, send, True))
    blks = frames // ROWS
    gus, gubs, halves = [], [], ()
    for size, part in UP_PARTS:
        results = run_up((gb_h, gb_l), slope, (adt_h, adt_l), down_weight, size, part, halves, waits=sums.waits())
        *halves, gub, gu_h, gu_l = sums.advance(results)
        gus.append((gu_h, gu_l))
        gubs.append(gub)
    up_total = sums.add(halves_steps(*halves, False), {3: 2})
    normed, gh_edge = [], edge
    for clip in range(clips):
        results = run_norm(band_ids, gus, up_weight, norm, istd, scale_table, gh_edge, clip, waits=sums.waits())
        gh_edge = results[1]
        normed.append(sums.advance(results))
    gh = [v[0][None] for v in normed]
    gh_edge = sums.add(one_step(normed[-1][1], ("tm", 1)))
    late = blks // 2
    wave, tail = run_wave(offsets, spec, consts, clips, late, blks - late, waits=sums.waits())
    wave, tail = sums.advance((wave, tail))
    arrived = sums.add(one_step(tail, "next"))
    gh_edge = sums.finish(gh_edge)
    so_far = ()
    gm = gm.reshape(clips, frames, width)
    for clip in range(clips):
        so_far = run_conv(
            offsets, inputs, edge, gh[clip], gh_edge, gm, conv_weight, clip, so_far, waits=sums.waits()
        )
        so_far = sums.advance(so_far)
    grad_inputs, acc = so_far
    pack = pl.pallas_call(pack_kernel, out_shape=SDS((32, width), F32), name="pack")(
        acc, small, *[v[2] for v in normed], *[v[3] for v in normed], *gubs
    )
    small_total = sums.add(whole_steps(pack))

    arrived = sums.finish(arrived)
    wave, over = run_wave(offsets, spec, consts, clips, 0, late, (arrived, wave), waits=sums.waits())
    wave, over = sums.advance((wave, over))
    over = to_chunks(over[:, :2].reshape(clips, nfft))
    at = late * clips * PAIRS * half // LANES
    mended = lax.dynamic_slice_in_dim(wave, at, over.shape[0]) + over
    waveform = from_chunks(lax.dynamic_update_slice_in_dim(wave, mended, at, 0), clips)

    first_total = sums.finish(first_total)
    head_grad, down_grad = sums.advance(
        run_order(
            first_order_kernel,
            first_total,
            [SDS((nfft + 2, width), F32), SDS((hidden, width), F32)],
            waits=sums.waits(),
        )
    )
    up_total = sums.finish(up_total)
    (up_grad,) = sums.advance(
        run_order(
            up_order_kernel,
            up_total,
            [SDS((width, hidden), F32)],
            [pltpu.VMEM((hidden, width), F32)],
            waits=sums.waits(),
        )
    )
    pack = sums.finish(small_total)
    small_shapes = [(KERNEL, width), (width,), scale_table.shape, scale_table.shape]
    small_shapes += [(width,), (width,), (nfft + 2,), (hidden,)]
    gcw, gcb, gscale, gshift, gls, gdb, ghb, gub = pl.pallas_call(
        unpack_kernel, out_shape=[SDS(shape, F32) for shape in small_shapes], name="unpack"
    )(pack)
    return (
        waveform,
        grad_inputs,
        gcw,
        gcb,
        gscale,
        gshift,
        up_grad,
        gub,
        down_grad,
        gdb,
        gls,
        head_grad.T,
        ghb,
    )


def solution(mesh):
    in_specs = (P("clip", "tm", None), P("clip"), P("clip")) + (P(),) * 11 + (P("clip", "tm"),)
    out_specs = (P("clip", "tm"), P("clip", "tm", None)) + (P(),) * 11
    return jax.shard_map(body, mesh=mesh, in_specs=in_specs, out_specs=out_specs, check_vma=False)
```
